256 devices in a mesh: kv: 64 (over y, z, core), tp: 4 (over x).
Axes of the slice: x: 4, y: 4, z: 8, core: 2. Of those that a mesh axis runs over, the one named last changes fastest.
Arguments:
- queries: bfloat16 [3, 512, 8192], P(None, ('kv', 'tp')), may hold values from -35 to 35
- new_keys: bfloat16 [3, 512, 1024], P(None, ('kv', 'tp')), may hold values from -6 to 6
- new_values: bfloat16 [3, 512, 1024], P(None, ('kv', 'tp')), may hold values from -6 to 6
- key_cache: bfloat16 [2560, 256, 1024], P('kv', None, 'tp'), may hold values from -21 to 21
- value_cache: bfloat16 [2560, 256, 1024], P('kv', None, 'tp'), may hold values from -6 to 6
- context_lengths: int32 [512], replicated, may hold values from 1 to 32768, as said below
- piece_slots: int32 [512, 128], replicated, may hold values from -1 to 2559, as said below
Outputs:
- attended: bfloat16 [3, 512, 8192], P(None, ('kv', 'tp'))
The draws below stay inside these ranges and needn't reach their ends.
Inputs may be any that keep to these rules, and one draw needn't show every extreme that they name: Row b holds ceil(context_lengths[b] / 256) cache slots; some row holds 32768 tokens. piece_slots[b, p] is owner * 40 + local slot of the slot holding tokens p * 256 to (p + 1) * 256 - 1 of row b for p below ceil(context_lengths[b] / 256), and -1 after. Every slot holds exactly one piece. The slots of the 8 rows of one index of kv lie at most 3 times on one owner, and for some index of kv exactly 3 times on every owner.
All inputs are finite; a program needn't handle non-finite values.
Results may differ from the reference program's by a relative error of at most 0.0051.
Values may be sent and summed in bfloat16 or wider, within the bound.
A program may use at most 128 MiB of HBM per device.

```python
import math
import jax
import jax.numpy as jnp
from jax import lax

HQ = 64
KVH = 8
HD = 128
STEPS = 3
ROWS_DEV = 2
SLOTS_DEV = 40
SLOT_LEN = 256
PIECES = 128
ROWS = 512
TOTAL_SLOTS = 2560
CAP = 3
N_KV = 64
N_TP = 4


def piece_plan(key):
    rows_group = ROWS_DEV * N_TP
    keys = jax.random.split(key, 7)
    special = jax.random.randint(keys[0], (), 0, N_KV)
    star_row = jax.random.randint(keys[1], (), 0, rows_group)
    remain = SLOTS_DEV * N_KV - CAP * N_KV
    base_share = remain // (N_KV - 1)
    leftover = remain % (N_KV - 1)
    groups = jnp.arange(N_KV, dtype=jnp.int32)
    others = jnp.where(groups < special, groups, groups - 1)
    base = base_share + (others < leftover).astype(jnp.int32)
    pair_id = others // 2
    pair_count = (N_KV - 1) // 2
    shifts = jax.random.randint(keys[2], (N_KV,), 0, base_share - rows_group + 1)
    moved = jnp.where(others % 2 == 0, shifts[jnp.clip(pair_id, 0, N_KV - 1)], -shifts[jnp.clip(pair_id, 0, N_KV - 1)])
    moved = jnp.where(pair_id >= pair_count, 0, moved)
    group_total = jnp.where(groups == special, CAP * N_KV, base + moved)
    is_star = (groups[:, None] == special) & (jnp.arange(rows_group, dtype=jnp.int32)[None, :] == star_row)
    share = jnp.where(groups == special, group_total - PIECES, group_total)
    sharers = jnp.where(groups == special, rows_group - 1, rows_group)
    weights = jax.random.randint(keys[3], (N_KV, rows_group), 1, 9)
    weights = jnp.where(is_star, 0, weights)
    running = jnp.cumsum(weights, axis=1)
    whole = running[:, -1:]
    extra = (share - sharers)[:, None]
    marks = extra * running // whole
    parts = marks - jnp.concatenate([jnp.zeros((N_KV, 1), jnp.int32), marks[:, :-1]], axis=1)
    counts = jnp.where(is_star, PIECES, parts + 1).reshape(-1).astype(jnp.int32)
    fills = jax.random.randint(keys[4], counts.shape, 1, SLOT_LEN + 1)
    fills = jnp.where(counts == PIECES, SLOT_LEN, fills)
    lengths = ((counts - 1) * SLOT_LEN + fills).astype(jnp.int32)
    starts = jnp.cumsum(counts) - counts
    columns = jnp.arange(PIECES, dtype=jnp.int32)
    packed = starts[:, None] + columns[None, :]
    used = columns[None, :] < counts[:, None]
    shuffled = jax.random.permutation(keys[5], N_KV).astype(jnp.int32)
    turned = jax.random.randint(keys[6], (N_KV,), 0, SLOTS_DEV)
    owner = shuffled[packed % N_KV]
    local = (packed // N_KV + turned[owner]) % SLOTS_DEV
    slots = jnp.where(used, owner * SLOTS_DEV + local, -1).astype(jnp.int32)
    return (lengths, slots)


def draw_context_lengths(key, part):
    return piece_plan(key)[0]


def draw_piece_slots(key, part):
    return piece_plan(key)[1]


def draw_queries(key, part):
    key = jax.random.fold_in(key, 3)
    first = jax.random.fold_in(key, 0)
    rows = ROWS_DEV * N_TP * N_KV
    values = 2.5 * jnp.clip(jax.random.normal(first, (STEPS, rows, HQ, HD), jnp.float32), -6.0, 6.0)
    values = jnp.clip(values, -35.0, 35.0)
    return values.reshape(STEPS, rows, HQ * HD).astype(jnp.bfloat16)


def draw_key_cache(key, part):
    key = jax.random.fold_in(key, 5)
    values = jnp.clip(jax.random.normal(key, (SLOTS_DEV * N_KV, SLOT_LEN, KVH, HD), jnp.float32), -6.0, 6.0)
    return values.reshape(SLOTS_DEV * N_KV, SLOT_LEN, KVH * HD).astype(jnp.bfloat16)


def steps_of(stream_key, dims, cuts, least, top_value):
    loudness = 1.0
    for axis_at, shards_of in cuts:
        heights = jax.random.uniform(jax.random.fold_in(jax.random.fold_in(stream_key, 6), axis_at), (shards_of,), jnp.float32, least / len(cuts), top_value / len(cuts))
        loudness = loudness * jnp.repeat(jnp.exp(heights), dims[axis_at] // shards_of).reshape((-1,) + (1,) * (len(dims) - 1 - axis_at))
    return loudness


def gaussian(key, dims, deviation, bound, pieces=(), kind=jnp.bfloat16):
    values = deviation * jax.random.normal(key, dims, jnp.float32)
    if pieces:
        values = values * steps_of(key, dims, pieces, -0.22, 0.18)
    return jnp.clip(values, -bound, bound).astype(kind)


def setup_inputs(seed: int = 0) -> dict:
    arg_keys = jax.random.split(jax.random.key(seed), 8)
    return {
        "queries": draw_queries(jax.random.fold_in(arg_keys[7], 71), 0),
        "new_keys": gaussian(arg_keys[1], (STEPS, ROWS, KVH * HD), 1.0, 6.0, ((1, 256),)),
        "new_values": gaussian(arg_keys[2], (STEPS, ROWS, KVH * HD), 1.0, 6.0, ((1, 256),)),
        "key_cache": draw_key_cache(jax.random.fold_in(arg_keys[7], 71), 0),
        "value_cache": gaussian(arg_keys[4], (TOTAL_SLOTS, SLOT_LEN, KVH * HD), 1.0, 6.0, ((0, 64), (2, 4))),
        "context_lengths": draw_context_lengths(jax.random.fold_in(arg_keys[7], 71), 0),
        "piece_slots": draw_piece_slots(jax.random.fold_in(arg_keys[7], 71), 0),
    }


def piece_attention(slot_queries, slot_keys, slot_values, counts):
    steps, slots, width = slot_queries.shape
    group = HQ // KVH
    grid = slot_queries.astype(jnp.float32).reshape(steps, slots, KVH, group, HD)
    keys = slot_keys.astype(jnp.float32).reshape(slots, SLOT_LEN, KVH, HD)
    values = slot_values.astype(jnp.float32).reshape(slots, SLOT_LEN, KVH, HD)
    scores = jnp.einsum('tskgc,snkc->sktgn', grid, keys) * (1.0 / math.sqrt(HD))
    live = jnp.arange(SLOT_LEN, dtype=jnp.int32)[None, None, None, None, :] < counts[:, None, None, None, None]
    scores = jnp.where(live, scores, -jnp.inf)
    top = lax.optimization_barrier(jnp.max(scores, axis=-1))
    expo = jnp.exp(scores - top[..., None])
    total = lax.optimization_barrier(jnp.sum(expo, axis=-1))
    weights = expo.astype(jnp.bfloat16).astype(jnp.float32)
    summed = jnp.einsum('sktgn,snkc->sktgc', weights, values)
    return (top, total, (summed / total[..., None]).astype(jnp.bfloat16))

def reference(queries, new_keys, new_values, key_cache, value_cache, context_lengths, piece_slots):
    rows = queries.shape[1]
    group = HQ // KVH
    used = piece_slots >= 0
    flat_pos = jnp.arange(rows * PIECES, dtype=jnp.int32)
    target = jnp.where(used, piece_slots, TOTAL_SLOTS).reshape(-1).astype(jnp.int32)
    holder = jnp.zeros((TOTAL_SLOTS,), jnp.int32).at[target].set(flat_pos, mode='drop')
    slot_row = holder // PIECES
    slot_piece = holder % PIECES
    counts = jnp.minimum(SLOT_LEN, context_lengths[slot_row] - slot_piece * SLOT_LEN)

    def one_owner(index):
        start = (index * SLOTS_DEV).astype(jnp.int32)
        block_keys = lax.dynamic_slice_in_dim(key_cache, start, SLOTS_DEV, 0)
        block_values = lax.dynamic_slice_in_dim(value_cache, start, SLOTS_DEV, 0)
        block_rows = lax.dynamic_slice_in_dim(slot_row, start, SLOTS_DEV, 0)
        block_counts = lax.dynamic_slice_in_dim(counts, start, SLOTS_DEV, 0)
        return piece_attention(queries[:, block_rows], block_keys, block_values, block_counts)
    top, total, out = lax.map(one_owner, jnp.arange(N_KV, dtype=jnp.int32))
    top = top.reshape((TOTAL_SLOTS,) + top.shape[2:])
    total = total.reshape((TOTAL_SLOTS,) + total.shape[2:])
    out = out.reshape((TOTAL_SLOTS,) + out.shape[2:])
    grid = queries.astype(jnp.float32).reshape(STEPS, rows, KVH, group, HD)
    fresh_keys = new_keys.astype(jnp.float32).reshape(STEPS, rows, KVH, HD)
    fresh_values = new_values.astype(jnp.float32).reshape(STEPS, rows, KVH, HD)
    new_scores = jnp.einsum('tbkgc,ubkc->bktgu', grid, fresh_keys) * (1.0 / math.sqrt(HD))
    order = jnp.arange(STEPS, dtype=jnp.int32)
    causal = order[None, :] <= order[:, None]
    new_scores = jnp.where(causal[:, None, :], new_scores, -jnp.inf)
    new_top = lax.optimization_barrier(jnp.max(new_scores, axis=-1))
    new_exp = jnp.exp(new_scores - new_top[..., None])
    new_total = lax.optimization_barrier(jnp.sum(new_exp, axis=-1))
    new_out = jnp.einsum('bktgu,ubkc->bktgc', new_exp, fresh_values)
    row_top = new_top.at[slot_row].max(top)
    scale = total * jnp.exp(top - row_top[slot_row])
    new_scale = jnp.exp(new_top - row_top)
    row_total = new_total * new_scale + jax.ops.segment_sum(scale, slot_row, num_segments=rows)
    numer = new_out * new_scale[..., None] + jax.ops.segment_sum(scale[..., None] * out.astype(jnp.float32), slot_row, num_segments=rows)
    result = numer / row_total[..., None]
    result = jnp.transpose(result, (2, 0, 1, 3, 4)).reshape(STEPS, rows, HQ * HD)
    return result.astype(jnp.bfloat16)
```

```python
import functools
import heapq
import math

import jax
import jax.numpy as jnp
from jax import lax
from jax.experimental import pallas as pl
from jax.experimental.pallas import tpu as pltpu
from jax.sharding import PartitionSpec as P

HD = 128
NEG = -1e30
MESH = pl.DeviceIdType.MESH
F32 = jnp.float32
BF16 = jnp.bfloat16


class Dims:
    def __init__(self, ny, nz, ntp, rows_dev, slots, slot_len, steps, kv_local, group):
        self.ny, self.nz, self.ntp, self.rd = ny, nz, ntp, rows_dev
        self.slots, self.slot_len = slots, slot_len
        self.steps, self.kvl, self.group = steps, kv_local, group
        self.rg = rows_dev * ntp
        self.kv = ny * nz * 2
        self.rows = self.kv * self.rg
        self.q = steps * kv_local * group
        self.split = (5 * self.rg) // 8
        self.size = {"y": ny, "z": nz}
        self.hops = {a: (n // 2, n - 1 - n // 2) for a, n in self.size.items()}
        self.rows_of = ((0, self.split), (self.split, self.rg - self.split))


def gather_order(d):
    sizes = [n * d.q * HD * 2 for _, n in d.rows_of]
    free = {"y": 0.0, "z": 0.0}
    heap, order, count = [], [], [0]

    def send(now, msg):
        part, phase = msg[0], msg[1]
        axis = "zy"[part] if phase == 1 else "yz"[part]
        begin = max(now, free[axis])
        free[axis] = begin + sizes[part] / 100e3
        count[0] += 1
        heapq.heappush(heap, (free[axis] + 2.0, count[0], msg))

    for msg in gather_children(d, None):
        send(0.0, msg)
    while heap:
        now, _, msg = heapq.heappop(heap)
        order.append(msg)
        for child in gather_children(d, msg):
            send(now, child)
    return order


def gather_children(d, msg):
    out = []
    if msg is None:
        for phase in (1, 2):
            for part in (0, 1):
                axis = "zy"[part] if phase == 1 else "yz"[part]
                for way in (0, 1):
                    if d.hops[axis][way] >= 1:
                        out.append((part, phase, way, 1, 0))
        return out
    part, phase, way, j, oa = msg
    first, second = ("z", "y") if part == 0 else ("y", "z")
    axis = first if phase == 1 else second
    if j < d.hops[axis][way]:
        out.append((part, phase, way, j + 1, oa))
    if phase == 1:
        here = -j if way == 0 else j
        for w2 in (0, 1):
            if d.hops[second][w2] >= 1:
                out.append((part, 2, w2, 1, here))
    return out


def iota(shape, dim):
    return lax.broadcasted_iota(jnp.int32, shape, dim)


def slot_plan(d, kv, ps, ctx, out, pieces):
    partner = kv + 1 - 2 * lax.rem(kv, 2)
    core = lax.rem(kv, 2)
    chunks = d.rows // 128
    eye = iota((128, 128), 0) == iota((128, 128), 1)
    lane = iota((128, 128), 1)
    row_in = iota((128, 128), 0)

    def to_col(row):
        return jnp.sum(jnp.where(eye, jnp.broadcast_to(row, (128, 128)), 0), axis=1, keepdims=True)

    def to_row(col):
        return jnp.sum(jnp.where(eye, jnp.broadcast_to(col, (128, 128)), 0), axis=0, keepdims=True)

    zero = jnp.zeros((1, 128), jnp.int32)
    state = [[jnp.zeros((1, 1), jnp.int32), zero, zero] for _ in (0, 1)]

    def piece(side, c):
        base, acc_val, acc_row = state[side]
        owner = kv if side == 0 else partner
        local = ps[c * 128 : (c + 1) * 128, :] - owner * d.slots
        hit = (local >= 0) & (local < d.slots)
        many = jnp.sum(hit.astype(jnp.int32), axis=1, keepdims=True)
        many_row = to_row(many)
        before = jnp.sum(jnp.where(row_in < lane, many, 0), axis=0, keepdims=True)
        start_row = before + base
        last = jnp.where(many_row > 0, jnp.minimum(start_row + many_row - 1, d.slots), d.slots)
        out[5 + side * chunks + c : 6 + side * chunks + c, :] = last
        base = base + jnp.sum(many_row, axis=1, keepdims=True)
        start = to_col(start_row)
        if side == 0:
            length = to_col(ctx[c : c + 1, :])
            left = jnp.clip(length - lane * d.slot_len, 0, d.slot_len)
            far = 1 << 30
            code = jnp.where(hit, lane * 32768 + local * 512 + left, far)
        for k in range(3):
            at = (lane == start + k) & (many > k)
            acc_row += jnp.sum(jnp.where(at, row_in + c * 128, 0), axis=0, keepdims=True)
            if side == 0:
                first = jnp.min(code, axis=1, keepdims=True)
                code = jnp.where(code == first, far, code)
                acc_val += jnp.sum(jnp.where(at, lax.rem(first, 32768), 0), axis=0, keepdims=True)
        state[side] = [base, acc_val, acc_row]

    def finish():
        for side in (0, 1):
            _, acc_val, acc_row = state[side]
            mine = lax.rem(acc_row // d.rg, 2) == core
            place = (acc_row // (2 * d.rg)) * d.rg + lax.rem(acc_row, d.rg)
            place = jnp.clip(place, 0, d.rows // 2 - 1)
            if side == 0:
                same = (iota((1, 128), 1) > 0) & (pltpu.roll(acc_row, 1, 1) == acc_row)
                out[0:1, :] = jnp.where(mine, place, -1)
                out[1:2, :] = jnp.clip(acc_val // 512, 0, d.slots - 1)
                out[2:3, :] = lax.rem(acc_val, 512)
                out[3:4, :] = jnp.where(same, 1, 0)
            else:
                out[4:5, :] = jnp.where(mine, place, 0)

    for c in range(chunks):
        for side in (0, 1):
            pieces.append(functools.partial(piece, side, c))
    pieces.append(finish)


def main_kernel(
    d, order, ps, ctx, qx, nk, nv, kc, vc, out,
    psv, planv, meta, g, qp, qs, kb, vb, o, t, r0, r0s, r1, r1s, d0, d0s, d1, d1s, f, fs, rf, rfs,
    io_sem, kv_sem, tp_send, tp_recv, ag_send, ag_recv, fw_send, fw_recv, ex_send, ex_recv,
    s0_send, s0_recv, s1_send, s1_recv, fin_send, fin_recv,
):
    kv = lax.axis_index("kv")
    tp = lax.axis_index("tp")
    core = lax.rem(kv, 2)
    sgn = 1 - 2 * core
    chip = kv // 2
    pos = {"y": chip // d.nz, "z": lax.rem(chip, d.nz)}

    near = {}

    def coord(axis, k):
        n = d.size[axis]
        if (axis, k) not in near:
            near[axis, k] = lax.rem(pos[axis] + sgn * k + n, n)
        return near[axis, k]

    def chip_at(oy, oz):
        return coord("y", oy) * d.nz + coord("z", oz)

    def kv_at(oy, oz):
        return chip_at(oy, oz) * 2 + core

    def neighbour(axis, step):
        return (kv_at(step, 0) if axis == "y" else kv_at(0, step), tp)

    partner = (kv + sgn, tp)

    def remote(src, dst, ss, rs, dev):
        return pltpu.make_async_remote_copy(
            src_ref=src, dst_ref=dst, send_sem=ss, recv_sem=rs, device_id=dev, device_id_type=MESH
        )

    chunks = d.rows // 128

    ps_copy = pltpu.make_async_copy(ps, psv, io_sem.at[0])
    ps_copy.start()
    parts_kv = kv_sem.shape[1]
    per = d.slots // parts_kv
    kv_copies = []
    for n in range(parts_kv):
        for which, (src, dst) in enumerate(((kc, kb), (vc, vb))):
            cp = pltpu.make_async_copy(
                src.at[pl.ds(n * per, per)], dst.at[pl.ds(n * per, per)], kv_sem.at[which, n]
            )
            cp.start()
            kv_copies.append(cp)

    friends = [partner]
    for axis in ("y", "z"):
        for way in (0, 1):
            if d.hops[axis][way]:
                friends.append(neighbour(axis, 1 - 2 * way))
    for k in range(1, d.ntp):
        friends.append((kv, lax.rem(tp + k, d.ntp)))
    barrier = pltpu.get_barrier_semaphore()
    for dev in friends:
        pl.semaphore_signal(barrier, inc=1, device_id=dev, device_id_type=MESH)
    pl.semaphore_wait(barrier, len(friends))

    waits = []

    own = chip * d.rg
    tp_copies = []
    for k in range(1, d.ntp):
        other = lax.rem(tp + k, d.ntp)
        cp = remote(
            qx.at[other], g.at[pl.ds(own + tp * d.rd, d.rd)], tp_send.at[k - 1], tp_recv.at[k - 1], (kv, other)
        )
        cp.start()
        waits.append(cp)
    g[pl.ds(own + tp * d.rd, d.rd)] = qx[tp]
    for k in range(1, d.ntp):
        source = lax.rem(tp - k + d.ntp, d.ntp)
        remote(
            qx.at[tp], g.at[pl.ds(own + source * d.rd, d.rd)], tp_send.at[k - 1], tp_recv.at[k - 1], (kv, source)
        ).wait_recv()

    number = {msg: n for n, msg in enumerate(order)}

    def place(msg, back):
        part, phase, way, j, oa = msg
        turn = 1 if way == 0 else -1
        steps = j - 1 if back else j
        o1 = -turn * steps if phase == 1 else oa
        o2 = 0 if phase == 1 else -turn * steps
        oz, oy = (o1, o2) if part == 0 else (o2, o1)
        start, count = d.rows_of[part]
        return g.at[pl.ds(chip_at(oy, oz) * d.rg + start, count)]

    def ship(msg):
        part, phase, way, j, oa = msg
        axis = "zy"[part] if phase == 1 else "yz"[part]
        n = number[msg]
        src = place(msg, True)
        cp = remote(src, src, ag_send.at[n], ag_recv.at[n], neighbour(axis, 1 - 2 * way))
        cp.start()
        waits.append(cp)

    for msg in gather_children(d, None):
        ship(msg)
    ps_copy.wait()
    pieces = []
    slot_plan(d, kv, psv, ctx, planv, pieces)
    plan_copy = pltpu.make_async_copy(planv, meta, io_sem.at[1])
    for place_in, msg in enumerate(order):
        n = number[msg]
        landed = place(msg, False)
        remote(landed, landed, ag_send.at[n], ag_recv.at[n], partner).wait_recv()
        for child in gather_children(d, msg):
            ship(child)
        if place_in >= 8 and place_in % 3 == 0 and pieces:
            pieces.pop(0)()
    while pieces:
        pieces.pop(0)()
    plan_copy.start()
    plan_copy.wait()

    def pick(i, c):
        for u in range(4):
            qs[4 * i + u] = g[meta[4, 4 * i + u]]
        return c

    lax.fori_loop(0, d.slots // 4, pick, 0)
    cp = remote(qs, qp, fw_send.at[0], fw_recv.at[0], partner)
    cp.start()
    for copy in kv_copies:
        copy.wait()
    cp.wait()

    head = lax.rem(iota((d.q, 128), 0) // d.group, d.kvl)
    head_masks = [(head == k).astype(F32).astype(BF16) for k in range(d.kvl)]
    lane128 = iota((d.q, 128), 1)
    lane_slot = iota((d.q, d.slot_len), 1)
    scale = 1.0 / math.sqrt(HD)

    unroll = 4

    def attend_many(it, carry):
        m_p, l_p, o_p, mc, lc = carry
        at = [it * unroll + u for u in range(unroll)]
        rows = [meta[0, i] for i in at]
        qs = [jnp.where(row >= 0, g[jnp.maximum(row, 0)], qp[i]) for row, i in zip(rows, at)]
        q2 = [jnp.concatenate([q * mask for mask in head_masks], axis=1) for q in qs]
        slots = [meta[1, i] for i in at]
        score = [
            lax.dot_general(q, kb[slot], (((1,), (1,)), ((), ())), preferred_element_type=F32)
            for q, slot in zip(q2, slots)
        ]
        score = [jnp.where(lane_slot < meta[2, i], x * scale, NEG) for x, i in zip(score, at)]
        tops = [jnp.max(x, axis=1, keepdims=True) for x in score]
        ps = [jnp.exp(x - m) for x, m in zip(score, tops)]
        sums = [jnp.dot(p.astype(BF16), vb[slot], preferred_element_type=F32) for p, slot in zip(ps, slots)]
        totals = [jnp.sum(p, axis=1, keepdims=True) for p in ps]
        accs = []
        for u, i in enumerate(at):
            o_s = sums[u][:, :HD]
            for k in range(1, d.kvl):
                o_s = jnp.where(head == k, sums[u][:, k * HD : (k + 1) * HD], o_s)
            m_q = jnp.where(meta[3, i] > 0, m_p, NEG)
            m = jnp.maximum(m_q, tops[u])
            a, b = jnp.exp(m_q - m), jnp.exp(tops[u] - m)
            l_p = l_p * a + totals[u] * b
            o_p = o_p * a + o_s * b
            m_p = m
            accs.append(o_p.astype(BF16))
            mc = jnp.where(lane128 == i, m_p, mc)
            lc = jnp.where(lane128 == i, l_p, lc)
        for u, i in enumerate(at):
            o[0, i] = accs[u]
        return m_p, l_p, o_p, mc, lc

    zero_col = jnp.zeros((d.q, 1), F32)
    zero = jnp.zeros((d.q, 128), F32)
    _, _, _, mc, lc = lax.fori_loop(
        0, d.slots // unroll, attend_many, (zero_col, zero_col, zero, jnp.full((d.q, 128), NEG, F32), zero)
    )
    pad = jnp.zeros((128 - d.q, 128), F32)
    mt = jnp.transpose(jnp.concatenate([mc, pad], axis=0))
    lt = jnp.transpose(jnp.concatenate([lc, pad], axis=0))
    table = jnp.where(iota((128, 128), 1) < 64, mt, pltpu.roll(lt, 64, 1))
    spare = t.shape[1] - d.slots
    t[0] = table[: t.shape[1]]
    nobody = jnp.where(iota((spare, 128), 1) < 64, NEG, 0.0)
    for side in (0, 1):
        t[side, pl.ds(d.slots, spare)] = nobody
        o[side, d.slots] = jnp.zeros((d.q, 128), BF16)

    for n, ref in enumerate((o, t)):
        cp = remote(
            ref.at[0, pl.ds(0, d.slots)], ref.at[1, pl.ds(0, d.slots)], ex_send.at[n], ex_recv.at[n], partner
        )
        cp.start()
        waits.append(cp)
    for n, ref in enumerate((o, t)):
        remote(
            ref.at[0, pl.ds(0, d.slots)], ref.at[1, pl.ds(0, d.slots)], ex_send.at[n], ex_recv.at[n], partner
        ).wait_recv()

    lane8 = iota((8, 128), 1)

    def pad8(x):
        if x.shape[0] == 8:
            return x
        return jnp.concatenate([x, jnp.zeros((8 - x.shape[0], 128), F32)], axis=0)

    def prepare(stats, count):
        top = functools.reduce(jnp.maximum, stats)
        es = [jnp.exp(st - top) for st in stats]
        total = sum(e * pltpu.roll(st, 64, 1) for e, st in zip(es, stats))
        tile = jnp.where(lane8 < 64, top, pltpu.roll(total, 64, 1))[:count]
        return tile, jnp.transpose(jnp.concatenate(es, axis=0))

    def apply(tile, cols, rows, many, count, out_d, out_s):
        out_s[...] = tile
        for r in range(count):
            acc = None
            for k in range(many):
                term = rows(k, r).astype(F32) * cols[: d.q, k * 8 + r : k * 8 + r + 1]
                acc = term if acc is None else acc + term
            out_d[r] = acc.astype(BF16)

    def merge(jobs, count):
        tiles = [[pad8(x[1][...]) for x in ins] for ins, _ in jobs]
        ready = [prepare(stats, count) for stats in tiles]
        for (ins, dst), (tile, cols) in zip(jobs, ready):
            apply(tile, cols, lambda k, r: ins[k][0][r], len(ins), count, *dst)

    per_row = 128 // d.rg

    class Part:
        def __init__(self, first, second, rows, recv, recv_s, mine, mine_s, send_sem, recv_sem):
            self.first, self.second = first, second
            self.start, self.count = rows
            self.recv, self.recv_s, self.mine, self.mine_s = recv, recv_s, mine, mine_s
            self.send_sem, self.recv_sem = send_sem, recv_sem
            self.n1, self.lanes = d.size[first], d.size[second]
            self.h1, self.h2 = d.hops[first], d.hops[second]
            self.phase2 = sum(self.h1) * self.lanes
            self.to = {
                (axis, way): neighbour(axis, 1 - 2 * way) for axis in (first, second) for way in (0, 1)
            }

        def id1(self, way, j, lane):
            return (way * self.h1[0] + j - 1) * self.lanes + lane

        def id2(self, way, j):
            return self.phase2 + way * self.h2[0] + j - 1

        def bufs(self, n):
            return self.recv.at[n], self.recv_s.at[n]

        def chip_sum(self, o1, lane):
            n = (o1 % self.n1) * self.lanes + lane
            return self.mine.at[n], self.mine_s.at[n]

        def copies(self, src, n, axis, way):
            return [
                remote(a, b, self.send_sem.at[k, n], self.recv_sem.at[k, n], self.to[axis, way])
                for k, (a, b) in enumerate(zip(src, self.bufs(n)))
            ]

        def send(self, src, n, axis, way):
            for cp in self.copies(src, n, axis, way):
                cp.start()

        def wait(self, n):
            for cp in self.copies(self.bufs(n), n, self.first, 0):
                cp.wait_recv()

        def wait_sent(self, n):
            for cp in self.copies(self.bufs(n), n, self.first, 0):
                cp.wait_send()

        def lane(self, k):
            return (self.h2[0] + ((k + 1) // 2) * (1 if k % 2 else -1)) % self.lanes

        def build(self, offsets, k):
            lane = self.lane(k)
            jobs = []
            for o1 in offsets:
                oy, oz = (o1, lane) if self.first == "y" else (lane, o1)
                kv_to = kv_at(oy, oz)
                line, col = lax.div(kv_to, per_row), lax.rem(kv_to, per_row) * d.rg + self.start
                ids, stats = [], []
                for side in (0, 1):
                    ids.append([meta[5 + side * chunks + line, col + r] for r in range(self.count)])
                    stats.append(
                        pad8(jnp.concatenate([t[side, pl.ds(i, 1), :] for i in ids[side]], axis=0))
                    )
                jobs.append((ids, stats, self.chip_sum(o1, lane)))
            ready = [prepare(stats, self.count) for _, stats, _ in jobs]
            for (ids, _, dst), (tile, cols) in zip(jobs, ready):
                apply(tile, cols, lambda k, r: o[k, ids[k][r]], 2, self.count, *dst)

        def launch(self, k):
            ways = [way for way in (0, 1) if self.h1[way]]
            far = [(1 - 2 * way) * self.h1[way] for way in ways]
            self.build(far, k)
            lane = self.lane(k)
            for way, o1 in zip(ways, far):
                self.send(self.chip_sum(o1, lane), self.id1(way, 1, lane), self.first, way)

        def rest(self, k):
            for j in range(1, self.h1[0]):
                ways = [way for way in (0, 1) if j < self.h1[way]]
                self.build([(1 - 2 * way) * (self.h1[way] - j) for way in ways], k)
            self.build([0], k)

        def relay(self, j, k):
            lane = self.lane(k)
            ways = [way for way in (0, 1) if j < self.h1[way]]
            jobs = []
            for way in ways:
                n = self.id1(way, j, lane)
                self.wait(n)
                left = (1 - 2 * way) * (self.h1[way] - j)
                jobs.append(([self.bufs(n), self.chip_sum(left, lane)], self.bufs(n)))
            merge(jobs, self.count)
            for way, (_, src) in zip(ways, jobs):
                self.send(src, self.id1(way, j + 1, lane), self.first, way)

        def second_step(self, k, result):
            lane = self.lane(k)
            ids = [self.id1(way, self.h1[way], lane) for way in (0, 1) if self.h1[way]]
            last = k == self.lanes - 1
            if last:
                ids += [self.id2(way, self.h2[way]) for way in (0, 1) if self.h2[way]]
            elif k >= 2:
                ids.append(self.id2(k % 2, k // 2))
            for n in ids:
                self.wait(n)
            ins = [self.bufs(n) for n in ids] + [self.chip_sum(0, lane)]
            dst = result if last else ins[0]
            merge([(ins, dst)], self.count)
            if not last:
                self.send(dst, self.id2(k % 2, k // 2 + 1), self.second, k % 2)

        def drain(self):
            def body(n, c):
                self.wait_sent(n)
                return c

            lax.fori_loop(0, self.phase2 + sum(self.h2), body, 0)

    p0 = Part("y", "z", d.rows_of[0], r0, r0s, d0, d0s, s0_send, s0_recv)
    p1 = Part("z", "y", d.rows_of[1], r1, r1s, d1, d1s, s1_send, s1_recv)
    fin0 = (f.at[pl.ds(p0.start, p0.count)], fs.at[pl.ds(p0.start, p0.count)])
    fin1 = (f.at[pl.ds(p1.start, p1.count)], fs.at[pl.ds(p1.start, p1.count)])

    lag = 2
    steps = []
    for n, (p, fin) in enumerate(((p1, fin1), (p0, fin0))):
        last = p.lanes - 1
        for k in range(p.lanes):
            steps.append((k, 4, n, functools.partial(p.launch, k)))
            steps.append((k, 5, n, functools.partial(p.rest, k)))
            for j in range(1, p.h1[0]):
                steps.append((k + lag * j, 1, n, functools.partial(p.relay, j, k)))
            late = lag * p.h1[0] + k + (lag - 1 if k == last else 0)
            steps.append((late, 3, n, functools.partial(p.second_step, k, fin)))
    steps.sort(key=lambda x: x[:3])
    for _, _, _, run in steps:
        run()

    for n in range(d.ntp):
        for i in range(d.rd):
            rfs_row = fs[n * d.rd + i : n * d.rd + i + 1, :]
            b1s_tmp = rfs_row
            rfs.at[d.ntp + n][i : i + 1, :] = b1s_tmp

    def final(k, dst_t, src_t, dev_t):
        return [
            remote(f.at[pl.ds(src_t * d.rd, d.rd)], rf.at[dst_t], fin_send.at[0, k], fin_recv.at[0, k], (kv, dev_t)),
            remote(rfs.at[d.ntp + src_t], rfs.at[dst_t], fin_send.at[1, k], fin_recv.at[1, k], (kv, dev_t)),
        ]

    for k in range(1, d.ntp):
        other = lax.rem(tp + k, d.ntp)
        for cp in final(k - 1, tp, other, other):
            cp.start()
            waits.append(cp)
    rf[tp] = f[pl.ds(tp * d.rd, d.rd)]
    rfs[tp] = rfs[d.ntp + tp]

    nkf, nvf = nk[...].astype(F32), nv[...].astype(F32)
    fresh = []
    for h in range(d.ntp):
        for i in range(d.rd):
            tops, totals, outs = [], [], []
            qf = qx[h, i].astype(F32)
            for step in range(d.steps):
                for k in range(d.kvl):
                    at = (step * d.kvl + k) * d.group
                    kk = h * d.kvl + k
                    qs = qf[at : at + d.group]
                    scores = [
                        jnp.sum(qs * nkf[u, i, kk : kk + 1, :], axis=1, keepdims=True) * scale
                        for u in range(step + 1)
                    ]
                    top = functools.reduce(jnp.maximum, scores)
                    ws = [jnp.exp(x - top) for x in scores]
                    tops.append(top)
                    totals.append(sum(ws))
                    outs.append(sum(w * nvf[u, i, kk : kk + 1, :] for u, w in enumerate(ws)))
            fresh.append([jnp.concatenate(x, axis=0) for x in (tops, totals, outs)])

    for k in range(1, d.ntp):
        source = lax.rem(tp - k + d.ntp, d.ntp)
        for cp in final(k - 1, source, tp, source):
            cp.wait_recv()
    for h in range(d.ntp):
        cols = jnp.transpose(pad8(rfs[h]))
        for i in range(d.rd):
            top_n, total_n, out_n = fresh[h * d.rd + i]
            top_c, total_c = cols[: d.q, i : i + 1], cols[64 : 64 + d.q, i : i + 1]
            top = jnp.maximum(top_n, top_c)
            a, b = jnp.exp(top_n - top), jnp.exp(top_c - top)
            numer = out_n * a + rf[h, i].astype(F32) * b
            out[h, i] = (numer / (total_n * a + total_c * b)).astype(BF16)

    for cp in waits:
        cp.wait_send()
    p0.drain()
    p1.drain()


def make_shards(d):
    order = gather_order(d)

    def shards(queries, new_keys, new_values, key_cache, value_cache, context_lengths, piece_slots):
        steps, rd, width = queries.shape
        chunks = d.rows // 128
        vmem = pl.BlockSpec(memory_space=pltpu.VMEM)
        hbm = pl.BlockSpec(memory_space=pl.ANY)
        qh = queries.reshape(steps, rd, d.ntp, d.kvl * d.group, HD)
        qx = jnp.transpose(qh, (2, 1, 0, 3, 4)).reshape(d.ntp, rd, d.q, HD)
        nk = new_keys.reshape(steps, rd, d.ntp * d.kvl, HD)
        nv = new_values.reshape(steps, rd, d.ntp * d.kvl, HD)
        c0, c1 = d.rows_of[0][1], d.rows_of[1][1]
        n0 = sum(d.hops["y"]) * d.nz + sum(d.hops["z"])
        n1 = sum(d.hops["z"]) * d.ny + sum(d.hops["y"])
        pad = d.slots + 8
        dma = pltpu.SemaphoreType.DMA
        sem = lambda *shape: dma(shape)
        nt = max(d.ntp - 1, 1)
        plan_rows = -(-(5 + 2 * chunks) // 8) * 8
        scratch = [
            pltpu.VMEM(piece_slots.shape, jnp.int32),
            pltpu.VMEM((plan_rows, 128), jnp.int32),
            pltpu.SMEM((plan_rows, 128), jnp.int32),
            pltpu.VMEM((d.rows // 2, d.q, HD), BF16),
            pltpu.VMEM((d.slots, d.q, HD), BF16),
            pltpu.VMEM((d.slots, d.q, HD), BF16),
            pltpu.VMEM(key_cache.shape, BF16),
            pltpu.VMEM(value_cache.shape, BF16),
            pltpu.VMEM((2, pad, d.q, HD), BF16),
            pltpu.VMEM((2, pad, 128), F32),
            pltpu.VMEM((n0, c0, d.q, HD), BF16),
            pltpu.VMEM((n0, c0, 128), F32),
            pltpu.VMEM((n1, c1, d.q, HD), BF16),
            pltpu.VMEM((n1, c1, 128), F32),
            pltpu.VMEM((d.ny * d.nz, c0, d.q, HD), BF16),
            pltpu.VMEM((d.ny * d.nz, c0, 128), F32),
            pltpu.VMEM((d.ny * d.nz, c1, d.q, HD), BF16),
            pltpu.VMEM((d.ny * d.nz, c1, 128), F32),
            pltpu.VMEM((d.rg, d.q, HD), BF16),
            pltpu.VMEM((d.rg, 128), F32),
            pltpu.VMEM((d.ntp, rd, d.q, HD), BF16),
            pltpu.VMEM((2 * d.ntp, rd, 128), F32),
            sem(2), sem(2, 4), sem(nt), sem(nt), sem(len(order)), sem(len(order)), sem(1), sem(1),
            sem(2), sem(2), sem(2, n0), sem(2, n0), sem(2, n1), sem(2, n1), sem(2, nt), sem(2, nt),
        ]
        result = pl.pallas_call(
            functools.partial(main_kernel, d, order),
            out_shape=jax.ShapeDtypeStruct((d.ntp, rd, d.q, HD), BF16),
            in_specs=[hbm, vmem, vmem, vmem, vmem, hbm, hbm],
            out_specs=vmem,
            scratch_shapes=scratch,
            compiler_params=pltpu.CompilerParams(
                collective_id=0, has_side_effects=True, vmem_limit_bytes=60 * 1024 * 1024
            ),
        )(piece_slots, context_lengths.reshape(chunks, 128), qx, nk, nv, key_cache, value_cache)
        result = result.reshape(d.ntp, rd, steps, d.kvl * d.group, HD)
        return jnp.transpose(result, (2, 1, 0, 3, 4)).reshape(steps, rd, width)

    return shards


def solution(mesh):
    d = Dims(4, 8, 4, 2, 40, 256, 3, 2, 8)
    return build(mesh, d)


def build(mesh, d):
    placed = (
        P(None, ("kv", "tp"), None),
        P(None, ("kv", "tp"), None),
        P(None, ("kv", "tp"), None),
        P("kv", None, "tp"),
        P("kv", None, "tp"),
        P(),
        P(),
    )
    return jax.shard_map(
        make_shards(d),
        mesh=mesh,
        in_specs=placed,
        out_specs=P(None, ("kv", "tp"), None),
        check_vma=False,
    )
```

```python
import functools
import math

import jax
import jax.numpy as jnp
from jax import lax
from jax.experimental import pallas as pl
from jax.experimental.pallas import tpu as pltpu
from jax.sharding import PartitionSpec as P

HD = 128
NEG = -1e30
MESH = pl.DeviceIdType.MESH
F32 = jnp.float32
BF16 = jnp.bfloat16


class Dims:
    def __init__(self, ny, nz, ntp, rows_dev, slots, slot_len, steps, kv_local, group):
        self.ny, self.nz, self.ntp, self.rd = ny, nz, ntp, rows_dev
        self.slots, self.slot_len = slots, slot_len
        self.steps, self.kvl, self.group = steps, kv_local, group
        self.rg = rows_dev * ntp
        self.kv = ny * nz * 2
        self.rows = self.kv * self.rg
        self.q = steps * kv_local * group
        self.split = (5 * self.rg) // 8
        self.size = {"y": ny, "z": nz}
        self.hops = {a: (n // 2, n - 1 - n // 2) for a, n in self.size.items()}
        self.rows_of = ((0, self.split), (self.split, self.rg - self.split))


def list_order(tasks, limit, latency=1.75, rate=95e3, tick=0.02):
    left = {t[0]: t for t in tasks}
    flying = {"y": [], "z": []}
    arrived, order = {}, []
    now, busy, running = 0.0, 0.0, None
    while left or running:
        if now >= busy - 1e-9:
            if running:
                for msg, axis, size in running[4]:
                    flying[axis].append([msg, size])
                running = None
            ready, urgent = [], set()
            for name, _, waits, before, _, paced, rank in left.values():
                if any(arrived.get(w, 1e9) > now for w in waits):
                    continue
                if any(x in left for x in before):
                    urgent.update(before)
                elif not paced or len(flying[paced]) < limit:
                    ready.append((rank, name))
            ready = [((0.5,) + r[1:] if n in urgent and r[0] > 0.5 else r, n) for r, n in ready]
            if ready:
                name = min(ready)[1]
                running = left.pop(name)
                order.append(name)
                busy = now + running[1]
        for axis, copies in flying.items():
            for c in copies:
                c[1] -= rate * tick / len(copies)
                if c[1] <= 0:
                    arrived[c[0]] = now + tick + latency
            flying[axis] = [c for c in copies if c[1] > 0]
        now += tick
    return order


def gather_order(d, limit=2):
    tasks, depth = [], {}

    def hops(msg):
        return max([1 + hops(c) for c in gather_children(d, msg)], default=0)

    def add(msg):
        for child in gather_children(d, msg):
            part, phase = child[0], child[1]
            axis = "zy"[part] if phase == 1 else "yz"[part]
            size = d.rows_of[part][1] * d.q * HD * 2
            before = [("wait", msg)] if msg else []
            rank = (0, -hops(child), len(tasks))
            tasks.append((("send", child), 0.06, [], before, [(child, axis, size)], axis, rank))
            tasks.append((("wait", child), 0.12, [child], [], [], None, (1, 0, len(tasks))))
            add(child)

    add(None)
    return list_order(tasks, limit)


def gather_children(d, msg):
    out = []
    if msg is None:
        for phase in (1, 2):
            for part in (0, 1):
                axis = "zy"[part] if phase == 1 else "yz"[part]
                for way in (0, 1):
                    if d.hops[axis][way] >= 1:
                        out.append((part, phase, way, 1, 0))
        return out
    part, phase, way, j, oa = msg
    first, second = ("z", "y") if part == 0 else ("y", "z")
    axis = first if phase == 1 else second
    if j < d.hops[axis][way]:
        out.append((part, phase, way, j + 1, oa))
    if phase == 1:
        here = -j if way == 0 else j
        for w2 in (0, 1):
            if d.hops[second][w2] >= 1:
                out.append((part, 2, w2, 1, here))
    return out


def iota(shape, dim):
    return lax.broadcasted_iota(jnp.int32, shape, dim)


def slot_plan(d, kv, ps, ctx, out, pieces):
    partner = kv + 1 - 2 * lax.rem(kv, 2)
    core = lax.rem(kv, 2)
    chunks = d.rows // 128
    eye = iota((128, 128), 0) == iota((128, 128), 1)
    lane = iota((128, 128), 1)
    row_in = iota((128, 128), 0)

    def to_col(row):
        return jnp.sum(jnp.where(eye, jnp.broadcast_to(row, (128, 128)), 0), axis=1, keepdims=True)

    def to_row(col):
        return jnp.sum(jnp.where(eye, jnp.broadcast_to(col, (128, 128)), 0), axis=0, keepdims=True)

    zero = jnp.zeros((1, 128), jnp.int32)
    state = [[jnp.zeros((1, 1), jnp.int32), zero, zero] for _ in (0, 1)]

    def piece(side, c):
        base, acc_val, acc_row = state[side]
        owner = kv if side == 0 else partner
        local = ps[c * 128 : (c + 1) * 128, :] - owner * d.slots
        hit = (local >= 0) & (local < d.slots)
        many = jnp.sum(hit.astype(jnp.int32), axis=1, keepdims=True)
        many_row = to_row(many)
        before = jnp.sum(jnp.where(row_in < lane, many, 0), axis=0, keepdims=True)
        start_row = before + base
        last = jnp.where(many_row > 0, jnp.minimum(start_row + many_row - 1, d.slots), d.slots)
        out[5 + side * chunks + c : 6 + side * chunks + c, :] = last
        base = base + jnp.sum(many_row, axis=1, keepdims=True)
        start = to_col(start_row)
        if side == 0:
            length = to_col(ctx[c : c + 1, :])
            left = jnp.clip(length - lane * d.slot_len, 0, d.slot_len)
            far = 1 << 30
            code = jnp.where(hit, lane * 32768 + local * 512 + left, far)
        for k in range(3):
            at = (lane == start + k) & (many > k)
            acc_row += jnp.sum(jnp.where(at, row_in + c * 128, 0), axis=0, keepdims=True)
            if side == 0:
                first = jnp.min(code, axis=1, keepdims=True)
                code = jnp.where(code == first, far, code)
                acc_val += jnp.sum(jnp.where(at, lax.rem(first, 32768), 0), axis=0, keepdims=True)
        state[side] = [base, acc_val, acc_row]

    def finish():
        for side in (0, 1):
            _, acc_val, acc_row = state[side]
            mine = lax.rem(acc_row // d.rg, 2) == core
            place = (acc_row // (2 * d.rg)) * d.rg + lax.rem(acc_row, d.rg)
            place = jnp.clip(place, 0, d.rows // 2 - 1)
            if side == 0:
                same = (iota((1, 128), 1) > 0) & (pltpu.roll(acc_row, 1, 1) == acc_row)
                out[0:1, :] = jnp.where(mine, place, -1)
                out[1:2, :] = jnp.clip(acc_val // 512, 0, d.slots - 1)
                out[2:3, :] = lax.rem(acc_val, 512)
                out[3:4, :] = jnp.where(same, 1, 0)
            else:
                out[4:5, :] = jnp.where(mine, place, 0)

    for c in range(chunks):
        for side in (0, 1):
            pieces.append(functools.partial(piece, side, c))
    pieces.append(finish)


def main_kernel(
    d, order, ps, ctx, q_in, nk_in, nv_in, kc, vc, out,
    q_raw, nk, nv, stage, wide, qx, psv, planv, meta, g, qp, qs, kb, vb, o, t, r0, r0s, r1, r1s, d0, d0s, d1, d1s, f, fs, rf, rfs,
    io_sem, kv_sem, tp_send, tp_recv, ag_send, ag_recv, fw_send, fw_recv, ex_send, ex_recv,
    s0_send, s0_recv, s1_send, s1_recv, fin_send, fin_recv,
):
    kv = lax.axis_index("kv")
    tp = lax.axis_index("tp")
    core = lax.rem(kv, 2)
    sgn = 1 - 2 * core
    chip = kv // 2
    pos = {"y": chip // d.nz, "z": lax.rem(chip, d.nz)}

    near = {}

    def coord(axis, k):
        n = d.size[axis]
        if (axis, k) not in near:
            near[axis, k] = lax.rem(pos[axis] + sgn * k + n, n)
        return near[axis, k]

    def chip_at(oy, oz):
        return coord("y", oy) * d.nz + coord("z", oz)

    def kv_at(oy, oz):
        return chip_at(oy, oz) * 2 + core

    def neighbour(axis, step):
        return (kv_at(step, 0) if axis == "y" else kv_at(0, step), tp)

    partner = (kv + sgn, tp)

    def remote(src, dst, ss, rs, dev):
        return pltpu.make_async_remote_copy(
            src_ref=src, dst_ref=dst, send_sem=ss, recv_sem=rs, device_id=dev, device_id_type=MESH
        )

    chunks = d.rows // 128

    q_copy = pltpu.make_async_copy(q_in, q_raw, io_sem.at[2])
    q_copy.start()
    new_copies = [
        pltpu.make_async_copy(src, dst, io_sem.at[n])
        for n, (src, dst) in enumerate(((nk_in, nk), (nv_in, nv)), 3)
    ]
    for cp in new_copies:
        cp.start()
    ps_copy = pltpu.make_async_copy(ps, psv, io_sem.at[0])
    ps_copy.start()
    parts_kv = kv_sem.shape[1]
    per = d.slots // parts_kv
    kv_copies = []
    for n in range(parts_kv):
        for which, (src, dst) in enumerate(((kc, kb), (vc, vb))):
            cp = pltpu.make_async_copy(
                src.at[pl.ds(n * per, per)], dst.at[pl.ds(n * per, per)], kv_sem.at[which, n]
            )
            cp.start()
            kv_copies.append(cp)

    friends = [partner]
    for axis in ("y", "z"):
        for way in (0, 1):
            if d.hops[axis][way]:
                friends.append(neighbour(axis, 1 - 2 * way))
    for k in range(1, d.ntp):
        friends.append((kv, lax.rem(tp + k, d.ntp)))
    barrier = pltpu.get_barrier_semaphore()
    for dev in friends:
        pl.semaphore_signal(barrier, inc=1, device_id=dev, device_id_type=MESH)

    q_copy.wait()
    heads = d.kvl * d.group
    for step in range(d.steps):
        q_step = q_raw[step].astype(F32)
        for h in range(d.ntp):
            for i in range(d.rd):
                for j in range(heads):
                    at = (h * heads + j) * HD
                    stage[h, i, pl.ds(step * heads + j, 1), :] = q_step[i : i + 1, at : at + HD]
    qx[...] = stage[...].astype(BF16)
    pl.semaphore_wait(barrier, len(friends))

    waits = []

    own = chip * d.rg
    tp_copies = []
    for k in range(1, d.ntp):
        other = lax.rem(tp + k, d.ntp)
        cp = remote(
            qx.at[other], g.at[pl.ds(own + tp * d.rd, d.rd)], tp_send.at[k - 1], tp_recv.at[k - 1], (kv, other)
        )
        cp.start()
        waits.append(cp)
    g[pl.ds(own + tp * d.rd, d.rd)] = qx[tp]
    for k in range(1, d.ntp):
        source = lax.rem(tp - k + d.ntp, d.ntp)
        remote(
            qx.at[tp], g.at[pl.ds(own + source * d.rd, d.rd)], tp_send.at[k - 1], tp_recv.at[k - 1], (kv, source)
        ).wait_recv()

    number = {msg: n for n, msg in enumerate(msg for what, msg in order if what == "send")}

    def place(msg, back):
        part, phase, way, j, oa = msg
        turn = 1 if way == 0 else -1
        steps = j - 1 if back else j
        o1 = -turn * steps if phase == 1 else oa
        o2 = 0 if phase == 1 else -turn * steps
        oz, oy = (o1, o2) if part == 0 else (o2, o1)
        start, count = d.rows_of[part]
        return g.at[pl.ds(chip_at(oy, oz) * d.rg + start, count)]

    def ship(msg):
        part, phase, way, j, oa = msg
        axis = "zy"[part] if phase == 1 else "yz"[part]
        n = number[msg]
        src = place(msg, True)
        cp = remote(src, src, ag_send.at[n], ag_recv.at[n], neighbour(axis, 1 - 2 * way))
        cp.start()
        waits.append(cp)

    ps_copy.wait()
    pieces = []
    slot_plan(d, kv, psv, ctx, planv, pieces)
    plan_copy = pltpu.make_async_copy(planv, meta, io_sem.at[1])
    for place_in, (what, msg) in enumerate(order):
        if what == "send":
            ship(msg)
            continue
        n = number[msg]
        landed = place(msg, False)
        remote(landed, landed, ag_send.at[n], ag_recv.at[n], partner).wait_recv()
        if place_in >= 24 and place_in % 3 == 0 and pieces:
            pieces.pop(0)()
    while pieces:
        pieces.pop(0)()
    plan_copy.start()
    plan_copy.wait()

    def pick(i, c):
        for u in range(4):
            qs[4 * i + u] = g[meta[4, 4 * i + u]]
        return c

    lax.fori_loop(0, d.slots // 4, pick, 0)
    cp = remote(qs, qp, fw_send.at[0], fw_recv.at[0], partner)
    cp.start()
    for copy in kv_copies:
        copy.wait()
    cp.wait()

    head = lax.rem(iota((d.q, 128), 0) // d.group, d.kvl)
    head_masks = [(head == k).astype(F32).astype(BF16) for k in range(d.kvl)]
    lane128 = iota((d.q, 128), 1)
    lane_slot = iota((d.q, d.slot_len), 1)
    scale = 1.0 / math.sqrt(HD)

    unroll = 4

    def attend_many(it, carry):
        m_p, l_p, o_p, mc, lc = carry
        at = [it * unroll + u for u in range(unroll)]
        rows = [meta[0, i] for i in at]
        qs = [jnp.where(row >= 0, g[jnp.maximum(row, 0)], qp[i]) for row, i in zip(rows, at)]
        q2 = [jnp.concatenate([q * mask for mask in head_masks], axis=1) for q in qs]
        slots = [meta[1, i] for i in at]
        score = [
            lax.dot_general(q, kb[slot], (((1,), (1,)), ((), ())), preferred_element_type=F32)
            for q, slot in zip(q2, slots)
        ]
        score = [jnp.where(lane_slot < meta[2, i], x * scale, NEG) for x, i in zip(score, at)]
        tops = [jnp.max(x, axis=1, keepdims=True) for x in score]
        ps = [jnp.exp(x - m) for x, m in zip(score, tops)]
        sums = [jnp.dot(p.astype(BF16), vb[slot], preferred_element_type=F32) for p, slot in zip(ps, slots)]
        totals = [jnp.sum(p, axis=1, keepdims=True) for p in ps]
        accs = []
        for u, i in enumerate(at):
            o_s = sums[u][:, :HD]
            for k in range(1, d.kvl):
                o_s = jnp.where(head == k, sums[u][:, k * HD : (k + 1) * HD], o_s)
            m_q = jnp.where(meta[3, i] > 0, m_p, NEG)
            m = jnp.maximum(m_q, tops[u])
            a, b = jnp.exp(m_q - m), jnp.exp(tops[u] - m)
            l_p = l_p * a + totals[u] * b
            o_p = o_p * a + o_s * b
            m_p = m
            accs.append(o_p.astype(BF16))
            mc = jnp.where(lane128 == i, m_p, mc)
            lc = jnp.where(lane128 == i, l_p, lc)
        for u, i in enumerate(at):
            o[0, i] = accs[u]
        return m_p, l_p, o_p, mc, lc

    zero_col = jnp.zeros((d.q, 1), F32)
    zero = jnp.zeros((d.q, 128), F32)
    _, _, _, mc, lc = lax.fori_loop(
        0, d.slots // unroll, attend_many, (zero_col, zero_col, zero, jnp.full((d.q, 128), NEG, F32), zero)
    )
    pad = jnp.zeros((128 - d.q, 128), F32)
    mt = jnp.transpose(jnp.concatenate([mc, pad], axis=0))
    lt = jnp.transpose(jnp.concatenate([lc, pad], axis=0))
    table = jnp.where(iota((128, 128), 1) < 64, mt, pltpu.roll(lt, 64, 1))
    spare = t.shape[1] - d.slots
    t[0] = table[: t.shape[1]]
    nobody = jnp.where(iota((spare, 128), 1) < 64, NEG, 0.0)
    for side in (0, 1):
        t[side, pl.ds(d.slots, spare)] = nobody
        o[side, d.slots] = jnp.zeros((d.q, 128), BF16)

    for n, ref in enumerate((o, t)):
        cp = remote(
            ref.at[0, pl.ds(0, d.slots)], ref.at[1, pl.ds(0, d.slots)], ex_send.at[n], ex_recv.at[n], partner
        )
        cp.start()
        waits.append(cp)
    for n, ref in enumerate((o, t)):
        remote(
            ref.at[0, pl.ds(0, d.slots)], ref.at[1, pl.ds(0, d.slots)], ex_send.at[n], ex_recv.at[n], partner
        ).wait_recv()

    lane8 = iota((8, 128), 1)

    def pad8(x):
        if x.shape[0] == 8:
            return x
        return jnp.concatenate([x, jnp.zeros((8 - x.shape[0], 128), F32)], axis=0)

    def prepare(stats, count):
        top = functools.reduce(jnp.maximum, stats)
        es = [jnp.exp(st - top) for st in stats]
        total = sum(e * pltpu.roll(st, 64, 1) for e, st in zip(es, stats))
        tile = jnp.where(lane8 < 64, top, pltpu.roll(total, 64, 1))[:count]
        return tile, jnp.transpose(jnp.concatenate(es, axis=0))

    def apply(tile, cols, rows, many, count, out_d, out_s):
        out_s[...] = tile
        for r in range(count):
            acc = None
            for k in range(many):
                term = rows(k, r).astype(F32) * cols[: d.q, k * 8 + r : k * 8 + r + 1]
                acc = term if acc is None else acc + term
            out_d[r] = acc.astype(BF16)

    def merge(jobs, count):
        tiles = [[pad8(x[1][...]) for x in ins] for ins, _ in jobs]
        ready = [prepare(stats, count) for stats in tiles]
        for (ins, dst), (tile, cols) in zip(jobs, ready):
            apply(tile, cols, lambda k, r: ins[k][0][r], len(ins), count, *dst)

    per_row = 128 // d.rg

    class Part:
        def __init__(self, first, second, rows, recv, recv_s, mine, mine_s, send_sem, recv_sem):
            self.first, self.second = first, second
            self.start, self.count = rows
            self.recv, self.recv_s, self.mine, self.mine_s = recv, recv_s, mine, mine_s
            self.send_sem, self.recv_sem = send_sem, recv_sem
            self.n1, self.lanes = d.size[first], d.size[second]
            self.h1, self.h2 = d.hops[first], d.hops[second]
            self.phase2 = sum(self.h1) * self.lanes
            self.to = {
                (axis, way): neighbour(axis, 1 - 2 * way) for axis in (first, second) for way in (0, 1)
            }

        def id1(self, way, j, lane):
            return (way * self.h1[0] + j - 1) * self.lanes + lane

        def id2(self, way, j):
            return self.phase2 + way * self.h2[0] + j - 1

        def bufs(self, n):
            return self.recv.at[n], self.recv_s.at[n]

        def chip_sum(self, o1, lane):
            n = (o1 % self.n1) * self.lanes + lane
            return self.mine.at[n], self.mine_s.at[n]

        def copies(self, src, n, axis, way):
            return [
                remote(a, b, self.send_sem.at[k, n], self.recv_sem.at[k, n], self.to[axis, way])
                for k, (a, b) in enumerate(zip(src, self.bufs(n)))
            ]

        def send(self, src, n, axis, way):
            for cp in self.copies(src, n, axis, way):
                cp.start()

        def wait(self, n):
            for cp in self.copies(self.bufs(n), n, self.first, 0):
                cp.wait_recv()

        def wait_sent(self, n):
            for cp in self.copies(self.bufs(n), n, self.first, 0):
                cp.wait_send()

        def lane(self, k):
            return (self.h2[0] + ((k + 1) // 2) * (1 if k % 2 else -1)) % self.lanes

        def build(self, offsets, k):
            lane = self.lane(k)
            jobs = []
            for o1 in offsets:
                oy, oz = (o1, lane) if self.first == "y" else (lane, o1)
                kv_to = kv_at(oy, oz)
                line, col = lax.div(kv_to, per_row), lax.rem(kv_to, per_row) * d.rg + self.start
                ids, stats = [], []
                for side in (0, 1):
                    ids.append([meta[5 + side * chunks + line, col + r] for r in range(self.count)])
                    stats.append(
                        pad8(jnp.concatenate([t[side, pl.ds(i, 1), :] for i in ids[side]], axis=0))
                    )
                jobs.append((ids, stats, self.chip_sum(o1, lane)))
            ready = [prepare(stats, self.count) for _, stats, _ in jobs]
            for (ids, _, dst), (tile, cols) in zip(jobs, ready):
                apply(tile, cols, lambda k, r: o[k, ids[k][r]], 2, self.count, *dst)

        def launch(self, k):
            ways = [way for way in (0, 1) if self.h1[way]]
            far = [(1 - 2 * way) * self.h1[way] for way in ways]
            self.build(far, k)
            lane = self.lane(k)
            for way, o1 in zip(ways, far):
                self.send(self.chip_sum(o1, lane), self.id1(way, 1, lane), self.first, way)

        def rest(self, k):
            for j in range(1, self.h1[0]):
                ways = [way for way in (0, 1) if j < self.h1[way]]
                self.build([(1 - 2 * way) * (self.h1[way] - j) for way in ways], k)
            self.build([0], k)

        def relay(self, j, k):
            lane = self.lane(k)
            ways = [way for way in (0, 1) if j < self.h1[way]]
            jobs = []
            for way in ways:
                n = self.id1(way, j, lane)
                self.wait(n)
                left = (1 - 2 * way) * (self.h1[way] - j)
                jobs.append(([self.bufs(n), self.chip_sum(left, lane)], self.bufs(n)))
            merge(jobs, self.count)
            for way, (_, src) in zip(ways, jobs):
                self.send(src, self.id1(way, j + 1, lane), self.first, way)

        def second_step(self, k, result):
            lane = self.lane(k)
            ids = [self.id1(way, self.h1[way], lane) for way in (0, 1) if self.h1[way]]
            last = k == self.lanes - 1
            if last:
                ids += [self.id2(way, self.h2[way]) for way in (0, 1) if self.h2[way]]
            elif k >= 2:
                ids.append(self.id2(k % 2, k // 2))
            for n in ids:
                self.wait(n)
            ins = [self.bufs(n) for n in ids] + [self.chip_sum(0, lane)]
            dst = result if last else ins[0]
            merge([(ins, dst)], self.count)
            if not last:
                self.send(dst, self.id2(k % 2, k // 2 + 1), self.second, k % 2)

        def drain(self):
            def body(n, c):
                self.wait_sent(n)
                return c

            lax.fori_loop(0, self.phase2 + sum(self.h2), body, 0)

    p0 = Part("y", "z", d.rows_of[0], r0, r0s, d0, d0s, s0_send, s0_recv)
    p1 = Part("z", "y", d.rows_of[1], r1, r1s, d1, d1s, s1_send, s1_recv)
    fin0 = (f.at[pl.ds(p0.start, p0.count)], fs.at[pl.ds(p0.start, p0.count)])
    fin1 = (f.at[pl.ds(p1.start, p1.count)], fs.at[pl.ds(p1.start, p1.count)])

    lag = 2
    steps = []
    for n, (p, fin) in enumerate(((p1, fin1), (p0, fin0))):
        last = p.lanes - 1
        for k in range(p.lanes):
            steps.append((k, 4, n, functools.partial(p.launch, k)))
            steps.append((k, 5, n, functools.partial(p.rest, k)))
            for j in range(1, p.h1[0]):
                steps.append((k + lag * j, 1, n, functools.partial(p.relay, j, k)))
            late = lag * p.h1[0] + k + (lag - 1 if k == last else 0)
            steps.append((late, 3, n, functools.partial(p.second_step, k, fin)))
    steps.sort(key=lambda x: x[:3])
    for _, _, _, run in steps:
        run()

    for n in range(d.ntp):
        for i in range(d.rd):
            rfs_row = fs[n * d.rd + i : n * d.rd + i + 1, :]
            b1s_tmp = rfs_row
            rfs.at[d.ntp + n][i : i + 1, :] = b1s_tmp

    def final(k, dst_t, src_t, dev_t):
        return [
            remote(f.at[pl.ds(src_t * d.rd, d.rd)], rf.at[dst_t], fin_send.at[0, k], fin_recv.at[0, k], (kv, dev_t)),
            remote(rfs.at[d.ntp + src_t], rfs.at[dst_t], fin_send.at[1, k], fin_recv.at[1, k], (kv, dev_t)),
        ]

    for k in range(1, d.ntp):
        other = lax.rem(tp + k, d.ntp)
        for cp in final(k - 1, tp, other, other):
            cp.start()
            waits.append(cp)
    rf[tp] = f[pl.ds(tp * d.rd, d.rd)]
    rfs[tp] = rfs[d.ntp + tp]

    for cp in new_copies:
        cp.wait()
    nkf = [nk[u].astype(F32) for u in range(d.steps)]
    nvf = [nv[u].astype(F32) for u in range(d.steps)]
    fresh = []
    for h in range(d.ntp):
        for i in range(d.rd):
            tops, totals, outs = [], [], []
            qf = qx[h, i].astype(F32)
            for step in range(d.steps):
                for k in range(d.kvl):
                    at = (step * d.kvl + k) * d.group
                    kk = h * d.kvl + k
                    qs = qf[at : at + d.group]
                    scores = [
                        jnp.sum(qs * nkf[u][i : i + 1, kk * HD : (kk + 1) * HD], axis=1, keepdims=True) * scale
                        for u in range(step + 1)
                    ]
                    top = functools.reduce(jnp.maximum, scores)
                    ws = [jnp.exp(x - top) for x in scores]
                    tops.append(top)
                    totals.append(sum(ws))
                    outs.append(sum(w * nvf[u][i : i + 1, kk * HD : (kk + 1) * HD] for u, w in enumerate(ws)))
            fresh.append([jnp.concatenate(x, axis=0) for x in (tops, totals, outs)])

    for k in range(1, d.ntp):
        source = lax.rem(tp - k + d.ntp, d.ntp)
        for cp in final(k - 1, source, tp, source):
            cp.wait_recv()
    for h in range(d.ntp):
        cols = jnp.transpose(pad8(rfs[h]))
        for i in range(d.rd):
            top_n, total_n, out_n = fresh[h * d.rd + i]
            top_c, total_c = cols[: d.q, i : i + 1], cols[64 : 64 + d.q, i : i + 1]
            top = jnp.maximum(top_n, top_c)
            a, b = jnp.exp(top_n - top), jnp.exp(top_c - top)
            numer = out_n * a + rf[h, i].astype(F32) * b
            stage[h, i] = numer / (total_n * a + total_c * b)
    for step in range(d.steps):
        for h in range(d.ntp):
            for i in range(d.rd):
                for j in range(heads):
                    at = (h * heads + j) * HD
                    wide[i : i + 1, at : at + HD] = stage[h, i, pl.ds(step * heads + j, 1), :]
        out[step] = wide[...].astype(BF16)

    for cp in waits:
        cp.wait_send()
    p0.drain()
    p1.drain()


def make_shards(d):
    order = gather_order(d)

    def shards(queries, new_keys, new_values, key_cache, value_cache, context_lengths, piece_slots):
        steps, rd, width = queries.shape
        chunks = d.rows // 128
        vmem = pl.BlockSpec(memory_space=pltpu.VMEM)
        hbm = pl.BlockSpec(memory_space=pl.ANY)
        c0, c1 = d.rows_of[0][1], d.rows_of[1][1]
        n0 = sum(d.hops["y"]) * d.nz + sum(d.hops["z"])
        n1 = sum(d.hops["z"]) * d.ny + sum(d.hops["y"])
        pad = d.slots + 8
        dma = pltpu.SemaphoreType.DMA
        sem = lambda *shape: dma(shape)
        nt = max(d.ntp - 1, 1)
        plan_rows = -(-(5 + 2 * chunks) // 8) * 8
        scratch = [
            pltpu.VMEM(queries.shape, BF16),
            pltpu.VMEM(new_keys.shape, BF16),
            pltpu.VMEM(new_values.shape, BF16),
            pltpu.VMEM((d.ntp, rd, d.q, HD), F32),
            pltpu.VMEM((rd, width), F32),
            pltpu.VMEM((d.ntp, rd, d.q, HD), BF16),
            pltpu.VMEM(piece_slots.shape, jnp.int32),
            pltpu.VMEM((plan_rows, 128), jnp.int32),
            pltpu.SMEM((plan_rows, 128), jnp.int32),
            pltpu.VMEM((d.rows // 2, d.q, HD), BF16),
            pltpu.VMEM((d.slots, d.q, HD), BF16),
            pltpu.VMEM((d.slots, d.q, HD), BF16),
            pltpu.VMEM(key_cache.shape, BF16),
            pltpu.VMEM(value_cache.shape, BF16),
            pltpu.VMEM((2, pad, d.q, HD), BF16),
            pltpu.VMEM((2, pad, 128), F32),
            pltpu.VMEM((n0, c0, d.q, HD), BF16),
            pltpu.VMEM((n0, c0, 128), F32),
            pltpu.VMEM((n1, c1, d.q, HD), BF16),
            pltpu.VMEM((n1, c1, 128), F32),
            pltpu.VMEM((d.ny * d.nz, c0, d.q, HD), BF16),
            pltpu.VMEM((d.ny * d.nz, c0, 128), F32),
            pltpu.VMEM((d.ny * d.nz, c1, d.q, HD), BF16),
            pltpu.VMEM((d.ny * d.nz, c1, 128), F32),
            pltpu.VMEM((d.rg, d.q, HD), BF16),
            pltpu.VMEM((d.rg, 128), F32),
            pltpu.VMEM((d.ntp, rd, d.q, HD), BF16),
            pltpu.VMEM((2 * d.ntp, rd, 128), F32),
            sem(5), sem(2, 4), sem(nt), sem(nt), sem(len(order) // 2), sem(len(order) // 2), sem(1), sem(1),
            sem(2), sem(2), sem(2, n0), sem(2, n0), sem(2, n1), sem(2, n1), sem(2, nt), sem(2, nt),
        ]
        result = pl.pallas_call(
            functools.partial(main_kernel, d, order),
            out_shape=jax.ShapeDtypeStruct(queries.shape, BF16),
            in_specs=[hbm, vmem, hbm, hbm, hbm, hbm, hbm],
            out_specs=vmem,
            scratch_shapes=scratch,
            compiler_params=pltpu.CompilerParams(
                collective_id=0, has_side_effects=True, vmem_limit_bytes=60 * 1024 * 1024
            ),
        )(piece_slots, context_lengths.reshape(chunks, 128), queries, new_keys, new_values, key_cache, value_cache)
        return result

    return shards


def solution(mesh):
    d = Dims(4, 8, 4, 2, 40, 256, 3, 2, 8)
    return build(mesh, d)


def build(mesh, d):
    placed = (
        P(None, ("kv", "tp"), None),
        P(None, ("kv", "tp"), None),
        P(None, ("kv", "tp"), None),
        P("kv", None, "tp"),
        P("kv", None, "tp"),
        P(),
        P(),
    )
    return jax.shard_map(
        make_shards(d),
        mesh=mesh,
        in_specs=placed,
        out_specs=P(None, ("kv", "tp"), None),
        check_vma=False,
    )
```

```python
import functools
import math

import jax
import jax.numpy as jnp
from jax import lax
from jax.experimental import pallas as pl
from jax.experimental.pallas import tpu as pltpu
from jax.sharding import PartitionSpec as P

HD = 128
NEG = -1e30
MESH = pl.DeviceIdType.MESH
F32 = jnp.float32
BF16 = jnp.bfloat16


class Dims:
    def __init__(self, ny, nz, ntp, rows_dev, slots, slot_len, steps, kv_local, group):
        self.ny, self.nz, self.ntp, self.rd = ny, nz, ntp, rows_dev
        self.slots, self.slot_len = slots, slot_len
        self.steps, self.kvl, self.group = steps, kv_local, group
        self.rg = rows_dev * ntp
        self.kv = ny * nz * 2
        self.rows = self.kv * self.rg
        self.q = steps * kv_local * group
        self.split = (5 * self.rg) // 8
        self.size = {"y": ny, "z": nz}
        self.hops = {a: (n // 2, n - 1 - n // 2) for a, n in self.size.items()}
        self.rows_of = ((0, self.split), (self.split, self.rg - self.split))


def list_order(tasks, limit, latency=1.75, rate=95e3, tick=0.02):
    left = {t[0]: t for t in tasks}
    flying = {"y": [], "z": []}
    arrived, order = {}, []
    now, busy, running = 0.0, 0.0, None
    while left or running:
        if now >= busy - 1e-9:
            if running:
                for msg, axis, size in running[4]:
                    flying[axis].append([msg, size])
                running = None
            ready, urgent = [], set()
            for name, _, waits, before, _, paced, rank in left.values():
                if any(arrived.get(w, 1e9) > now for w in waits):
                    continue
                if any(x in left for x in before):
                    urgent.update(before)
                elif not paced or len(flying[paced]) < limit:
                    ready.append((rank, name))
            ready = [((0.5,) + r[1:] if n in urgent and r[0] > 0.5 else r, n) for r, n in ready]
            if ready:
                name = min(ready)[1]
                running = left.pop(name)
                order.append(name)
                busy = now + running[1]
        for axis, copies in flying.items():
            for c in copies:
                c[1] -= rate * tick / len(copies)
                if c[1] <= 0:
                    arrived[c[0]] = now + tick + latency
            flying[axis] = [c for c in copies if c[1] > 0]
        now += tick
    return order


def gather_order(d, limit=2):
    tasks, depth = [], {}

    def hops(msg):
        return max([1 + hops(c) for c in gather_children(d, msg)], default=0)

    def add(msg):
        for child in gather_children(d, msg):
            part, phase = child[0], child[1]
            axis = "zy"[part] if phase == 1 else "yz"[part]
            size = d.rows_of[part][1] * d.q * HD * 2
            before = [("wait", msg)] if msg else []
            rank = (0, -hops(child), len(tasks))
            tasks.append((("send", child), 0.06, [], before, [(child, axis, size)], axis, rank))
            tasks.append((("wait", child), 0.12, [child], [], [], None, (1, 0, len(tasks))))
            add(child)

    add(None)
    return list_order(tasks, limit)


def gather_children(d, msg):
    out = []
    if msg is None:
        for phase in (1, 2):
            for part in (0, 1):
                axis = "zy"[part] if phase == 1 else "yz"[part]
                for way in (0, 1):
                    if d.hops[axis][way] >= 1:
                        out.append((part, phase, way, 1, 0))
        return out
    part, phase, way, j, oa = msg
    first, second = ("z", "y") if part == 0 else ("y", "z")
    axis = first if phase == 1 else second
    if j < d.hops[axis][way]:
        out.append((part, phase, way, j + 1, oa))
    if phase == 1:
        here = -j if way == 0 else j
        for w2 in (0, 1):
            if d.hops[second][w2] >= 1:
                out.append((part, 2, w2, 1, here))
    return out


def iota(shape, dim):
    return lax.broadcasted_iota(jnp.int32, shape, dim)


def slot_plan(d, kv, ps, ctx, out, pieces):
    partner = kv + 1 - 2 * lax.rem(kv, 2)
    core = lax.rem(kv, 2)
    chunks = d.rows // 128
    eye = iota((128, 128), 0) == iota((128, 128), 1)
    lane = iota((128, 128), 1)
    row_in = iota((128, 128), 0)

    def to_col(row):
        return jnp.sum(jnp.where(eye, jnp.broadcast_to(row, (128, 128)), 0), axis=1, keepdims=True)

    def to_row(col):
        return jnp.sum(jnp.where(eye, jnp.broadcast_to(col, (128, 128)), 0), axis=0, keepdims=True)

    zero = jnp.zeros((1, 128), jnp.int32)
    state = [[jnp.zeros((1, 1), jnp.int32), zero, zero] for _ in (0, 1)]

    def piece(side, c):
        base, acc_val, acc_row = state[side]
        owner = kv if side == 0 else partner
        local = ps[c * 128 : (c + 1) * 128, :] - owner * d.slots
        hit = (local >= 0) & (local < d.slots)
        many = jnp.sum(hit.astype(jnp.int32), axis=1, keepdims=True)
        many_row = to_row(many)
        before = jnp.sum(jnp.where(row_in < lane, many, 0), axis=0, keepdims=True)
        start_row = before + base
        last = jnp.where(many_row > 0, jnp.minimum(start_row + many_row - 1, d.slots), d.slots)
        out[5 + side * chunks + c : 6 + side * chunks + c, :] = last
        base = base + jnp.sum(many_row, axis=1, keepdims=True)
        start = to_col(start_row)
        if side == 0:
            length = to_col(ctx[c : c + 1, :])
            left = jnp.clip(length - lane * d.slot_len, 0, d.slot_len)
            far = 1 << 30
            code = jnp.where(hit, lane * 32768 + local * 512 + left, far)
        for k in range(3):
            at = (lane == start + k) & (many > k)
            acc_row += jnp.sum(jnp.where(at, row_in + c * 128, 0), axis=0, keepdims=True)
            if side == 0:
                first = jnp.min(code, axis=1, keepdims=True)
                code = jnp.where(code == first, far, code)
                acc_val += jnp.sum(jnp.where(at, lax.rem(first, 32768), 0), axis=0, keepdims=True)
        state[side] = [base, acc_val, acc_row]

    def finish():
        for side in (0, 1):
            _, acc_val, acc_row = state[side]
            mine = lax.rem(acc_row // d.rg, 2) == core
            place = (acc_row // (2 * d.rg)) * d.rg + lax.rem(acc_row, d.rg)
            place = jnp.clip(place, 0, d.rows // 2 - 1)
            if side == 0:
                same = (iota((1, 128), 1) > 0) & (pltpu.roll(acc_row, 1, 1) == acc_row)
                out[0:1, :] = jnp.where(mine, place, -1)
                out[1:2, :] = jnp.clip(acc_val // 512, 0, d.slots - 1)
                out[2:3, :] = lax.rem(acc_val, 512)
                out[3:4, :] = jnp.where(same, 1, 0)
            else:
                out[4:5, :] = jnp.where(mine, place, 0)

    for c in range(chunks):
        for side in (0, 1):
            pieces.append(functools.partial(piece, side, c))
    pieces.append(finish)


def main_kernel(
    d, order, ps, ctx, q_in, nk_in, nv_in, kc, vc, out,
    q_raw, nk, nv, stage, qx, psv, planv, meta, g, qp, qs, kb, vb, o, t, r0, r0s, r1, r1s, d0, d0s, d1, d1s, f, fs, rf, rfs,
    io_sem, kv_sem, tp_send, tp_recv, ag_send, ag_recv, fw_send, fw_recv, ex_send, ex_recv,
    s0_send, s0_recv, s1_send, s1_recv, fin_send, fin_recv,
):
    kv = lax.axis_index("kv")
    tp = lax.axis_index("tp")
    core = lax.rem(kv, 2)
    sgn = 1 - 2 * core
    chip = kv // 2
    pos = {"y": chip // d.nz, "z": lax.rem(chip, d.nz)}

    near = {}

    def coord(axis, k):
        n = d.size[axis]
        if (axis, k) not in near:
            near[axis, k] = lax.rem(pos[axis] + sgn * k + n, n)
        return near[axis, k]

    def chip_at(oy, oz):
        return coord("y", oy) * d.nz + coord("z", oz)

    def kv_at(oy, oz):
        return chip_at(oy, oz) * 2 + core

    def neighbour(axis, step):
        return (kv_at(step, 0) if axis == "y" else kv_at(0, step), tp)

    partner = (kv + sgn, tp)

    def remote(src, dst, ss, rs, dev):
        return pltpu.make_async_remote_copy(
            src_ref=src, dst_ref=dst, send_sem=ss, recv_sem=rs, device_id=dev, device_id_type=MESH
        )

    chunks = d.rows // 128

    q_copy = pltpu.make_async_copy(q_in, q_raw, io_sem.at[2])
    q_copy.start()
    new_copies = [
        pltpu.make_async_copy(src, dst, io_sem.at[n])
        for n, (src, dst) in enumerate(((nk_in, nk), (nv_in, nv)), 3)
    ]
    for cp in new_copies:
        cp.start()
    ps_copy = pltpu.make_async_copy(ps, psv, io_sem.at[0])
    ps_copy.start()
    parts_kv = kv_sem.shape[1]
    per = d.slots // parts_kv
    kv_copies = []
    for n in range(parts_kv):
        for which, (src, dst) in enumerate(((kc, kb), (vc, vb))):
            cp = pltpu.make_async_copy(
                src.at[pl.ds(n * per, per)], dst.at[pl.ds(n * per, per)], kv_sem.at[which, n]
            )
            cp.start()
            kv_copies.append(cp)

    friends = [partner]
    for axis in ("y", "z"):
        for way in (0, 1):
            if d.hops[axis][way]:
                friends.append(neighbour(axis, 1 - 2 * way))
    for k in range(1, d.ntp):
        friends.append((kv, lax.rem(tp + k, d.ntp)))
    barrier = pltpu.get_barrier_semaphore()
    for dev in friends:
        pl.semaphore_signal(barrier, inc=1, device_id=dev, device_id_type=MESH)

    q_copy.wait()
    heads = d.kvl * d.group
    for step in range(d.steps):
        q_step = q_raw[step].astype(F32)
        for h in range(d.ntp):
            for i in range(d.rd):
                for j in range(heads):
                    at = (h * heads + j) * HD
                    stage[h, i, pl.ds(step * heads + j, 1), :] = q_step[i : i + 1, at : at + HD]
    qx[...] = stage[...].astype(BF16)
    pl.semaphore_wait(barrier, len(friends))

    waits = []

    own = chip * d.rg
    tp_copies = []
    for k in range(1, d.ntp):
        other = lax.rem(tp + k, d.ntp)
        cp = remote(
            qx.at[other], g.at[pl.ds(own + tp * d.rd, d.rd)], tp_send.at[k - 1], tp_recv.at[k - 1], (kv, other)
        )
        cp.start()
        waits.append(cp)
    g[pl.ds(own + tp * d.rd, d.rd)] = qx[tp]
    for k in range(1, d.ntp):
        source = lax.rem(tp - k + d.ntp, d.ntp)
        remote(
            qx.at[tp], g.at[pl.ds(own + source * d.rd, d.rd)], tp_send.at[k - 1], tp_recv.at[k - 1], (kv, source)
        ).wait_recv()

    number = {msg: n for n, msg in enumerate(msg for what, msg in order if what == "send")}

    def place(msg, back):
        part, phase, way, j, oa = msg
        turn = 1 if way == 0 else -1
        steps = j - 1 if back else j
        o1 = -turn * steps if phase == 1 else oa
        o2 = 0 if phase == 1 else -turn * steps
        oz, oy = (o1, o2) if part == 0 else (o2, o1)
        start, count = d.rows_of[part]
        return g.at[pl.ds(chip_at(oy, oz) * d.rg + start, count)]

    def ship(msg):
        part, phase, way, j, oa = msg
        axis = "zy"[part] if phase == 1 else "yz"[part]
        n = number[msg]
        src = place(msg, True)
        cp = remote(src, src, ag_send.at[n], ag_recv.at[n], neighbour(axis, 1 - 2 * way))
        cp.start()
        waits.append(cp)

    ps_copy.wait()
    pieces = []
    slot_plan(d, kv, psv, ctx, planv, pieces)
    plan_copy = pltpu.make_async_copy(planv, meta, io_sem.at[1])
    for place_in, (what, msg) in enumerate(order):
        if what == "send":
            ship(msg)
            continue
        n = number[msg]
        landed = place(msg, False)
        remote(landed, landed, ag_send.at[n], ag_recv.at[n], partner).wait_recv()
        if place_in >= 16 and pieces:
            pieces.pop(0)()
            if not pieces:
                plan_copy.start()
    if pieces:
        while pieces:
            pieces.pop(0)()
        plan_copy.start()
    plan_copy.wait()

    def pick(i, c):
        for u in range(4):
            qs[4 * i + u] = g[meta[4, 4 * i + u]]
        return c

    lax.fori_loop(0, d.slots // 4, pick, 0)
    cp = remote(qs, qp, fw_send.at[0], fw_recv.at[0], partner)
    cp.start()
    for copy in kv_copies + new_copies:
        copy.wait()
    for other in waits:
        other.wait_send()
    waits.clear()
    cp.wait()

    head = lax.rem(iota((d.q, 128), 0) // d.group, d.kvl)
    head_masks = [(head == k).astype(F32).astype(BF16) for k in range(d.kvl)]
    lane128 = iota((d.q, 128), 1)
    lane_slot = iota((d.q, d.slot_len), 1)
    scale = 1.0 / math.sqrt(HD)

    unroll = 8

    def attend_many(it, carry):
        m_p, l_p, o_p, mc, lc = carry
        at = [it * unroll + u for u in range(unroll)]
        rows = [meta[0, i] for i in at]
        qs = [jnp.where(row >= 0, g[jnp.maximum(row, 0)], qp[i]) for row, i in zip(rows, at)]
        q2 = [jnp.concatenate([q * mask for mask in head_masks], axis=1) for q in qs]
        slots = [meta[1, i] for i in at]
        score = [
            lax.dot_general(q, kb[slot], (((1,), (1,)), ((), ())), preferred_element_type=F32)
            for q, slot in zip(q2, slots)
        ]
        score = [jnp.where(lane_slot < meta[2, i], x * scale, NEG) for x, i in zip(score, at)]
        tops = [jnp.max(x, axis=1, keepdims=True) for x in score]
        ps = [jnp.exp(x - m) for x, m in zip(score, tops)]
        sums = [jnp.dot(p.astype(BF16), vb[slot], preferred_element_type=F32) for p, slot in zip(ps, slots)]
        totals = [jnp.sum(p, axis=1, keepdims=True) for p in ps]
        accs = []
        for u, i in enumerate(at):
            o_s = sums[u][:, :HD]
            for k in range(1, d.kvl):
                o_s = jnp.where(head == k, sums[u][:, k * HD : (k + 1) * HD], o_s)
            m_q = jnp.where(meta[3, i] > 0, m_p, NEG)
            m = jnp.maximum(m_q, tops[u])
            a, b = jnp.exp(m_q - m), jnp.exp(tops[u] - m)
            l_p = l_p * a + totals[u] * b
            o_p = o_p * a + o_s * b
            m_p = m
            accs.append(o_p.astype(BF16))
            mc = jnp.where(lane128 == i, m_p, mc)
            lc = jnp.where(lane128 == i, l_p, lc)
        for u, i in enumerate(at):
            o[0, i] = accs[u]
        return m_p, l_p, o_p, mc, lc

    zero_col = jnp.zeros((d.q, 1), F32)
    zero = jnp.zeros((d.q, 128), F32)
    _, _, _, mc, lc = lax.fori_loop(
        0, d.slots // unroll, attend_many, (zero_col, zero_col, zero, jnp.full((d.q, 128), NEG, F32), zero)
    )
    pad = jnp.zeros((128 - d.q, 128), F32)
    mt = jnp.transpose(jnp.concatenate([mc, pad], axis=0))
    lt = jnp.transpose(jnp.concatenate([lc, pad], axis=0))
    table = jnp.where(iota((128, 128), 1) < 64, mt, pltpu.roll(lt, 64, 1))
    spare = t.shape[1] - d.slots
    t[0] = table[: t.shape[1]]
    nobody = jnp.where(iota((spare, 128), 1) < 64, NEG, 0.0)
    for side in (0, 1):
        t[side, pl.ds(d.slots, spare)] = nobody
        o[side, d.slots] = jnp.zeros((d.q, 128), BF16)

    for n, ref in enumerate((o, t)):
        cp = remote(
            ref.at[0, pl.ds(0, d.slots)], ref.at[1, pl.ds(0, d.slots)], ex_send.at[n], ex_recv.at[n], partner
        )
        cp.start()
        waits.append(cp)
    for n, ref in enumerate((o, t)):
        remote(
            ref.at[0, pl.ds(0, d.slots)], ref.at[1, pl.ds(0, d.slots)], ex_send.at[n], ex_recv.at[n], partner
        ).wait_recv()

    lane8 = iota((8, 128), 1)

    def pad8(x):
        if x.shape[0] == 8:
            return x
        return jnp.concatenate([x, jnp.zeros((8 - x.shape[0], 128), F32)], axis=0)

    def prepare(stats, count):
        top = functools.reduce(jnp.maximum, stats)
        es = [jnp.exp(st - top) for st in stats]
        total = sum(e * pltpu.roll(st, 64, 1) for e, st in zip(es, stats))
        tile = jnp.where(lane8 < 64, top, pltpu.roll(total, 64, 1))[:count]
        return tile, jnp.transpose(jnp.concatenate(es, axis=0))

    def apply(tile, cols, rows, many, count, out_d, out_s):
        out_s[...] = tile
        for r in range(count):
            acc = None
            for k in range(many):
                term = rows(k, r).astype(F32) * cols[: d.q, k * 8 + r : k * 8 + r + 1]
                acc = term if acc is None else acc + term
            out_d[r] = acc.astype(BF16)

    def merge(jobs, count):
        tiles = [[pad8(x[1][...]) for x in ins] for ins, _ in jobs]
        ready = [prepare(stats, count) for stats in tiles]
        for (ins, dst), (tile, cols) in zip(jobs, ready):
            apply(tile, cols, lambda k, r: ins[k][0][r], len(ins), count, *dst)

    per_row = 128 // d.rg

    class Part:
        def __init__(self, first, second, rows, recv, recv_s, mine, mine_s, send_sem, recv_sem):
            self.first, self.second = first, second
            self.start, self.count = rows
            self.recv, self.recv_s, self.mine, self.mine_s = recv, recv_s, mine, mine_s
            self.send_sem, self.recv_sem = send_sem, recv_sem
            self.n1, self.lanes = d.size[first], d.size[second]
            self.h1, self.h2 = d.hops[first], d.hops[second]
            self.phase2 = sum(self.h1) * self.lanes
            self.to = {
                (axis, way): neighbour(axis, 1 - 2 * way) for axis in (first, second) for way in (0, 1)
            }

        def id1(self, way, j, lane):
            return (way * self.h1[0] + j - 1) * self.lanes + lane

        def id2(self, way, j):
            return self.phase2 + way * self.h2[0] + j - 1

        def bufs(self, n):
            return self.recv.at[n], self.recv_s.at[n]

        def chip_sum(self, o1, lane):
            n = (o1 % self.n1) * self.lanes + lane
            return self.mine.at[n], self.mine_s.at[n]

        def copies(self, src, n, axis, way):
            return [
                remote(a, b, self.send_sem.at[k, n], self.recv_sem.at[k, n], self.to[axis, way])
                for k, (a, b) in enumerate(zip(src, self.bufs(n)))
            ]

        def send(self, src, n, axis, way):
            for cp in self.copies(src, n, axis, way):
                cp.start()

        def wait(self, n):
            for cp in self.copies(self.bufs(n), n, self.first, 0):
                cp.wait_recv()

        def wait_sent(self, n):
            for cp in self.copies(self.bufs(n), n, self.first, 0):
                cp.wait_send()

        def lane(self, k):
            return (self.h2[0] + ((k + 1) // 2) * (1 if k % 2 else -1)) % self.lanes

        def build(self, offsets, k):
            lane = self.lane(k)
            jobs = []
            for o1 in offsets:
                oy, oz = (o1, lane) if self.first == "y" else (lane, o1)
                kv_to = kv_at(oy, oz)
                line, col = lax.div(kv_to, per_row), lax.rem(kv_to, per_row) * d.rg + self.start
                ids, stats = [], []
                for side in (0, 1):
                    ids.append([meta[5 + side * chunks + line, col + r] for r in range(self.count)])
                    stats.append(
                        pad8(jnp.concatenate([t[side, pl.ds(i, 1), :] for i in ids[side]], axis=0))
                    )
                jobs.append((ids, stats, self.chip_sum(o1, lane)))
            ready = [prepare(stats, self.count) for _, stats, _ in jobs]
            for (ids, _, dst), (tile, cols) in zip(jobs, ready):
                apply(tile, cols, lambda k, r: o[k, ids[k][r]], 2, self.count, *dst)

        def launch(self, k):
            ways = [way for way in (0, 1) if self.h1[way]]
            far = [(1 - 2 * way) * self.h1[way] for way in ways]
            self.build(far, k)
            lane = self.lane(k)
            for way, o1 in zip(ways, far):
                self.send(self.chip_sum(o1, lane), self.id1(way, 1, lane), self.first, way)

        def rest(self, k):
            for j in range(1, self.h1[0]):
                ways = [way for way in (0, 1) if j < self.h1[way]]
                self.build([(1 - 2 * way) * (self.h1[way] - j) for way in ways], k)
            self.build([0], k)

        def relay(self, j, k):
            lane = self.lane(k)
            ways = [way for way in (0, 1) if j < self.h1[way]]
            jobs = []
            for way in ways:
                n = self.id1(way, j, lane)
                self.wait(n)
                left = (1 - 2 * way) * (self.h1[way] - j)
                jobs.append(([self.bufs(n), self.chip_sum(left, lane)], self.bufs(n)))
            merge(jobs, self.count)
            for way, (_, src) in zip(ways, jobs):
                self.send(src, self.id1(way, j + 1, lane), self.first, way)

        def second_step(self, k, result):
            lane = self.lane(k)
            ids = [self.id1(way, self.h1[way], lane) for way in (0, 1) if self.h1[way]]
            last = k == self.lanes - 1
            if last:
                ids += [self.id2(way, self.h2[way]) for way in (0, 1) if self.h2[way]]
            elif k >= 2:
                ids.append(self.id2(k % 2, k // 2))
            for n in ids:
                self.wait(n)
            ins = [self.bufs(n) for n in ids] + [self.chip_sum(0, lane)]
            dst = result if last else ins[0]
            merge([(ins, dst)], self.count)
            if not last:
                self.send(dst, self.id2(k % 2, k // 2 + 1), self.second, k % 2)

        def drain(self):
            def body(n, c):
                self.wait_sent(n)
                return c

            lax.fori_loop(0, self.phase2 + sum(self.h2), body, 0)

    p0 = Part("y", "z", d.rows_of[0], r0, r0s, d0, d0s, s0_send, s0_recv)
    p1 = Part("z", "y", d.rows_of[1], r1, r1s, d1, d1s, s1_send, s1_recv)
    fin0 = (f.at[pl.ds(p0.start, p0.count)], fs.at[pl.ds(p0.start, p0.count)])
    fin1 = (f.at[pl.ds(p1.start, p1.count)], fs.at[pl.ds(p1.start, p1.count)])

    lag = 2
    steps = []
    for n, (p, fin) in enumerate(((p1, fin1), (p0, fin0))):
        last = p.lanes - 1
        for k in range(p.lanes):
            steps.append((k, 4, n, functools.partial(p.launch, k)))
            steps.append((k, 5, n, functools.partial(p.rest, k)))
            for j in range(1, p.h1[0]):
                steps.append((k + lag * j, 1, n, functools.partial(p.relay, j, k)))
            late = lag * p.h1[0] + k + (lag - 1 if k == last else 0)
            steps.append((late, 3, n, functools.partial(p.second_step, k, fin)))
    steps.sort(key=lambda x: x[:3])
    for _, _, _, run in steps:
        run()

    for n in range(d.ntp):
        for i in range(d.rd):
            rfs_row = fs[n * d.rd + i : n * d.rd + i + 1, :]
            b1s_tmp = rfs_row
            rfs.at[d.ntp + n][i : i + 1, :] = b1s_tmp

    def final(k, dst_t, src_t, dev_t):
        return [
            remote(f.at[pl.ds(src_t * d.rd, d.rd)], rf.at[dst_t], fin_send.at[0, k], fin_recv.at[0, k], (kv, dev_t)),
            remote(rfs.at[d.ntp + src_t], rfs.at[dst_t], fin_send.at[1, k], fin_recv.at[1, k], (kv, dev_t)),
        ]

    for k in range(1, d.ntp):
        other = lax.rem(tp + k, d.ntp)
        for cp in final(k - 1, tp, other, other):
            cp.start()
            waits.append(cp)
    rf[tp] = f[pl.ds(tp * d.rd, d.rd)]
    rfs[tp] = rfs[d.ntp + tp]

    nkf = [nk[u].astype(F32) for u in range(d.steps)]
    nvf = [nv[u].astype(F32) for u in range(d.steps)]
    fresh = []
    for h in range(d.ntp):
        for i in range(d.rd):
            tops, totals, outs = [], [], []
            qf = qx[h, i].astype(F32)
            for step in range(d.steps):
                for k in range(d.kvl):
                    at = (step * d.kvl + k) * d.group
                    kk = h * d.kvl + k
                    qs = qf[at : at + d.group]
                    scores = [
                        jnp.sum(qs * nkf[u][i : i + 1, kk * HD : (kk + 1) * HD], axis=1, keepdims=True) * scale
                        for u in range(step + 1)
                    ]
                    top = functools.reduce(jnp.maximum, scores)
                    ws = [jnp.exp(x - top) for x in scores]
                    tops.append(top)
                    totals.append(sum(ws))
                    outs.append(sum(w * nvf[u][i : i + 1, kk * HD : (kk + 1) * HD] for u, w in enumerate(ws)))
            fresh.append([jnp.concatenate(x, axis=0) for x in (tops, totals, outs)])

    p0.drain()
    p1.drain()
    for k in range(1, d.ntp):
        source = lax.rem(tp - k + d.ntp, d.ntp)
        for cp in final(k - 1, source, tp, source):
            cp.wait_recv()
    for h in range(d.ntp):
        cols = jnp.transpose(pad8(rfs[h]))
        for i in range(d.rd):
            top_n, total_n, out_n = fresh[h * d.rd + i]
            top_c, total_c = cols[: d.q, i : i + 1], cols[64 : 64 + d.q, i : i + 1]
            top = jnp.maximum(top_n, top_c)
            a, b = jnp.exp(top_n - top), jnp.exp(top_c - top)
            numer = out_n * a + rf[h, i].astype(F32) * b
            result = (numer / (total_n * a + total_c * b)).astype(BF16)
            for step in range(d.steps):
                out[step, i, pl.ds(h * heads, heads)] = result[step * heads : (step + 1) * heads]

    for cp in waits:
        cp.wait_send()


def make_shards(d):
    order = gather_order(d)

    def shards(queries, new_keys, new_values, key_cache, value_cache, context_lengths, piece_slots):
        steps, rd, width = queries.shape
        chunks = d.rows // 128
        vmem = pl.BlockSpec(memory_space=pltpu.VMEM)
        hbm = pl.BlockSpec(memory_space=pl.ANY)
        c0, c1 = d.rows_of[0][1], d.rows_of[1][1]
        n0 = sum(d.hops["y"]) * d.nz + sum(d.hops["z"])
        n1 = sum(d.hops["z"]) * d.ny + sum(d.hops["y"])
        pad = d.slots + 8
        dma = pltpu.SemaphoreType.DMA
        sem = lambda *shape: dma(shape)
        nt = max(d.ntp - 1, 1)
        plan_rows = -(-(5 + 2 * chunks) // 8) * 8
        scratch = [
            pltpu.VMEM(queries.shape, BF16),
            pltpu.VMEM(new_keys.shape, BF16),
            pltpu.VMEM(new_values.shape, BF16),
            pltpu.VMEM((d.ntp, rd, d.q, HD), F32),
            pltpu.VMEM((d.ntp, rd, d.q, HD), BF16),
            pltpu.VMEM(piece_slots.shape, jnp.int32),
            pltpu.VMEM((plan_rows, 128), jnp.int32),
            pltpu.SMEM((plan_rows, 128), jnp.int32),
            pltpu.VMEM((d.rows // 2, d.q, HD), BF16),
            pltpu.VMEM((d.slots, d.q, HD), BF16),
            pltpu.VMEM((d.slots, d.q, HD), BF16),
            pltpu.VMEM(key_cache.shape, BF16),
            pltpu.VMEM(value_cache.shape, BF16),
            pltpu.VMEM((2, pad, d.q, HD), BF16),
            pltpu.VMEM((2, pad, 128), F32),
            pltpu.VMEM((n0, c0, d.q, HD), BF16),
            pltpu.VMEM((n0, c0, 128), F32),
            pltpu.VMEM((n1, c1, d.q, HD), BF16),
            pltpu.VMEM((n1, c1, 128), F32),
            pltpu.VMEM((d.ny * d.nz, c0, d.q, HD), BF16),
            pltpu.VMEM((d.ny * d.nz, c0, 128), F32),
            pltpu.VMEM((d.ny * d.nz, c1, d.q, HD), BF16),
            pltpu.VMEM((d.ny * d.nz, c1, 128), F32),
            pltpu.VMEM((d.rg, d.q, HD), BF16),
            pltpu.VMEM((d.rg, 128), F32),
            pltpu.VMEM((d.ntp, rd, d.q, HD), BF16),
            pltpu.VMEM((2 * d.ntp, rd, 128), F32),
            sem(5), sem(2, 4), sem(nt), sem(nt), sem(len(order) // 2), sem(len(order) // 2), sem(1), sem(1),
            sem(2), sem(2), sem(2, n0), sem(2, n0), sem(2, n1), sem(2, n1), sem(2, nt), sem(2, nt),
        ]
        result = pl.pallas_call(
            functools.partial(main_kernel, d, order),
            out_shape=jax.ShapeDtypeStruct((steps, rd, width // HD, HD), BF16),
            in_specs=[hbm, vmem, hbm, hbm, hbm, hbm, hbm],
            out_specs=vmem,
            scratch_shapes=scratch,
            compiler_params=pltpu.CompilerParams(
                collective_id=0, has_side_effects=True, vmem_limit_bytes=60 * 1024 * 1024
            ),
        )(piece_slots, context_lengths.reshape(chunks, 128), queries, new_keys, new_values, key_cache, value_cache)
        return result.reshape(steps, rd, width)

    return shards


def solution(mesh):
    d = Dims(4, 8, 4, 2, 40, 256, 3, 2, 8)
    return build(mesh, d)


def build(mesh, d):
    placed = (
        P(None, ("kv", "tp"), None),
        P(None, ("kv", "tp"), None),
        P(None, ("kv", "tp"), None),
        P("kv", None, "tp"),
        P("kv", None, "tp"),
        P(),
        P(),
    )
    return jax.shard_map(
        make_shards(d),
        mesh=mesh,
        in_specs=placed,
        out_specs=P(None, ("kv", "tp"), None),
        check_vma=False,
    )
```

```python
import functools
import math

import jax
import jax.numpy as jnp
from jax import lax
from jax.experimental import pallas as pl
from jax.experimental.pallas import tpu as pltpu
from jax.sharding import PartitionSpec as P

HD = 128
NEG = -1e30
MESH = pl.DeviceIdType.MESH
F32 = jnp.float32
BF16 = jnp.bfloat16


class Dims:
    def __init__(self, ny, nz, ntp, rows_dev, slots, slot_len, steps, kv_local, group):
        self.ny, self.nz, self.ntp, self.rd = ny, nz, ntp, rows_dev
        self.slots, self.slot_len = slots, slot_len
        self.steps, self.kvl, self.group = steps, kv_local, group
        self.rg = rows_dev * ntp
        self.kv = ny * nz * 2
        self.rows = self.kv * self.rg
        self.q = steps * kv_local * group
        self.split = (5 * self.rg) // 8
        self.size = {"y": ny, "z": nz}
        self.hops = {a: (n // 2, n - 1 - n // 2) for a, n in self.size.items()}
        self.rows_of = ((0, self.split), (self.split, self.rg - self.split))


def list_order(tasks, limit, latency, rate=95e3, tick=0.02):
    left = {t[0]: t for t in tasks}
    flying = {"y": [], "z": []}
    arrived, order = {}, []
    now, busy, running = 0.0, 0.0, None
    while left or running:
        if now >= busy - 1e-9:
            if running:
                for msg, axis, size in running[4]:
                    flying[axis].append([msg, size])
                running = None
            ready, urgent = [], set()
            for name, _, waits, before, _, paced, rank in left.values():
                if any(arrived.get(w, 1e9) > now for w in waits):
                    continue
                if any(x in left for x in before):
                    urgent.update(before)
                elif not paced or len(flying[paced]) < limit:
                    ready.append((rank, name))
            ready = [((0.5,) + r[1:] if n in urgent and r[0] > 0.5 else r, n) for r, n in ready]
            if ready:
                name = min(ready)[1]
                running = left.pop(name)
                order.append(name)
                busy = now + running[1]
        for axis, copies in flying.items():
            room = rate * tick
            for c in copies:
                part = min(room, c[1])
                c[1] -= part
                room -= part
                if c[1] <= 1e-9:
                    arrived[c[0]] = now + tick + latency
            flying[axis] = [c for c in copies if c[1] > 1e-9]
        now += tick
    return order


def gather_order(d, limit=2, latency=2.0):
    tasks, depth = [], {}

    def hops(msg):
        return max([1 + hops(c) for c in gather_children(d, msg)], default=0)

    def add(msg):
        for child in gather_children(d, msg):
            part, phase = child[0], child[1]
            axis = "zy"[part] if phase == 1 else "yz"[part]
            size = d.rows_of[part][1] * d.q * HD * 2
            before = [("wait", msg)] if msg else []
            rank = (0, -hops(child), len(tasks))
            tasks.append((("send", child), 0.06, [], before, [(child, axis, size)], axis, rank))
            tasks.append((("wait", child), 0.12, [child], [], [], None, (1, 0, len(tasks))))
            add(child)

    add(None)
    return list_order(tasks, limit, latency)


def gather_children(d, msg):
    out = []
    if msg is None:
        for phase in (1, 2):
            for part in (0, 1):
                axis = "zy"[part] if phase == 1 else "yz"[part]
                for way in (0, 1):
                    if d.hops[axis][way] >= 1:
                        out.append((part, phase, way, 1, 0))
        return out
    part, phase, way, j, oa = msg
    first, second = ("z", "y") if part == 0 else ("y", "z")
    axis = first if phase == 1 else second
    if j < d.hops[axis][way]:
        out.append((part, phase, way, j + 1, oa))
    if phase == 1:
        here = -j if way == 0 else j
        for w2 in (0, 1):
            if d.hops[second][w2] >= 1:
                out.append((part, 2, w2, 1, here))
    return out


def reduce_order(d, limit=2, latency=2.75):
    tasks = []

    def add(name, cost, waits, before, sends, paced, kind, ahead):
        tasks.append((name, cost, waits, before, sends, paced, (kind, -ahead, len(tasks))))

    for n, (first, second) in enumerate((("y", "z"), ("z", "y"))):
        h1, h2, lanes = d.hops[first], d.hops[second], d.size[second]
        size = d.rows_of[n][1] * (d.q * HD * 2 + 512)
        for k in range(lanes):
            last = k == lanes - 1
            tail = 0 if last else h2[k % 2] - k // 2
            for w in (0, 1):
                if not h1[w]:
                    continue
                go = [((n, 1, w, 1, k), first, size)]
                add(("launch", n, w, k), 0.08, [], [], go, first, 1, h1[w] + tail)
                for j in range(1, h1[w]):
                    ahead = h1[w] - j + tail
                    pre = ("prebuild", n, w, j, k)
                    add(pre, 0.06, [], [], [], None, 2, ahead)
                    go = [((n, 1, w, j + 1, k), first, size)]
                    add(("relay", n, w, j, k), 0.22, [(n, 1, w, j, k)], [pre], go, None, 0, ahead)
            waits = [(n, 1, w, h1[w], k) for w in (0, 1) if h1[w]]
            if last:
                waits += [(n, 2, w, h2[w]) for w in (0, 1) if h2[w]]
            elif k >= 2:
                waits.append((n, 2, k % 2, k // 2))
            pre = ("build", n, 0, k)
            add(pre, 0.06, [], [], [], None, 2, tail)
            go = [] if last else [((n, 2, k % 2, k // 2 + 1), second, size)]
            add(("second", n, k), 0.28, waits, [pre], go, None, 0, tail)
    return list_order(tasks, limit, latency)


def iota(shape, dim):
    return lax.broadcasted_iota(jnp.int32, shape, dim)


def slot_plan(d, kv, ps, ctx, out, pieces):
    partner = kv + 1 - 2 * lax.rem(kv, 2)
    core = lax.rem(kv, 2)
    chunks = d.rows // 128
    eye = iota((128, 128), 0) == iota((128, 128), 1)
    lane = iota((128, 128), 1)
    row_in = iota((128, 128), 0)

    def to_col(row):
        return jnp.sum(jnp.where(eye, jnp.broadcast_to(row, (128, 128)), 0), axis=1, keepdims=True)

    def to_row(col):
        return jnp.sum(jnp.where(eye, jnp.broadcast_to(col, (128, 128)), 0), axis=0, keepdims=True)

    zero = jnp.zeros((1, 128), jnp.int32)
    base = [jnp.zeros((1, 1), jnp.int32) for _ in (0, 1)]
    acc = [[zero, zero, zero] for _ in (0, 1)]
    held = {}

    def piece(side, c):
        if side == 0:
            for n, owner in enumerate((kv, partner)):
                local = ps[c * 128 : (c + 1) * 128, :] - owner * d.slots
                hit = (local >= 0) & (local < d.slots)
                many = jnp.sum(hit.astype(jnp.int32), axis=1, keepdims=True)
                before = jnp.sum(jnp.where(row_in < lane, many, 0), axis=0, keepdims=True)
                start = to_col(before + base[n])
                last = jnp.where(many > 0, jnp.clip(start + many - 1, 0, d.slots), d.slots)
                out[5 + n * chunks + c : 6 + n * chunks + c, :] = to_row(last)
                base[n] = base[n] + jnp.sum(many, axis=0, keepdims=True)
                held[n] = (local, hit, many, start, last)
        local, hit, many, start, _ = held[side]
        elsewhere = held[1 - side][4]
        if side == 0:
            length = to_col(ctx[c : c + 1, :])
            left = jnp.clip(length - lane * d.slot_len, 0, d.slot_len)
            far = 1 << 30
            code = jnp.where(hit, lane * 32768 + local * 512 + left, far)
        for k in range(3):
            at = (lane == start + k) & (many > k)
            acc[side][1] += jnp.sum(jnp.where(at, row_in + c * 128, 0), axis=0, keepdims=True)
            acc[side][2] += jnp.sum(jnp.where(at, elsewhere, 0), axis=0, keepdims=True)
            if side == 0:
                first = jnp.min(code, axis=1, keepdims=True)
                code = jnp.where(code == first, far, code)
                acc[side][0] += jnp.sum(jnp.where(at, lax.rem(first, 32768), 0), axis=0, keepdims=True)

    def finish():
        for side in (0, 1):
            acc_val, acc_row, other = acc[side]
            out[5 + 2 * chunks + side : 6 + 2 * chunks + side, :] = jnp.clip(other, 0, d.slots)
            mine = lax.rem(acc_row // d.rg, 2) == core
            place = (acc_row // (2 * d.rg)) * d.rg + lax.rem(acc_row, d.rg)
            place = jnp.clip(place, 0, d.rows // 2 - 1)
            if side == 0:
                same = (iota((1, 128), 1) > 0) & (pltpu.roll(acc_row, 1, 1) == acc_row)
                out[0:1, :] = jnp.where(mine, place, -1)
                out[1:2, :] = jnp.clip(acc_val // 512, 0, d.slots - 1)
                out[2:3, :] = lax.rem(acc_val, 512)
                out[3:4, :] = jnp.where(same, 1, 0)
            else:
                out[4:5, :] = jnp.where(mine, place, 0)

    for c in range(chunks):
        for side in (0, 1):
            pieces.append(functools.partial(piece, side, c))
    pieces.append(finish)


def main_kernel(
    d, order, plan_reduce, ps, ctx, q_in, nk_in, nv_in, kc, vc, out,
    q_raw, nk, nv, stage, qx, psv, planv, meta, g, qp, qs, kb, vb, o, t, r0, r0s, r1, r1s, d0, d0s, d1, d1s, f, fs, rf, rfs,
    io_sem, kv_sem, tp_send, tp_recv, ag_send, ag_recv, fw_send, fw_recv, ex_send, ex_recv,
    s0_send, s0_recv, s1_send, s1_recv, fin_send, fin_recv,
):
    kv = lax.axis_index("kv")
    tp = lax.axis_index("tp")
    core = lax.rem(kv, 2)
    sgn = 1 - 2 * core
    chip = kv // 2
    pos = {"y": chip // d.nz, "z": lax.rem(chip, d.nz)}

    near = {}

    def coord(axis, k):
        n = d.size[axis]
        if (axis, k) not in near:
            near[axis, k] = lax.rem(pos[axis] + sgn * k + n, n)
        return near[axis, k]

    def chip_at(oy, oz):
        return coord("y", oy) * d.nz + coord("z", oz)

    def kv_at(oy, oz):
        return chip_at(oy, oz) * 2 + core

    def neighbour(axis, step):
        return (kv_at(step, 0) if axis == "y" else kv_at(0, step), tp)

    partner = (kv + sgn, tp)

    def remote(src, dst, ss, rs, dev):
        return pltpu.make_async_remote_copy(
            src_ref=src, dst_ref=dst, send_sem=ss, recv_sem=rs, device_id=dev, device_id_type=MESH
        )

    chunks = d.rows // 128

    q_copy = pltpu.make_async_copy(q_in, q_raw, io_sem.at[2])
    q_copy.start()
    new_copies = [
        pltpu.make_async_copy(src, dst, io_sem.at[n])
        for n, (src, dst) in enumerate(((nk_in, nk), (nv_in, nv)), 3)
    ]
    for cp in new_copies:
        cp.start()
    ps_copy = pltpu.make_async_copy(ps, psv, io_sem.at[0])
    ps_copy.start()
    parts_kv = kv_sem.shape[1]
    per = d.slots // parts_kv
    kv_copies = []
    for n in range(parts_kv):
        for which, (src, dst) in enumerate(((kc, kb), (vc, vb))):
            cp = pltpu.make_async_copy(
                src.at[pl.ds(n * per, per)], dst.at[pl.ds(n * per, per)], kv_sem.at[which, n]
            )
            cp.start()
            kv_copies.append(cp)

    friends = [partner]
    for axis in ("y", "z"):
        for way in (0, 1):
            if d.hops[axis][way]:
                friends.append(neighbour(axis, 1 - 2 * way))
    for k in range(1, d.ntp):
        friends.append((kv, lax.rem(tp + k, d.ntp)))
    barrier = pltpu.get_barrier_semaphore()
    for dev in friends:
        pl.semaphore_signal(barrier, inc=1, device_id=dev, device_id_type=MESH)

    q_copy.wait()
    heads = d.kvl * d.group
    for step in range(d.steps):
        q_step = q_raw[step].astype(F32)
        for h in range(d.ntp):
            for i in range(d.rd):
                for j in range(heads):
                    at = (h * heads + j) * HD
                    stage[h, i, pl.ds(step * heads + j, 1), :] = q_step[i : i + 1, at : at + HD]
    qx[...] = stage[...].astype(BF16)
    pl.semaphore_wait(barrier, len(friends))

    waits = []

    own = chip * d.rg
    tp_copies = []
    for k in range(1, d.ntp):
        other = lax.rem(tp + k, d.ntp)
        cp = remote(
            qx.at[other], g.at[pl.ds(own + tp * d.rd, d.rd)], tp_send.at[k - 1], tp_recv.at[k - 1], (kv, other)
        )
        cp.start()
        waits.append(cp)
    g[pl.ds(own + tp * d.rd, d.rd)] = qx[tp]
    for k in range(1, d.ntp):
        source = lax.rem(tp - k + d.ntp, d.ntp)
        remote(
            qx.at[tp], g.at[pl.ds(own + source * d.rd, d.rd)], tp_send.at[k - 1], tp_recv.at[k - 1], (kv, source)
        ).wait_recv()

    number = {msg: n for n, msg in enumerate(msg for what, msg in order if what == "send")}

    def place(msg, back):
        part, phase, way, j, oa = msg
        turn = 1 if way == 0 else -1
        steps = j - 1 if back else j
        o1 = -turn * steps if phase == 1 else oa
        o2 = 0 if phase == 1 else -turn * steps
        oz, oy = (o1, o2) if part == 0 else (o2, o1)
        start, count = d.rows_of[part]
        return g.at[pl.ds(chip_at(oy, oz) * d.rg + start, count)]

    def ship(msg):
        part, phase, way, j, oa = msg
        axis = "zy"[part] if phase == 1 else "yz"[part]
        n = number[msg]
        src = place(msg, True)
        cp = remote(src, src, ag_send.at[n], ag_recv.at[n], neighbour(axis, 1 - 2 * way))
        cp.start()
        waits.append(cp)

    ps_copy.wait()
    pieces = []
    slot_plan(d, kv, psv, ctx, planv, pieces)
    plan_copy = pltpu.make_async_copy(planv, meta, io_sem.at[1])
    for place_in, (what, msg) in enumerate(order):
        if what == "send":
            ship(msg)
            continue
        n = number[msg]
        landed = place(msg, False)
        remote(landed, landed, ag_send.at[n], ag_recv.at[n], partner).wait_recv()
        if place_in >= 16 and pieces:
            pieces.pop(0)()
            if not pieces:
                plan_copy.start()
    if pieces:
        while pieces:
            pieces.pop(0)()
        plan_copy.start()
    plan_copy.wait()

    def pick(i, c):
        for u in range(4):
            qs[4 * i + u] = g[meta[4, 4 * i + u]]
        return c

    lax.fori_loop(0, d.slots // 4, pick, 0)
    cp = remote(qs, qp, fw_send.at[0], fw_recv.at[0], partner)
    cp.start()
    for copy in kv_copies + new_copies:
        copy.wait()
    for other in waits:
        other.wait_send()
    waits.clear()
    cp.wait()

    head = lax.rem(iota((d.q, 128), 0) // d.group, d.kvl)
    head_masks = [(head == k).astype(F32).astype(BF16) for k in range(d.kvl)]
    lane128 = iota((d.q, 128), 1)
    lane_slot = iota((d.q, d.slot_len), 1)
    scale = 1.0 / math.sqrt(HD)

    unroll = 8

    def attend_many(it, carry):
        m_p, l_p, o_p, mc, lc = carry
        at = [it * unroll + u for u in range(unroll)]
        rows = [meta[0, i] for i in at]
        qs = [jnp.where(row >= 0, g[jnp.maximum(row, 0)], qp[i]) for row, i in zip(rows, at)]
        q2 = [jnp.concatenate([q * mask for mask in head_masks], axis=1) for q in qs]
        slots = [meta[1, i] for i in at]
        score = [
            lax.dot_general(q, kb[slot], (((1,), (1,)), ((), ())), preferred_element_type=F32)
            for q, slot in zip(q2, slots)
        ]
        score = [jnp.where(lane_slot < meta[2, i], x * scale, NEG) for x, i in zip(score, at)]
        tops = [jnp.max(x, axis=1, keepdims=True) for x in score]
        ps = [jnp.exp(x - m) for x, m in zip(score, tops)]
        sums = [jnp.dot(p.astype(BF16), vb[slot], preferred_element_type=F32) for p, slot in zip(ps, slots)]
        totals = [jnp.sum(p, axis=1, keepdims=True) for p in ps]
        accs = []
        for u, i in enumerate(at):
            o_s = sums[u][:, :HD]
            for k in range(1, d.kvl):
                o_s = jnp.where(head == k, sums[u][:, k * HD : (k + 1) * HD], o_s)
            m_q = jnp.where(meta[3, i] > 0, m_p, NEG)
            m = jnp.maximum(m_q, tops[u])
            a, b = jnp.exp(m_q - m), jnp.exp(tops[u] - m)
            l_p = l_p * a + totals[u] * b
            o_p = o_p * a + o_s * b
            m_p = m
            accs.append(o_p.astype(BF16))
            mc = jnp.where(lane128 == i, m_p, mc)
            lc = jnp.where(lane128 == i, l_p, lc)
        for u, i in enumerate(at):
            o[0, i] = accs[u]
        return m_p, l_p, o_p, mc, lc

    zero_col = jnp.zeros((d.q, 1), F32)
    zero = jnp.zeros((d.q, 128), F32)
    _, _, _, mc, lc = lax.fori_loop(
        0, d.slots // unroll, attend_many, (zero_col, zero_col, zero, jnp.full((d.q, 128), NEG, F32), zero)
    )
    pad = jnp.zeros((128 - d.q, 128), F32)
    mt = jnp.transpose(jnp.concatenate([mc, pad], axis=0))
    lt = jnp.transpose(jnp.concatenate([lc, pad], axis=0))
    table = jnp.where(iota((128, 128), 1) < 64, mt, pltpu.roll(lt, 64, 1))
    spare = t.shape[1] - d.slots
    t[0] = table[: t.shape[1]]
    nobody = jnp.where(iota((spare, 128), 1) < 64, NEG, 0.0)
    for side in (0, 1):
        t[side, pl.ds(d.slots, spare)] = nobody
        o[side, d.slots] = jnp.zeros((d.q, 128), BF16)

    for n, ref in enumerate((o, t)):
        cp = remote(
            ref.at[0, pl.ds(0, d.slots)], ref.at[1, pl.ds(0, d.slots)], ex_send.at[n], ex_recv.at[n], partner
        )
        cp.start()
        waits.append(cp)
    for n, ref in enumerate((o, t)):
        remote(
            ref.at[0, pl.ds(0, d.slots)], ref.at[1, pl.ds(0, d.slots)], ex_send.at[n], ex_recv.at[n], partner
        ).wait_recv()

    for cp in waits:
        cp.wait_send()
    waits.clear()

    lane8 = iota((8, 128), 1)
    factors, tiles = [], {}
    for side in (0, 1):
        for at in range(0, d.slots, 8):
            ids = [meta[5 + 2 * chunks + side, at + u] for u in range(8)]
            theirs = jnp.concatenate([t[1 - side, pl.ds(i, 1), :] for i in ids], axis=0)
            mine = t[side, pl.ds(at, 8), :]
            top = jnp.maximum(mine, theirs)
            factor = jnp.exp(mine - top)
            factors.append(factor)
            tiles[side, at] = jnp.where(lane8 < 64, top, mine * pltpu.roll(factor, 64, 1))
    cols = jnp.transpose(jnp.concatenate(factors, axis=0))
    for (side, at), tile in tiles.items():
        t[side, pl.ds(at, 8), :] = tile
    for side in (0, 1):
        for i in range(d.slots):
            n = side * d.slots + i
            o[side, i] = (o[side, i].astype(F32) * cols[: d.q, n : n + 1]).astype(BF16)

    def pad8(x):
        if x.shape[0] == 8:
            return x
        return jnp.concatenate([x, jnp.zeros((8 - x.shape[0], 128), F32)], axis=0)

    def prepare(stats, count):
        top = functools.reduce(jnp.maximum, stats)
        es = [jnp.exp(st - top) for st in stats]
        total = sum(e * pltpu.roll(st, 64, 1) for e, st in zip(es, stats))
        tile = jnp.where(lane8 < 64, top, pltpu.roll(total, 64, 1))[:count]
        return tile, jnp.transpose(jnp.concatenate(es, axis=0))

    def apply(tile, cols, rows, many, count, out_d, out_s):
        out_s[...] = tile
        for r in range(count):
            acc = None
            for k in range(many):
                term = rows(k, r).astype(F32) * cols[: d.q, k * 8 + r : k * 8 + r + 1]
                acc = term if acc is None else acc + term
            out_d[r] = acc.astype(BF16)

    def merge(jobs, count):
        tiles = [[pad8(x[1][...]) for x in ins] for ins, _ in jobs]
        ready = [prepare(stats, count) for stats in tiles]
        for (ins, dst), (tile, cols) in zip(jobs, ready):
            apply(tile, cols, lambda k, r: ins[k][0][r], len(ins), count, *dst)

    per_row = 128 // d.rg

    class Part:
        def __init__(self, first, second, rows, recv, recv_s, mine, mine_s, send_sem, recv_sem):
            self.first, self.second = first, second
            self.start, self.count = rows
            self.recv, self.recv_s, self.mine, self.mine_s = recv, recv_s, mine, mine_s
            self.send_sem, self.recv_sem = send_sem, recv_sem
            self.n1, self.lanes = d.size[first], d.size[second]
            self.h1, self.h2 = d.hops[first], d.hops[second]
            self.phase2 = sum(self.h1) * self.lanes
            self.to = {
                (axis, way): neighbour(axis, 1 - 2 * way) for axis in (first, second) for way in (0, 1)
            }

        def id1(self, way, j, lane):
            return (way * self.h1[0] + j - 1) * self.lanes + lane

        def id2(self, way, j):
            return self.phase2 + way * self.h2[0] + j - 1

        def bufs(self, n):
            return self.recv.at[n], self.recv_s.at[n]

        def chip_sum(self, o1, lane):
            n = (o1 % self.n1) * self.lanes + lane
            return self.mine.at[n], self.mine_s.at[n]

        def copies(self, src, n, axis, way):
            return [
                remote(a, b, self.send_sem.at[k, n], self.recv_sem.at[k, n], self.to[axis, way])
                for k, (a, b) in enumerate(zip(src, self.bufs(n)))
            ]

        def send(self, src, n, axis, way):
            for cp in self.copies(src, n, axis, way):
                cp.start()

        def wait(self, n):
            for cp in self.copies(self.bufs(n), n, self.first, 0):
                cp.wait_recv()

        def wait_sent(self, n):
            for cp in self.copies(self.bufs(n), n, self.first, 0):
                cp.wait_send()

        def lane(self, k):
            return (self.h2[0] + ((k + 1) // 2) * (1 if k % 2 else -1)) % self.lanes

        def build(self, o1, k):
            lane = self.lane(k)
            oy, oz = (o1, lane) if self.first == "y" else (lane, o1)
            kv_to = kv_at(oy, oz)
            line, col = lax.div(kv_to, per_row), lax.rem(kv_to, per_row) * d.rg + self.start
            ids = [
                [meta[5 + side * chunks + line, col + r] for r in range(self.count)] for side in (0, 1)
            ]
            stats = [
                jnp.concatenate([t[side, pl.ds(i, 1), :] for i in ids[side]], axis=0) for side in (0, 1)
            ]
            dst, dst_s = self.chip_sum(o1, lane)
            dst_s[...] = jnp.where(
                lane8[: self.count] < 64, jnp.maximum(stats[0], stats[1]), stats[0] + stats[1]
            )
            for r in range(self.count):
                dst[r] = o[0, ids[0][r]] + o[1, ids[1][r]]

        def launch(self, way, k):
            o1 = (1 - 2 * way) * self.h1[way]
            self.build(o1, k)
            lane = self.lane(k)
            self.send(self.chip_sum(o1, lane), self.id1(way, 1, lane), self.first, way)

        def prebuild(self, way, j, k):
            self.build((1 - 2 * way) * (self.h1[way] - j), k)

        def relay(self, way, j, k):
            lane = self.lane(k)
            n = self.id1(way, j, lane)
            self.wait(n)
            left = (1 - 2 * way) * (self.h1[way] - j)
            src = self.bufs(n)
            merge([([src, self.chip_sum(left, lane)], src)], self.count)
            self.send(src, self.id1(way, j + 1, lane), self.first, way)

        def second_step(self, k, result):
            lane = self.lane(k)
            ids = [self.id1(way, self.h1[way], lane) for way in (0, 1) if self.h1[way]]
            last = k == self.lanes - 1
            if last:
                ids += [self.id2(way, self.h2[way]) for way in (0, 1) if self.h2[way]]
            elif k >= 2:
                ids.append(self.id2(k % 2, k // 2))
            for n in ids:
                self.wait(n)
            ins = [self.bufs(n) for n in ids] + [self.chip_sum(0, lane)]
            dst = result if last else ins[0]
            merge([(ins, dst)], self.count)
            if not last:
                self.send(dst, self.id2(k % 2, k // 2 + 1), self.second, k % 2)

        def drain(self):
            def body(n, c):
                self.wait_sent(n)
                return c

            lax.fori_loop(0, self.phase2 + sum(self.h2), body, 0)

    p0 = Part("y", "z", d.rows_of[0], r0, r0s, d0, d0s, s0_send, s0_recv)
    p1 = Part("z", "y", d.rows_of[1], r1, r1s, d1, d1s, s1_send, s1_recv)
    fin0 = (f.at[pl.ds(p0.start, p0.count)], fs.at[pl.ds(p0.start, p0.count)])
    fin1 = (f.at[pl.ds(p1.start, p1.count)], fs.at[pl.ds(p1.start, p1.count)])

    parts, fins = (p0, p1), (fin0, fin1)
    for what, n, *rest in plan_reduce:
        if what == "second":
            parts[n].second_step(*rest, fins[n])
        else:
            getattr(parts[n], what)(*rest)

    for n in range(d.ntp):
        for i in range(d.rd):
            rfs_row = fs[n * d.rd + i : n * d.rd + i + 1, :]
            b1s_tmp = rfs_row
            rfs.at[d.ntp + n][i : i + 1, :] = b1s_tmp

    def final(k, dst_t, src_t, dev_t):
        return [
            remote(f.at[pl.ds(src_t * d.rd, d.rd)], rf.at[dst_t], fin_send.at[0, k], fin_recv.at[0, k], (kv, dev_t)),
            remote(rfs.at[d.ntp + src_t], rfs.at[dst_t], fin_send.at[1, k], fin_recv.at[1, k], (kv, dev_t)),
        ]

    for k in range(1, d.ntp):
        other = lax.rem(tp + k, d.ntp)
        for cp in final(k - 1, tp, other, other):
            cp.start()
            waits.append(cp)
    rf[tp] = f[pl.ds(tp * d.rd, d.rd)]
    rfs[tp] = rfs[d.ntp + tp]

    nkf = [nk[u].astype(F32) for u in range(d.steps)]
    nvf = [nv[u].astype(F32) for u in range(d.steps)]
    fresh = []
    for h in range(d.ntp):
        for i in range(d.rd):
            tops, totals, outs = [], [], []
            qf = qx[h, i].astype(F32)
            for step in range(d.steps):
                for k in range(d.kvl):
                    at = (step * d.kvl + k) * d.group
                    kk = h * d.kvl + k
                    qs = qf[at : at + d.group]
                    scores = [
                        jnp.sum(qs * nkf[u][i : i + 1, kk * HD : (kk + 1) * HD], axis=1, keepdims=True) * scale
                        for u in range(step + 1)
                    ]
                    top = functools.reduce(jnp.maximum, scores)
                    ws = [jnp.exp(x - top) for x in scores]
                    tops.append(top)
                    totals.append(sum(ws))
                    outs.append(sum(w * nvf[u][i : i + 1, kk * HD : (kk + 1) * HD] for u, w in enumerate(ws)))
            fresh.append([jnp.concatenate(x, axis=0) for x in (tops, totals, outs)])

    p0.drain()
    p1.drain()
    for k in range(1, d.ntp):
        source = lax.rem(tp - k + d.ntp, d.ntp)
        for cp in final(k - 1, source, tp, source):
            cp.wait_recv()
    for h in range(d.ntp):
        cols = jnp.transpose(pad8(rfs[h]))
        for i in range(d.rd):
            top_n, total_n, out_n = fresh[h * d.rd + i]
            top_c, total_c = cols[: d.q, i : i + 1], cols[64 : 64 + d.q, i : i + 1]
            top = jnp.maximum(top_n, top_c)
            a, b = jnp.exp(top_n - top), jnp.exp(top_c - top)
            numer = out_n * a + rf[h, i].astype(F32) * b
            result = (numer / (total_n * a + total_c * b)).astype(BF16)
            for step in range(d.steps):
                out[step, i, pl.ds(h * heads, heads)] = result[step * heads : (step + 1) * heads]

    for cp in waits:
        cp.wait_send()


def make_shards(d):
    order = gather_order(d)
    plan_reduce = reduce_order(d)

    def shards(queries, new_keys, new_values, key_cache, value_cache, context_lengths, piece_slots):
        steps, rd, width = queries.shape
        chunks = d.rows // 128
        vmem = pl.BlockSpec(memory_space=pltpu.VMEM)
        hbm = pl.BlockSpec(memory_space=pl.ANY)
        c0, c1 = d.rows_of[0][1], d.rows_of[1][1]
        n0 = sum(d.hops["y"]) * d.nz + sum(d.hops["z"])
        n1 = sum(d.hops["z"]) * d.ny + sum(d.hops["y"])
        pad = d.slots + 8
        dma = pltpu.SemaphoreType.DMA
        sem = lambda *shape: dma(shape)
        nt = max(d.ntp - 1, 1)
        plan_rows = -(-(7 + 2 * chunks) // 8) * 8
        scratch = [
            pltpu.VMEM(queries.shape, BF16),
            pltpu.VMEM(new_keys.shape, BF16),
            pltpu.VMEM(new_values.shape, BF16),
            pltpu.VMEM((d.ntp, rd, d.q, HD), F32),
            pltpu.VMEM((d.ntp, rd, d.q, HD), BF16),
            pltpu.VMEM(piece_slots.shape, jnp.int32),
            pltpu.VMEM((plan_rows, 128), jnp.int32),
            pltpu.SMEM((plan_rows, 128), jnp.int32),
            pltpu.VMEM((d.rows // 2, d.q, HD), BF16),
            pltpu.VMEM((d.slots, d.q, HD), BF16),
            pltpu.VMEM((d.slots, d.q, HD), BF16),
            pltpu.VMEM(key_cache.shape, BF16),
            pltpu.VMEM(value_cache.shape, BF16),
            pltpu.VMEM((2, pad, d.q, HD), BF16),
            pltpu.VMEM((2, pad, 128), F32),
            pltpu.VMEM((n0, c0, d.q, HD), BF16),
            pltpu.VMEM((n0, c0, 128), F32),
            pltpu.VMEM((n1, c1, d.q, HD), BF16),
            pltpu.VMEM((n1, c1, 128), F32),
            pltpu.VMEM((d.ny * d.nz, c0, d.q, HD), BF16),
            pltpu.VMEM((d.ny * d.nz, c0, 128), F32),
            pltpu.VMEM((d.ny * d.nz, c1, d.q, HD), BF16),
            pltpu.VMEM((d.ny * d.nz, c1, 128), F32),
            pltpu.VMEM((d.rg, d.q, HD), BF16),
            pltpu.VMEM((d.rg, 128), F32),
            pltpu.VMEM((d.ntp, rd, d.q, HD), BF16),
            pltpu.VMEM((2 * d.ntp, rd, 128), F32),
            sem(5), sem(2, 4), sem(nt), sem(nt), sem(len(order) // 2), sem(len(order) // 2), sem(1), sem(1),
            sem(2), sem(2), sem(2, n0), sem(2, n0), sem(2, n1), sem(2, n1), sem(2, nt), sem(2, nt),
        ]
        result = pl.pallas_call(
            functools.partial(main_kernel, d, order, plan_reduce),
            out_shape=jax.ShapeDtypeStruct((steps, rd, width // HD, HD), BF16),
            in_specs=[hbm, vmem, hbm, hbm, hbm, hbm, hbm],
            out_specs=vmem,
            scratch_shapes=scratch,
            compiler_params=pltpu.CompilerParams(
                collective_id=0, has_side_effects=True, vmem_limit_bytes=60 * 1024 * 1024
            ),
        )(piece_slots, context_lengths.reshape(chunks, 128), queries, new_keys, new_values, key_cache, value_cache)
        return result.reshape(steps, rd, width)

    return shards


def solution(mesh):
    d = Dims(4, 8, 4, 2, 40, 256, 3, 2, 8)
    return build(mesh, d)


def build(mesh, d):
    placed = (
        P(None, ("kv", "tp"), None),
        P(None, ("kv", "tp"), None),
        P(None, ("kv", "tp"), None),
        P("kv", None, "tp"),
        P("kv", None, "tp"),
        P(),
        P(),
    )
    return jax.shard_map(
        make_shards(d),
        mesh=mesh,
        in_specs=placed,
        out_specs=P(None, ("kv", "tp"), None),
        check_vma=False,
    )
```

```python
import functools
import math

import jax
import jax.numpy as jnp
from jax import lax
from jax.experimental import pallas as pl
from jax.experimental.pallas import tpu as pltpu
from jax.sharding import PartitionSpec as P

HD = 128
NEG = -1e30
MESH = pl.DeviceIdType.MESH
F32 = jnp.float32
BF16 = jnp.bfloat16


class Dims:
    def __init__(self, ny, nz, ntp, rows_dev, slots, slot_len, steps, kv_local, group):
        self.ny, self.nz, self.ntp, self.rd = ny, nz, ntp, rows_dev
        self.slots, self.slot_len = slots, slot_len
        self.steps, self.kvl, self.group = steps, kv_local, group
        self.rg = rows_dev * ntp
        self.kv = ny * nz * 2
        self.rows = self.kv * self.rg
        self.q = steps * kv_local * group
        self.split = (5 * self.rg) // 8
        self.size = {"y": ny, "z": nz}
        self.hops = {a: (n // 2, n - 1 - n // 2) for a, n in self.size.items()}
        self.rows_of = ((0, self.split), (self.split, self.rg - self.split))


def list_order(tasks, limit, latency, rate=95e3, tick=0.02):
    left = {t[0]: t for t in tasks}
    flying = {"y": [], "z": []}
    arrived, order = {}, []
    now, busy, running = 0.0, 0.0, None
    while left or running:
        if now >= busy - 1e-9:
            if running:
                for msg, axis, size in running[4]:
                    flying[axis].append([msg, size])
                running = None
            ready, urgent = [], set()
            for name, _, waits, before, _, paced, rank in left.values():
                if any(arrived.get(w, 1e9) > now for w in waits):
                    continue
                if any(x in left for x in before):
                    urgent.update(before)
                elif not paced or len(flying[paced]) < limit:
                    ready.append((rank, name))
            ready = [((0.5,) + r[1:] if n in urgent and r[0] > 0.5 else r, n) for r, n in ready]
            if ready:
                name = min(ready)[1]
                running = left.pop(name)
                order.append(name)
                busy = now + running[1]
        for axis, copies in flying.items():
            room = rate * tick
            for c in copies:
                part = min(room, c[1])
                c[1] -= part
                room -= part
                if c[1] <= 1e-9:
                    arrived[c[0]] = now + tick + latency
            flying[axis] = [c for c in copies if c[1] > 1e-9]
        now += tick
    return order


def gather_order(d, limit=2, latency=2.0):
    tasks, depth = [], {}

    def hops(msg):
        return max([1 + hops(c) for c in gather_children(d, msg)], default=0)

    def add(msg):
        for child in gather_children(d, msg):
            part, phase = child[0], child[1]
            axis = "zy"[part] if phase == 1 else "yz"[part]
            size = d.rows_of[part][1] * d.q * HD * 2
            before = [("wait", msg)] if msg else []
            rank = (0, -hops(child), len(tasks))
            tasks.append((("send", child), 0.06, [], before, [(child, axis, size)], axis, rank))
            tasks.append((("wait", child), 0.12, [child], [], [], None, (1, 0, len(tasks))))
            add(child)

    add(None)
    return list_order(tasks, limit, latency)


def gather_children(d, msg):
    out = []
    if msg is None:
        for phase in (1, 2):
            for part in (0, 1):
                axis = "zy"[part] if phase == 1 else "yz"[part]
                for way in (0, 1):
                    if d.hops[axis][way] >= 1:
                        out.append((part, phase, way, 1, 0))
        return out
    part, phase, way, j, oa = msg
    first, second = ("z", "y") if part == 0 else ("y", "z")
    axis = first if phase == 1 else second
    if j < d.hops[axis][way]:
        out.append((part, phase, way, j + 1, oa))
    if phase == 1:
        here = -j if way == 0 else j
        for w2 in (0, 1):
            if d.hops[second][w2] >= 1:
                out.append((part, 2, w2, 1, here))
    return out


def reduce_order(d, limit=2, latency=2.75):
    tasks = []

    def add(name, cost, waits, before, sends, paced, kind, ahead):
        tasks.append((name, cost, waits, before, sends, paced, (kind, -ahead, len(tasks))))

    for n, (first, second) in enumerate((("y", "z"), ("z", "y"))):
        h1, h2, lanes = d.hops[first], d.hops[second], d.size[second]
        size = d.rows_of[n][1] * (d.q * HD * 2 + 512)
        for k in range(lanes):
            last = k == lanes - 1
            tail = 0 if last else h2[k % 2] - k // 2
            for w in (0, 1):
                if not h1[w]:
                    continue
                go = [((n, 1, w, 1, k), first, size)]
                add(("launch", n, w, k), 0.08, [], [], go, first, 1, h1[w] + tail)
                for j in range(1, h1[w]):
                    ahead = h1[w] - j + tail
                    pre = ("prebuild", n, w, j, k)
                    add(pre, 0.06, [], [], [], None, 2, ahead)
                    go = [((n, 1, w, j + 1, k), first, size)]
                    add(("relay", n, w, j, k), 0.22, [(n, 1, w, j, k)], [pre], go, None, 0, ahead)
            waits = [(n, 1, w, h1[w], k) for w in (0, 1) if h1[w]]
            if last:
                waits += [(n, 2, w, h2[w]) for w in (0, 1) if h2[w]]
            elif k >= 2:
                waits.append((n, 2, k % 2, k // 2))
            pre = ("build", n, 0, k)
            add(pre, 0.06, [], [], [], None, 2, tail)
            go = [] if last else [((n, 2, k % 2, k // 2 + 1), second, size)]
            add(("second", n, k), 0.28, waits, [pre], go, None, 0, tail)
    return list_order(tasks, limit, latency)


def iota(shape, dim):
    return lax.broadcasted_iota(jnp.int32, shape, dim)


def slot_plan(d, kv, ps, ctx, out, pieces):
    partner = kv + 1 - 2 * lax.rem(kv, 2)
    core = lax.rem(kv, 2)
    chunks = d.rows // 128
    eye = iota((128, 128), 0) == iota((128, 128), 1)
    lane = iota((128, 128), 1)
    row_in = iota((128, 128), 0)

    def to_col(row):
        return jnp.sum(jnp.where(eye, jnp.broadcast_to(row, (128, 128)), 0), axis=1, keepdims=True)

    def to_row(col):
        return jnp.sum(jnp.where(eye, jnp.broadcast_to(col, (128, 128)), 0), axis=0, keepdims=True)

    zero = jnp.zeros((1, 128), jnp.int32)
    base = [jnp.zeros((1, 1), jnp.int32) for _ in (0, 1)]
    acc = [[zero, zero, zero] for _ in (0, 1)]
    held = {}

    def piece(side, c):
        if side == 0:
            for n, owner in enumerate((kv, partner)):
                local = ps[c * 128 : (c + 1) * 128, :] - owner * d.slots
                hit = (local >= 0) & (local < d.slots)
                many = jnp.sum(hit.astype(jnp.int32), axis=1, keepdims=True)
                before = jnp.sum(jnp.where(row_in < lane, many, 0), axis=0, keepdims=True)
                start = to_col(before + base[n])
                last = jnp.where(many > 0, jnp.clip(start + many - 1, 0, d.slots), d.slots)
                out[5 + n * chunks + c : 6 + n * chunks + c, :] = to_row(last)
                base[n] = base[n] + jnp.sum(many, axis=0, keepdims=True)
                held[n] = (local, hit, many, start, last)
        local, hit, many, start, _ = held[side]
        elsewhere = held[1 - side][4]
        if side == 0:
            length = to_col(ctx[c : c + 1, :])
            left = jnp.clip(length - lane * d.slot_len, 0, d.slot_len)
            far = 1 << 30
            code = jnp.where(hit, lane * 32768 + local * 512 + left, far)
        for k in range(3):
            at = (lane == start + k) & (many > k)
            acc[side][1] += jnp.sum(jnp.where(at, row_in + c * 128, 0), axis=0, keepdims=True)
            acc[side][2] += jnp.sum(jnp.where(at, elsewhere, 0), axis=0, keepdims=True)
            if side == 0:
                first = jnp.min(code, axis=1, keepdims=True)
                code = jnp.where(code == first, far, code)
                acc[side][0] += jnp.sum(jnp.where(at, lax.rem(first, 32768), 0), axis=0, keepdims=True)

    def finish():
        for side in (0, 1):
            acc_val, acc_row, other = acc[side]
            out[5 + 2 * chunks + side : 6 + 2 * chunks + side, :] = jnp.clip(other, 0, d.slots)
            mine = lax.rem(acc_row // d.rg, 2) == core
            place = (acc_row // (2 * d.rg)) * d.rg + lax.rem(acc_row, d.rg)
            place = jnp.clip(place, 0, d.rows // 2 - 1)
            if side == 0:
                same = (iota((1, 128), 1) > 0) & (pltpu.roll(acc_row, 1, 1) == acc_row)
                out[0:1, :] = jnp.where(mine, place, -1)
                out[1:2, :] = jnp.clip(acc_val // 512, 0, d.slots - 1)
                out[2:3, :] = lax.rem(acc_val, 512)
                out[3:4, :] = jnp.where(same, 1, 0)
            else:
                out[4:5, :] = jnp.where(mine, place, 0)

    for c in range(chunks):
        for side in (0, 1):
            pieces.append(functools.partial(piece, side, c))
    pieces.append(finish)


def main_kernel(
    d, order, plan_reduce, ps, ctx, q_in, nk_in, nv_in, kc, vc, out,
    q_raw, nk, nv, stage, fresh, qx, psv, planv, meta, g, qp, qs, kb, vb, o, t, r0, r0s, r1, r1s, d0, d0s, d1, d1s, f, fs, rf, rfs,
    io_sem, kv_sem, tp_send, tp_recv, ag_send, ag_recv, fw_send, fw_recv, ex_send, ex_recv,
    s0_send, s0_recv, s1_send, s1_recv, fin_send, fin_recv,
):
    kv = lax.axis_index("kv")
    tp = lax.axis_index("tp")
    core = lax.rem(kv, 2)
    sgn = 1 - 2 * core
    chip = kv // 2
    pos = {"y": chip // d.nz, "z": lax.rem(chip, d.nz)}

    near = {}

    def coord(axis, k):
        n = d.size[axis]
        if (axis, k) not in near:
            near[axis, k] = lax.rem(pos[axis] + sgn * k + n, n)
        return near[axis, k]

    def chip_at(oy, oz):
        return coord("y", oy) * d.nz + coord("z", oz)

    def kv_at(oy, oz):
        return chip_at(oy, oz) * 2 + core

    def neighbour(axis, step):
        return (kv_at(step, 0) if axis == "y" else kv_at(0, step), tp)

    partner = (kv + sgn, tp)

    def remote(src, dst, ss, rs, dev):
        return pltpu.make_async_remote_copy(
            src_ref=src, dst_ref=dst, send_sem=ss, recv_sem=rs, device_id=dev, device_id_type=MESH
        )

    chunks = d.rows // 128

    q_copy = pltpu.make_async_copy(q_in, q_raw, io_sem.at[2])
    q_copy.start()
    new_copies = [
        pltpu.make_async_copy(src, dst, io_sem.at[n])
        for n, (src, dst) in enumerate(((nk_in, nk), (nv_in, nv)), 3)
    ]
    for cp in new_copies:
        cp.start()
    ps_copy = pltpu.make_async_copy(ps, psv, io_sem.at[0])
    ps_copy.start()
    parts_kv = kv_sem.shape[1]
    per = d.slots // parts_kv
    kv_copies = []
    for n in range(parts_kv):
        for which, (src, dst) in enumerate(((kc, kb), (vc, vb))):
            cp = pltpu.make_async_copy(
                src.at[pl.ds(n * per, per)], dst.at[pl.ds(n * per, per)], kv_sem.at[which, n]
            )
            cp.start()
            kv_copies.append(cp)

    friends = [partner]
    for axis in ("y", "z"):
        for way in (0, 1):
            if d.hops[axis][way]:
                friends.append(neighbour(axis, 1 - 2 * way))
    for k in range(1, d.ntp):
        friends.append((kv, lax.rem(tp + k, d.ntp)))
    barrier = pltpu.get_barrier_semaphore()
    for dev in friends:
        pl.semaphore_signal(barrier, inc=1, device_id=dev, device_id_type=MESH)

    q_copy.wait()
    heads = d.kvl * d.group
    for step in range(d.steps):
        q_step = q_raw[step].astype(F32)
        for h in range(d.ntp):
            for i in range(d.rd):
                for j in range(heads):
                    at = (h * heads + j) * HD
                    stage[h, i, pl.ds(step * heads + j, 1), :] = q_step[i : i + 1, at : at + HD]
    qx[...] = stage[...].astype(BF16)
    pl.semaphore_wait(barrier, len(friends))

    waits = []

    own = chip * d.rg
    tp_copies = []
    for k in range(1, d.ntp):
        other = lax.rem(tp + k, d.ntp)
        cp = remote(
            qx.at[other], g.at[pl.ds(own + tp * d.rd, d.rd)], tp_send.at[k - 1], tp_recv.at[k - 1], (kv, other)
        )
        cp.start()
        waits.append(cp)
    g[pl.ds(own + tp * d.rd, d.rd)] = qx[tp]
    for k in range(1, d.ntp):
        source = lax.rem(tp - k + d.ntp, d.ntp)
        remote(
            qx.at[tp], g.at[pl.ds(own + source * d.rd, d.rd)], tp_send.at[k - 1], tp_recv.at[k - 1], (kv, source)
        ).wait_recv()

    number = {msg: n for n, msg in enumerate(msg for what, msg in order if what == "send")}

    def place(msg, back):
        part, phase, way, j, oa = msg
        turn = 1 if way == 0 else -1
        steps = j - 1 if back else j
        o1 = -turn * steps if phase == 1 else oa
        o2 = 0 if phase == 1 else -turn * steps
        oz, oy = (o1, o2) if part == 0 else (o2, o1)
        start, count = d.rows_of[part]
        return g.at[pl.ds(chip_at(oy, oz) * d.rg + start, count)]

    def ship(msg):
        part, phase, way, j, oa = msg
        axis = "zy"[part] if phase == 1 else "yz"[part]
        n = number[msg]
        src = place(msg, True)
        cp = remote(src, src, ag_send.at[n], ag_recv.at[n], neighbour(axis, 1 - 2 * way))
        cp.start()
        waits.append(cp)

    ps_copy.wait()
    pieces = []
    slot_plan(d, kv, psv, ctx, planv, pieces)
    plan_copy = pltpu.make_async_copy(planv, meta, io_sem.at[1])
    for place_in, (what, msg) in enumerate(order):
        if what == "send":
            ship(msg)
            continue
        n = number[msg]
        landed = place(msg, False)
        remote(landed, landed, ag_send.at[n], ag_recv.at[n], partner).wait_recv()
        if place_in >= 16 and pieces:
            pieces.pop(0)()
            if not pieces:
                plan_copy.start()
    if pieces:
        while pieces:
            pieces.pop(0)()
        plan_copy.start()
    plan_copy.wait()

    unroll = 8

    def chunk(src, dst, send, recv, n):
        at = pl.ds(n * unroll, unroll)
        return remote(src.at[at], dst.at[at], send.at[n], recv.at[n], partner)

    def pick(n, c):
        for u in range(unroll):
            qs[n * unroll + u] = g[meta[4, n * unroll + u]]
        chunk(qs, qp, fw_send, fw_recv, n).start()
        return c

    chunks_of_slots = d.slots // unroll
    lax.fori_loop(0, chunks_of_slots, pick, 0)
    for copy in kv_copies + new_copies:
        copy.wait()
    for other in waits:
        other.wait_send()
    waits.clear()

    head = lax.rem(iota((d.q, 128), 0) // d.group, d.kvl)
    head_masks = [(head == k).astype(F32).astype(BF16) for k in range(d.kvl)]
    lane128 = iota((d.q, 128), 1)
    lane_slot = iota((d.q, d.slot_len), 1)
    scale = 1.0 / math.sqrt(HD)

    def attend_many(it, carry):
        chunk(qs, qp, fw_send, fw_recv, it).wait_recv()
        m_p, l_p, o_p, mc, lc = carry
        at = [it * unroll + u for u in range(unroll)]
        rows = [meta[0, i] for i in at]
        q1 = [jnp.where(row >= 0, g[jnp.maximum(row, 0)], qp[i]) for row, i in zip(rows, at)]
        q2 = [jnp.concatenate([q * mask for mask in head_masks], axis=1) for q in q1]
        slots = [meta[1, i] for i in at]
        score = [
            lax.dot_general(q, kb[slot], (((1,), (1,)), ((), ())), preferred_element_type=F32)
            for q, slot in zip(q2, slots)
        ]
        score = [jnp.where(lane_slot < meta[2, i], x * scale, NEG) for x, i in zip(score, at)]
        tops = [jnp.max(x, axis=1, keepdims=True) for x in score]
        ps = [jnp.exp(x - m) for x, m in zip(score, tops)]
        sums = [jnp.dot(p.astype(BF16), vb[slot], preferred_element_type=F32) for p, slot in zip(ps, slots)]
        totals = [jnp.sum(p, axis=1, keepdims=True) for p in ps]
        accs = []
        for u, i in enumerate(at):
            o_s = sums[u][:, :HD]
            for k in range(1, d.kvl):
                o_s = jnp.where(head == k, sums[u][:, k * HD : (k + 1) * HD], o_s)
            m_q = jnp.where(meta[3, i] > 0, m_p, NEG)
            m = jnp.maximum(m_q, tops[u])
            a, b = jnp.exp(m_q - m), jnp.exp(tops[u] - m)
            l_p = l_p * a + totals[u] * b
            o_p = o_p * a + o_s * b
            m_p = m
            accs.append(o_p.astype(BF16))
            mc = jnp.where(lane128 == i, m_p, mc)
            lc = jnp.where(lane128 == i, l_p, lc)
        for u, i in enumerate(at):
            o[0, i] = accs[u]
        chunk(o.at[0], o.at[1], ex_send, ex_recv, it).start()
        return m_p, l_p, o_p, mc, lc

    zero_col = jnp.zeros((d.q, 1), F32)
    zero = jnp.zeros((d.q, 128), F32)
    _, _, _, mc, lc = lax.fori_loop(
        0, d.slots // unroll, attend_many, (zero_col, zero_col, zero, jnp.full((d.q, 128), NEG, F32), zero)
    )
    pad = jnp.zeros((128 - d.q, 128), F32)
    mt = jnp.transpose(jnp.concatenate([mc, pad], axis=0))
    lt = jnp.transpose(jnp.concatenate([lc, pad], axis=0))
    table = jnp.where(iota((128, 128), 1) < 64, mt, pltpu.roll(lt, 64, 1))
    spare = t.shape[1] - d.slots
    t[0] = table[: t.shape[1]]
    nobody = jnp.where(iota((spare, 128), 1) < 64, NEG, 0.0)
    for side in (0, 1):
        t[side, pl.ds(d.slots, spare)] = nobody
        o[side, d.slots] = jnp.zeros((d.q, 128), BF16)

    table_copy = remote(
        t.at[0, pl.ds(0, d.slots)],
        t.at[1, pl.ds(0, d.slots)],
        ex_send.at[chunks_of_slots],
        ex_recv.at[chunks_of_slots],
        partner,
    )
    table_copy.start()

    nkf = [nk[u].astype(F32) for u in range(d.steps)]
    nvf = [nv[u].astype(F32) for u in range(d.steps)]
    for h in range(d.ntp):
        for i in range(d.rd):
            tops, totals, outs = [], [], []
            qf = qx[h, i].astype(F32)
            for step in range(d.steps):
                for k in range(d.kvl):
                    at = (step * d.kvl + k) * d.group
                    kk = h * d.kvl + k
                    q_k = qf[at : at + d.group]
                    scores = [
                        jnp.sum(q_k * nkf[u][i : i + 1, kk * HD : (kk + 1) * HD], axis=1, keepdims=True) * scale
                        for u in range(step + 1)
                    ]
                    top = functools.reduce(jnp.maximum, scores)
                    ws = [jnp.exp(x - top) for x in scores]
                    tops.append(top)
                    totals.append(sum(ws))
                    outs.append(sum(w * nvf[u][i : i + 1, kk * HD : (kk + 1) * HD] for u, w in enumerate(ws)))
            for n, x in enumerate((tops, totals)):
                fresh[h, i, n] = jnp.broadcast_to(jnp.concatenate(x, axis=0), (d.q, 128))
            stage[h, i] = jnp.concatenate(outs, axis=0)

    def exchanged(n, c):
        chunk(qs, qp, fw_send, fw_recv, n).wait_send()
        chunk(o.at[0], o.at[1], ex_send, ex_recv, n).wait()
        return c

    lax.fori_loop(0, chunks_of_slots, exchanged, 0)
    table_copy.wait()

    lane8 = iota((8, 128), 1)
    factors, tiles = [], {}
    for side in (0, 1):
        for at in range(0, d.slots, 8):
            ids = [meta[5 + 2 * chunks + side, at + u] for u in range(8)]
            theirs = jnp.concatenate([t[1 - side, pl.ds(i, 1), :] for i in ids], axis=0)
            mine = t[side, pl.ds(at, 8), :]
            top = jnp.maximum(mine, theirs)
            factor = jnp.exp(mine - top)
            factors.append(factor)
            tiles[side, at] = jnp.where(lane8 < 64, top, mine * pltpu.roll(factor, 64, 1))
    cols = jnp.transpose(jnp.concatenate(factors, axis=0))
    for (side, at), tile in tiles.items():
        t[side, pl.ds(at, 8), :] = tile
    for side in (0, 1):
        for i in range(d.slots):
            n = side * d.slots + i
            o[side, i] = (o[side, i].astype(F32) * cols[: d.q, n : n + 1]).astype(BF16)

    def pad8(x):
        if x.shape[0] == 8:
            return x
        return jnp.concatenate([x, jnp.zeros((8 - x.shape[0], 128), F32)], axis=0)

    def prepare(stats, count):
        top = functools.reduce(jnp.maximum, stats)
        es = [jnp.exp(st - top) for st in stats]
        total = sum(e * pltpu.roll(st, 64, 1) for e, st in zip(es, stats))
        tile = jnp.where(lane8 < 64, top, pltpu.roll(total, 64, 1))[:count]
        return tile, jnp.transpose(jnp.concatenate(es, axis=0))

    def apply(tile, cols, rows, many, count, out_d, out_s):
        out_s[...] = tile
        for r in range(count):
            acc = None
            for k in range(many):
                term = rows(k, r).astype(F32) * cols[: d.q, k * 8 + r : k * 8 + r + 1]
                acc = term if acc is None else acc + term
            out_d[r] = acc.astype(BF16)

    def merge(jobs, count):
        tiles = [[pad8(x[1][...]) for x in ins] for ins, _ in jobs]
        ready = [prepare(stats, count) for stats in tiles]
        for (ins, dst), (tile, cols) in zip(jobs, ready):
            apply(tile, cols, lambda k, r: ins[k][0][r], len(ins), count, *dst)

    per_row = 128 // d.rg

    class Part:
        def __init__(self, first, second, rows, recv, recv_s, mine, mine_s, send_sem, recv_sem):
            self.first, self.second = first, second
            self.start, self.count = rows
            self.recv, self.recv_s, self.mine, self.mine_s = recv, recv_s, mine, mine_s
            self.send_sem, self.recv_sem = send_sem, recv_sem
            self.n1, self.lanes = d.size[first], d.size[second]
            self.h1, self.h2 = d.hops[first], d.hops[second]
            self.phase2 = sum(self.h1) * self.lanes
            self.to = {
                (axis, way): neighbour(axis, 1 - 2 * way) for axis in (first, second) for way in (0, 1)
            }

        def id1(self, way, j, lane):
            return (way * self.h1[0] + j - 1) * self.lanes + lane

        def id2(self, way, j):
            return self.phase2 + way * self.h2[0] + j - 1

        def bufs(self, n):
            return self.recv.at[n], self.recv_s.at[n]

        def chip_sum(self, o1, lane):
            n = (o1 % self.n1) * self.lanes + lane
            return self.mine.at[n], self.mine_s.at[n]

        def copies(self, src, n, axis, way):
            return [
                remote(a, b, self.send_sem.at[k, n], self.recv_sem.at[k, n], self.to[axis, way])
                for k, (a, b) in enumerate(zip(src, self.bufs(n)))
            ]

        def send(self, src, n, axis, way):
            for cp in self.copies(src, n, axis, way):
                cp.start()

        def wait(self, n):
            for cp in self.copies(self.bufs(n), n, self.first, 0):
                cp.wait_recv()

        def wait_sent(self, n):
            for cp in self.copies(self.bufs(n), n, self.first, 0):
                cp.wait_send()

        def lane(self, k):
            return (self.h2[0] + ((k + 1) // 2) * (1 if k % 2 else -1)) % self.lanes

        def build(self, o1, k):
            lane = self.lane(k)
            oy, oz = (o1, lane) if self.first == "y" else (lane, o1)
            kv_to = kv_at(oy, oz)
            line, col = lax.div(kv_to, per_row), lax.rem(kv_to, per_row) * d.rg + self.start
            ids = [
                [meta[5 + side * chunks + line, col + r] for r in range(self.count)] for side in (0, 1)
            ]
            stats = [
                jnp.concatenate([t[side, pl.ds(i, 1), :] for i in ids[side]], axis=0) for side in (0, 1)
            ]
            dst, dst_s = self.chip_sum(o1, lane)
            dst_s[...] = jnp.where(
                lane8[: self.count] < 64, jnp.maximum(stats[0], stats[1]), stats[0] + stats[1]
            )
            for r in range(self.count):
                dst[r] = o[0, ids[0][r]] + o[1, ids[1][r]]

        def launch(self, way, k):
            o1 = (1 - 2 * way) * self.h1[way]
            self.build(o1, k)
            lane = self.lane(k)
            self.send(self.chip_sum(o1, lane), self.id1(way, 1, lane), self.first, way)

        def prebuild(self, way, j, k):
            self.build((1 - 2 * way) * (self.h1[way] - j), k)

        def relay(self, way, j, k):
            lane = self.lane(k)
            n = self.id1(way, j, lane)
            self.wait(n)
            left = (1 - 2 * way) * (self.h1[way] - j)
            src = self.bufs(n)
            merge([([src, self.chip_sum(left, lane)], src)], self.count)
            self.send(src, self.id1(way, j + 1, lane), self.first, way)

        def second_step(self, k, result):
            lane = self.lane(k)
            ids = [self.id1(way, self.h1[way], lane) for way in (0, 1) if self.h1[way]]
            last = k == self.lanes - 1
            if last:
                ids += [self.id2(way, self.h2[way]) for way in (0, 1) if self.h2[way]]
            elif k >= 2:
                ids.append(self.id2(k % 2, k // 2))
            for n in ids:
                self.wait(n)
            ins = [self.bufs(n) for n in ids] + [self.chip_sum(0, lane)]
            dst = result if last else ins[0]
            merge([(ins, dst)], self.count)
            if not last:
                self.send(dst, self.id2(k % 2, k // 2 + 1), self.second, k % 2)

        def drain(self):
            def body(n, c):
                self.wait_sent(n)
                return c

            lax.fori_loop(0, self.phase2 + sum(self.h2), body, 0)

    p0 = Part("y", "z", d.rows_of[0], r0, r0s, d0, d0s, s0_send, s0_recv)
    p1 = Part("z", "y", d.rows_of[1], r1, r1s, d1, d1s, s1_send, s1_recv)
    fin0 = (f.at[pl.ds(p0.start, p0.count)], fs.at[pl.ds(p0.start, p0.count)])
    fin1 = (f.at[pl.ds(p1.start, p1.count)], fs.at[pl.ds(p1.start, p1.count)])

    parts, fins = (p0, p1), (fin0, fin1)
    for what, n, *rest in plan_reduce:
        if what == "second":
            parts[n].second_step(*rest, fins[n])
        else:
            getattr(parts[n], what)(*rest)

    for n in range(d.ntp):
        for i in range(d.rd):
            rfs_row = fs[n * d.rd + i : n * d.rd + i + 1, :]
            b1s_tmp = rfs_row
            rfs.at[d.ntp + n][i : i + 1, :] = b1s_tmp

    def final(k, dst_t, src_t, dev_t):
        return [
            remote(f.at[pl.ds(src_t * d.rd, d.rd)], rf.at[dst_t], fin_send.at[0, k], fin_recv.at[0, k], (kv, dev_t)),
            remote(rfs.at[d.ntp + src_t], rfs.at[dst_t], fin_send.at[1, k], fin_recv.at[1, k], (kv, dev_t)),
        ]

    for k in range(1, d.ntp):
        other = lax.rem(tp + k, d.ntp)
        for cp in final(k - 1, tp, other, other):
            cp.start()
            waits.append(cp)
    rf[tp] = f[pl.ds(tp * d.rd, d.rd)]
    rfs[tp] = rfs[d.ntp + tp]

    p0.drain()
    p1.drain()
    for k in range(1, d.ntp):
        source = lax.rem(tp - k + d.ntp, d.ntp)
        for cp in final(k - 1, source, tp, source):
            cp.wait_recv()
    for h in range(d.ntp):
        cols = jnp.transpose(pad8(rfs[h]))
        for i in range(d.rd):
            top_n, total_n, out_n = fresh[h, i, 0], fresh[h, i, 1], stage[h, i]
            top_c, total_c = cols[: d.q, i : i + 1], cols[64 : 64 + d.q, i : i + 1]
            top = jnp.maximum(top_n, top_c)
            a, b = jnp.exp(top_n - top), jnp.exp(top_c - top)
            numer = out_n * a + rf[h, i].astype(F32) * b
            result = (numer / (total_n * a + total_c * b)).astype(BF16)
            for step in range(d.steps):
                out[step, i, pl.ds(h * heads, heads)] = result[step * heads : (step + 1) * heads]

    for cp in waits:
        cp.wait_send()


def make_shards(d):
    order = gather_order(d)
    plan_reduce = reduce_order(d)

    def shards(queries, new_keys, new_values, key_cache, value_cache, context_lengths, piece_slots):
        steps, rd, width = queries.shape
        chunks = d.rows // 128
        vmem = pl.BlockSpec(memory_space=pltpu.VMEM)
        hbm = pl.BlockSpec(memory_space=pl.ANY)
        c0, c1 = d.rows_of[0][1], d.rows_of[1][1]
        n0 = sum(d.hops["y"]) * d.nz + sum(d.hops["z"])
        n1 = sum(d.hops["z"]) * d.ny + sum(d.hops["y"])
        pad = d.slots + 8
        dma = pltpu.SemaphoreType.DMA
        sem = lambda *shape: dma(shape)
        nt = max(d.ntp - 1, 1)
        plan_rows = -(-(7 + 2 * chunks) // 8) * 8
        scratch = [
            pltpu.VMEM(queries.shape, BF16),
            pltpu.VMEM(new_keys.shape, BF16),
            pltpu.VMEM(new_values.shape, BF16),
            pltpu.VMEM((d.ntp, rd, d.q, HD), F32),
            pltpu.VMEM((d.ntp, rd, 2, d.q, 128), F32),
            pltpu.VMEM((d.ntp, rd, d.q, HD), BF16),
            pltpu.VMEM(piece_slots.shape, jnp.int32),
            pltpu.VMEM((plan_rows, 128), jnp.int32),
            pltpu.SMEM((plan_rows, 128), jnp.int32),
            pltpu.VMEM((d.rows // 2, d.q, HD), BF16),
            pltpu.VMEM((d.slots, d.q, HD), BF16),
            pltpu.VMEM((d.slots, d.q, HD), BF16),
            pltpu.VMEM(key_cache.shape, BF16),
            pltpu.VMEM(value_cache.shape, BF16),
            pltpu.VMEM((2, pad, d.q, HD), BF16),
            pltpu.VMEM((2, pad, 128), F32),
            pltpu.VMEM((n0, c0, d.q, HD), BF16),
            pltpu.VMEM((n0, c0, 128), F32),
            pltpu.VMEM((n1, c1, d.q, HD), BF16),
            pltpu.VMEM((n1, c1, 128), F32),
            pltpu.VMEM((d.ny * d.nz, c0, d.q, HD), BF16),
            pltpu.VMEM((d.ny * d.nz, c0, 128), F32),
            pltpu.VMEM((d.ny * d.nz, c1, d.q, HD), BF16),
            pltpu.VMEM((d.ny * d.nz, c1, 128), F32),
            pltpu.VMEM((d.rg, d.q, HD), BF16),
            pltpu.VMEM((d.rg, 128), F32),
            pltpu.VMEM((d.ntp, rd, d.q, HD), BF16),
            pltpu.VMEM((2 * d.ntp, rd, 128), F32),
            sem(5), sem(2, 4), sem(nt), sem(nt), sem(len(order) // 2), sem(len(order) // 2), sem(d.slots // 8), sem(d.slots // 8),
            sem(d.slots // 8 + 1), sem(d.slots // 8 + 1), sem(2, n0), sem(2, n0), sem(2, n1), sem(2, n1), sem(2, nt), sem(2, nt),
        ]
        result = pl.pallas_call(
            functools.partial(main_kernel, d, order, plan_reduce),
            out_shape=jax.ShapeDtypeStruct((steps, rd, width // HD, HD), BF16),
            in_specs=[hbm, vmem, hbm, hbm, hbm, hbm, hbm],
            out_specs=vmem,
            scratch_shapes=scratch,
            compiler_params=pltpu.CompilerParams(
                collective_id=0, has_side_effects=True, vmem_limit_bytes=60 * 1024 * 1024
            ),
        )(piece_slots, context_lengths.reshape(chunks, 128), queries, new_keys, new_values, key_cache, value_cache)
        return result.reshape(steps, rd, width)

    return shards


def solution(mesh):
    d = Dims(4, 8, 4, 2, 40, 256, 3, 2, 8)
    return build(mesh, d)


def build(mesh, d):
    placed = (
        P(None, ("kv", "tp"), None),
        P(None, ("kv", "tp"), None),
        P(None, ("kv", "tp"), None),
        P("kv", None, "tp"),
        P("kv", None, "tp"),
        P(),
        P(),
    )
    return jax.shard_map(
        make_shards(d),
        mesh=mesh,
        in_specs=placed,
        out_specs=P(None, ("kv", "tp"), None),
        check_vma=False,
    )
```

```python
import functools
import math

import jax
import jax.numpy as jnp
from jax import lax
from jax.experimental import pallas as pl
from jax.experimental.pallas import tpu as pltpu
from jax.sharding import PartitionSpec as P

HD = 128
NEG = -1e30
MESH = pl.DeviceIdType.MESH
F32 = jnp.float32
BF16 = jnp.bfloat16


class Dims:
    def __init__(self, ny, nz, ntp, rows_dev, slots, slot_len, steps, kv_local, group):
        self.ny, self.nz, self.ntp, self.rd = ny, nz, ntp, rows_dev
        self.slots, self.slot_len = slots, slot_len
        self.steps, self.kvl, self.group = steps, kv_local, group
        self.rg = rows_dev * ntp
        self.kv = ny * nz * 2
        self.rows = self.kv * self.rg
        self.q = steps * kv_local * group
        self.split = (5 * self.rg) // 8
        self.size = {"y": ny, "z": nz}
        self.hops = {a: (n // 2, n - 1 - n // 2) for a, n in self.size.items()}
        self.rows_of = ((0, self.split), (self.split, self.rg - self.split))


def list_order(tasks, limit, latency, rate=95e3, tick=0.02):
    left = {t[0]: t for t in tasks}
    flying = {"y": [], "z": []}
    arrived, order = {}, []
    now, busy, running = 0.0, 0.0, None
    while left or running:
        if now >= busy - 1e-9:
            if running:
                for msg, axis, size in running[4]:
                    flying[axis].append([msg, size])
                running = None
            ready, urgent = [], set()
            for name, _, waits, before, _, paced, rank in left.values():
                if any(arrived.get(w, 1e9) > now for w in waits):
                    continue
                if any(x in left for x in before):
                    urgent.update(before)
                elif not paced or len(flying[paced]) < limit:
                    ready.append((rank, name))
            ready = [((0.5,) + r[1:] if n in urgent and r[0] > 0.5 else r, n) for r, n in ready]
            if ready:
                name = min(ready)[1]
                running = left.pop(name)
                order.append(name)
                busy = now + running[1]
        for axis, copies in flying.items():
            room = rate * tick
            for c in copies:
                part = min(room, c[1])
                c[1] -= part
                room -= part
                if c[1] <= 1e-9:
                    arrived[c[0]] = now + tick + latency
            flying[axis] = [c for c in copies if c[1] > 1e-9]
        now += tick
    return order


def gather_order(d, limit=2, latency=2.0):
    tasks, depth = [], {}

    def hops(msg):
        return max([1 + hops(c) for c in gather_children(d, msg)], default=0)

    def add(msg):
        for child in gather_children(d, msg):
            part, phase = child[0], child[1]
            axis = "zy"[part] if phase == 1 else "yz"[part]
            size = d.rows_of[part][1] * d.q * HD * 2
            before = [("wait", msg)] if msg else []
            rank = (0, -hops(child), len(tasks))
            tasks.append((("send", child), 0.06, [], before, [(child, axis, size)], axis, rank))
            tasks.append((("wait", child), 0.12, [child], [], [], None, (1, 0, len(tasks))))
            add(child)

    add(None)
    return list_order(tasks, limit, latency)


def gather_children(d, msg):
    out = []
    if msg is None:
        for phase in (1, 2):
            for part in (0, 1):
                axis = "zy"[part] if phase == 1 else "yz"[part]
                for way in (0, 1):
                    if d.hops[axis][way] >= 1:
                        out.append((part, phase, way, 1, 0))
        return out
    part, phase, way, j, oa = msg
    first, second = ("z", "y") if part == 0 else ("y", "z")
    axis = first if phase == 1 else second
    if j < d.hops[axis][way]:
        out.append((part, phase, way, j + 1, oa))
    if phase == 1:
        here = -j if way == 0 else j
        for w2 in (0, 1):
            if d.hops[second][w2] >= 1:
                out.append((part, 2, w2, 1, here))
    return out


def reduce_order(d, limit=2, latency=2.75):
    tasks = []

    def add(name, cost, waits, before, sends, paced, kind, ahead):
        tasks.append((name, cost, waits, before, sends, paced, (kind, -ahead, len(tasks))))

    for n, (first, second) in enumerate((("y", "z"), ("z", "y"))):
        h1, h2, lanes = d.hops[first], d.hops[second], d.size[second]
        size = d.rows_of[n][1] * (d.q * HD * 2 + 512)
        for k in range(lanes):
            last = k == lanes - 1
            tail = 0 if last else h2[k % 2] - k // 2
            for w in (0, 1):
                if not h1[w]:
                    continue
                go = [((n, 1, w, 1, k), first, size)]
                add(("launch", n, w, k), 0.08, [], [], go, first, 1, h1[w] + tail)
                for j in range(1, h1[w]):
                    ahead = h1[w] - j + tail
                    pre = ("prebuild", n, w, j, k)
                    add(pre, 0.06, [], [], [], None, 2, ahead)
                    go = [((n, 1, w, j + 1, k), first, size)]
                    add(("relay", n, w, j, k), 0.22, [(n, 1, w, j, k)], [pre], go, None, 0, ahead)
            waits = [(n, 1, w, h1[w], k) for w in (0, 1) if h1[w]]
            if last:
                waits += [(n, 2, w, h2[w]) for w in (0, 1) if h2[w]]
            elif k >= 2:
                waits.append((n, 2, k % 2, k // 2))
            pre = ("build", n, 0, k)
            add(pre, 0.06, [], [], [], None, 2, tail)
            go = [] if last else [((n, 2, k % 2, k // 2 + 1), second, size)]
            add(("second", n, k), 0.28, waits, [pre], go, None, 0, tail)
    return list_order(tasks, limit, latency)


def iota(shape, dim):
    return lax.broadcasted_iota(jnp.int32, shape, dim)


def slot_plan(d, kv, ps, ctx, out, pieces):
    partner = kv + 1 - 2 * lax.rem(kv, 2)
    core = lax.rem(kv, 2)
    chunks = d.rows // 128
    eye = iota((128, 128), 0) == iota((128, 128), 1)
    lane = iota((128, 128), 1)
    row_in = iota((128, 128), 0)

    def to_col(row):
        return jnp.sum(jnp.where(eye, jnp.broadcast_to(row, (128, 128)), 0), axis=1, keepdims=True)

    def to_row(col):
        return jnp.sum(jnp.where(eye, jnp.broadcast_to(col, (128, 128)), 0), axis=0, keepdims=True)

    zero = jnp.zeros((1, 128), jnp.int32)
    base = [jnp.zeros((1, 1), jnp.int32) for _ in (0, 1)]
    acc = [[zero, zero, zero] for _ in (0, 1)]
    held = {}

    def piece(side, c):
        if side == 0:
            for n, owner in enumerate((kv, partner)):
                local = ps[c * 128 : (c + 1) * 128, :] - owner * d.slots
                hit = (local >= 0) & (local < d.slots)
                many = jnp.sum(hit.astype(jnp.int32), axis=1, keepdims=True)
                before = jnp.sum(jnp.where(row_in < lane, many, 0), axis=0, keepdims=True)
                start = to_col(before + base[n])
                last = jnp.where(many > 0, jnp.clip(start + many - 1, 0, d.slots), d.slots)
                out[5 + n * chunks + c : 6 + n * chunks + c, :] = to_row(last)
                base[n] = base[n] + jnp.sum(many, axis=0, keepdims=True)
                held[n] = (local, hit, many, start, last)
        local, hit, many, start, _ = held[side]
        elsewhere = held[1 - side][4]
        if side == 0:
            length = to_col(ctx[c : c + 1, :])
            left = jnp.clip(length - lane * d.slot_len, 0, d.slot_len)
            far = 1 << 30
            code = jnp.where(hit, lane * 32768 + local * 512 + left, far)
        for k in range(3):
            at = (lane == start + k) & (many > k)
            acc[side][1] += jnp.sum(jnp.where(at, row_in + c * 128, 0), axis=0, keepdims=True)
            acc[side][2] += jnp.sum(jnp.where(at, elsewhere, 0), axis=0, keepdims=True)
            if side == 0:
                first = jnp.min(code, axis=1, keepdims=True)
                code = jnp.where(code == first, far, code)
                acc[side][0] += jnp.sum(jnp.where(at, lax.rem(first, 32768), 0), axis=0, keepdims=True)

    def finish():
        for side in (0, 1):
            acc_val, acc_row, other = acc[side]
            out[5 + 2 * chunks + side : 6 + 2 * chunks + side, :] = jnp.clip(other, 0, d.slots)
            mine = lax.rem(acc_row // d.rg, 2) == core
            place = (acc_row // (2 * d.rg)) * d.rg + lax.rem(acc_row, d.rg)
            place = jnp.clip(place, 0, d.rows // 2 - 1)
            if side == 0:
                same = (iota((1, 128), 1) > 0) & (pltpu.roll(acc_row, 1, 1) == acc_row)
                out[0:1, :] = jnp.where(mine, place, -1)
                out[1:2, :] = jnp.clip(acc_val // 512, 0, d.slots - 1)
                out[2:3, :] = lax.rem(acc_val, 512)
                out[3:4, :] = jnp.where(same, 1, 0)
            else:
                out[4:5, :] = jnp.where(mine, place, 0)

    for c in range(chunks):
        for side in (0, 1):
            pieces.append(functools.partial(piece, side, c))
    pieces.append(finish)


def main_kernel(
    d, order, plan_reduce, ps, ctx, q_raw, nk, nv, kc, vc, out,
    stage, fresh, qx, planv, meta, g, qp, qs, kb, vb, o, t, r0, r0s, r1, r1s, d0, d0s, d1, d1s, f, fs, rf, rfs,
    io_sem, kv_sem, tp_send, tp_recv, ag_send, ag_recv, fw_send, fw_recv, ex_send, ex_recv,
    s0_send, s0_recv, s1_send, s1_recv, fin_send, fin_recv,
):
    kv = lax.axis_index("kv")
    tp = lax.axis_index("tp")
    core = lax.rem(kv, 2)
    sgn = 2 * core - 1
    chip = kv // 2
    pos = {"y": chip // d.nz, "z": lax.rem(chip, d.nz)}

    near = {}

    def coord(axis, k):
        n = d.size[axis]
        if (axis, k) not in near:
            near[axis, k] = lax.rem(pos[axis] + sgn * k + n, n)
        return near[axis, k]

    def chip_at(oy, oz):
        return coord("y", oy) * d.nz + coord("z", oz)

    def kv_at(oy, oz):
        return chip_at(oy, oz) * 2 + core

    def neighbour(axis, step):
        return (kv_at(step, 0) if axis == "y" else kv_at(0, step), tp)

    partner = (kv + 1 - 2 * core, tp)

    def remote(src, dst, ss, rs, dev):
        return pltpu.make_async_remote_copy(
            src_ref=src, dst_ref=dst, send_sem=ss, recv_sem=rs, device_id=dev, device_id_type=MESH
        )

    chunks = d.rows // 128

    parts_kv = kv_sem.shape[1]
    per = d.slots // parts_kv
    kv_copies = []
    for n in range(parts_kv):
        for which, (src, dst) in enumerate(((kc, kb), (vc, vb))):
            cp = pltpu.make_async_copy(
                src.at[pl.ds(n * per, per)], dst.at[pl.ds(n * per, per)], kv_sem.at[which, n]
            )
            cp.start()
            kv_copies.append(cp)

    friends = [partner]
    for axis in ("y", "z"):
        for way in (0, 1):
            if d.hops[axis][way]:
                friends.append(neighbour(axis, 1 - 2 * way))
    for k in range(1, d.ntp):
        friends.append((kv, lax.rem(tp + k, d.ntp)))
    barrier = pltpu.get_barrier_semaphore()
    for dev in friends:
        pl.semaphore_signal(barrier, inc=1, device_id=dev, device_id_type=MESH)

    heads = d.kvl * d.group
    for step in range(d.steps):
        q_step = q_raw[step].astype(F32)
        for h in range(d.ntp):
            for i in range(d.rd):
                for j in range(heads):
                    at = (h * heads + j) * HD
                    stage[h, i, pl.ds(step * heads + j, 1), :] = q_step[i : i + 1, at : at + HD]
    qx[...] = stage[...].astype(BF16)
    pl.semaphore_wait(barrier, len(friends))

    waits = []

    own = chip * d.rg
    tp_copies = []
    for k in range(1, d.ntp):
        other = lax.rem(tp + k, d.ntp)
        cp = remote(
            qx.at[other], g.at[pl.ds(own + tp * d.rd, d.rd)], tp_send.at[k - 1], tp_recv.at[k - 1], (kv, other)
        )
        cp.start()
        waits.append(cp)
    g[pl.ds(own + tp * d.rd, d.rd)] = qx[tp]
    for k in range(1, d.ntp):
        source = lax.rem(tp - k + d.ntp, d.ntp)
        remote(
            qx.at[tp], g.at[pl.ds(own + source * d.rd, d.rd)], tp_send.at[k - 1], tp_recv.at[k - 1], (kv, source)
        ).wait_recv()

    number = {msg: n for n, msg in enumerate(msg for what, msg in order if what == "send")}

    def place(msg, back):
        part, phase, way, j, oa = msg
        turn = 1 if way == 0 else -1
        steps = j - 1 if back else j
        o1 = -turn * steps if phase == 1 else oa
        o2 = 0 if phase == 1 else -turn * steps
        oz, oy = (o1, o2) if part == 0 else (o2, o1)
        start, count = d.rows_of[part]
        return g.at[pl.ds(chip_at(oy, oz) * d.rg + start, count)]

    def ship(msg):
        part, phase, way, j, oa = msg
        axis = "zy"[part] if phase == 1 else "yz"[part]
        n = number[msg]
        src = place(msg, True)
        cp = remote(src, src, ag_send.at[n], ag_recv.at[n], neighbour(axis, 1 - 2 * way))
        cp.start()
        waits.append(cp)

    pieces = []
    slot_plan(d, kv, ps, ctx, planv, pieces)
    plan_copy = pltpu.make_async_copy(planv, meta, io_sem.at[0])
    for place_in, (what, msg) in enumerate(order):
        if what == "send":
            ship(msg)
            continue
        n = number[msg]
        landed = place(msg, False)
        remote(landed, landed, ag_send.at[n], ag_recv.at[n], partner).wait_recv()
        if place_in >= 16 and pieces:
            pieces.pop(0)()
            if not pieces:
                plan_copy.start()
    if pieces:
        while pieces:
            pieces.pop(0)()
        plan_copy.start()
    plan_copy.wait()

    unroll = 8

    def chunk(src, dst, send, recv, n):
        at = pl.ds(n * unroll, unroll)
        return remote(src.at[at], dst.at[at], send.at[n], recv.at[n], partner)

    def pick(n, c):
        for u in range(unroll):
            qs[n * unroll + u] = g[meta[4, n * unroll + u]]
        chunk(qs, qp, fw_send, fw_recv, n).start()
        return c

    chunks_of_slots = d.slots // unroll
    lax.fori_loop(0, chunks_of_slots, pick, 0)
    for copy in kv_copies:
        copy.wait()
    for other in waits:
        other.wait_send()
    waits.clear()

    head = lax.rem(iota((d.q, 128), 0) // d.group, d.kvl)
    head_masks = [(head == k).astype(F32).astype(BF16) for k in range(d.kvl)]
    lane128 = iota((d.q, 128), 1)
    lane_slot = iota((d.q, d.slot_len), 1)
    scale = 1.0 / math.sqrt(HD)

    def attend_many(it, carry):
        chunk(qs, qp, fw_send, fw_recv, it).wait_recv()
        m_p, l_p, o_p, mc, lc = carry
        at = [it * unroll + u for u in range(unroll)]
        rows = [meta[0, i] for i in at]
        q1 = [jnp.where(row >= 0, g[jnp.maximum(row, 0)], qp[i]) for row, i in zip(rows, at)]
        q2 = [jnp.concatenate([q * mask for mask in head_masks], axis=1) for q in q1]
        slots = [meta[1, i] for i in at]
        score = [
            lax.dot_general(q, kb[slot], (((1,), (1,)), ((), ())), preferred_element_type=F32)
            for q, slot in zip(q2, slots)
        ]
        score = [jnp.where(lane_slot < meta[2, i], x * scale, NEG) for x, i in zip(score, at)]
        tops = [jnp.max(x, axis=1, keepdims=True) for x in score]
        ps = [jnp.exp(x - m) for x, m in zip(score, tops)]
        sums = [jnp.dot(p.astype(BF16), vb[slot], preferred_element_type=F32) for p, slot in zip(ps, slots)]
        totals = [jnp.sum(p, axis=1, keepdims=True) for p in ps]
        accs = []
        for u, i in enumerate(at):
            o_s = sums[u][:, :HD]
            for k in range(1, d.kvl):
                o_s = jnp.where(head == k, sums[u][:, k * HD : (k + 1) * HD], o_s)
            m_q = jnp.where(meta[3, i] > 0, m_p, NEG)
            m = jnp.maximum(m_q, tops[u])
            a, b = jnp.exp(m_q - m), jnp.exp(tops[u] - m)
            l_p = l_p * a + totals[u] * b
            o_p = o_p * a + o_s * b
            m_p = m
            accs.append(o_p.astype(BF16))
            mc = jnp.where(lane128 == i, m_p, mc)
            lc = jnp.where(lane128 == i, l_p, lc)
        for u, i in enumerate(at):
            o[0, i] = accs[u]
        chunk(o.at[0], o.at[1], ex_send, ex_recv, it).start()
        return m_p, l_p, o_p, mc, lc

    zero_col = jnp.zeros((d.q, 1), F32)
    zero = jnp.zeros((d.q, 128), F32)
    _, _, _, mc, lc = lax.fori_loop(
        0, d.slots // unroll, attend_many, (zero_col, zero_col, zero, jnp.full((d.q, 128), NEG, F32), zero)
    )
    pad = jnp.zeros((128 - d.q, 128), F32)
    mt = jnp.transpose(jnp.concatenate([mc, pad], axis=0))
    lt = jnp.transpose(jnp.concatenate([lc, pad], axis=0))
    table = jnp.where(iota((128, 128), 1) < 64, mt, pltpu.roll(lt, 64, 1))
    spare = t.shape[1] - d.slots
    t[0] = table[: t.shape[1]]
    nobody = jnp.where(iota((spare, 128), 1) < 64, NEG, 0.0)
    for side in (0, 1):
        t[side, pl.ds(d.slots, spare)] = nobody
        o[side, d.slots] = jnp.zeros((d.q, 128), BF16)

    table_copy = remote(
        t.at[0, pl.ds(0, d.slots)],
        t.at[1, pl.ds(0, d.slots)],
        ex_send.at[chunks_of_slots],
        ex_recv.at[chunks_of_slots],
        partner,
    )
    table_copy.start()

    nkf = [nk[u].astype(F32) for u in range(d.steps)]
    nvf = [nv[u].astype(F32) for u in range(d.steps)]
    for h in range(d.ntp):
        for i in range(d.rd):
            tops, totals, outs = [], [], []
            qf = qx[h, i].astype(F32)
            for step in range(d.steps):
                for k in range(d.kvl):
                    at = (step * d.kvl + k) * d.group
                    kk = h * d.kvl + k
                    q_k = qf[at : at + d.group]
                    scores = [
                        jnp.sum(q_k * nkf[u][i : i + 1, kk * HD : (kk + 1) * HD], axis=1, keepdims=True) * scale
                        for u in range(step + 1)
                    ]
                    top = functools.reduce(jnp.maximum, scores)
                    ws = [jnp.exp(x - top) for x in scores]
                    tops.append(top)
                    totals.append(sum(ws))
                    outs.append(sum(w * nvf[u][i : i + 1, kk * HD : (kk + 1) * HD] for u, w in enumerate(ws)))
            for n, x in enumerate((tops, totals)):
                fresh[h, i, n] = jnp.broadcast_to(jnp.concatenate(x, axis=0), (d.q, 128))
            stage[h, i] = jnp.concatenate(outs, axis=0)

    def exchanged(n, c):
        chunk(qs, qp, fw_send, fw_recv, n).wait_send()
        chunk(o.at[0], o.at[1], ex_send, ex_recv, n).wait()
        return c

    lax.fori_loop(0, chunks_of_slots, exchanged, 0)
    table_copy.wait()

    lane8 = iota((8, 128), 1)
    factors, tiles = [], {}
    for side in (0, 1):
        for at in range(0, d.slots, 8):
            ids = [meta[5 + 2 * chunks + side, at + u] for u in range(8)]
            theirs = jnp.concatenate([t[1 - side, pl.ds(i, 1), :] for i in ids], axis=0)
            mine = t[side, pl.ds(at, 8), :]
            top = jnp.maximum(mine, theirs)
            factor = jnp.exp(mine - top)
            factors.append(factor)
            tiles[side, at] = jnp.where(lane8 < 64, top, mine * pltpu.roll(factor, 64, 1))
    cols = jnp.transpose(jnp.concatenate(factors, axis=0))
    for (side, at), tile in tiles.items():
        t[side, pl.ds(at, 8), :] = tile
    for side in (0, 1):
        for i in range(d.slots):
            n = side * d.slots + i
            o[side, i] = (o[side, i].astype(F32) * cols[: d.q, n : n + 1]).astype(BF16)

    def pad8(x):
        if x.shape[0] == 8:
            return x
        return jnp.concatenate([x, jnp.zeros((8 - x.shape[0], 128), F32)], axis=0)

    def prepare(stats, count):
        top = functools.reduce(jnp.maximum, stats)
        es = [jnp.exp(st - top) for st in stats]
        total = sum(e * pltpu.roll(st, 64, 1) for e, st in zip(es, stats))
        tile = jnp.where(lane8 < 64, top, pltpu.roll(total, 64, 1))[:count]
        return tile, jnp.transpose(jnp.concatenate(es, axis=0))

    def apply(tile, cols, rows, many, count, out_d, out_s):
        out_s[...] = tile
        for r in range(count):
            acc = None
            for k in range(many):
                term = rows(k, r).astype(F32) * cols[: d.q, k * 8 + r : k * 8 + r + 1]
                acc = term if acc is None else acc + term
            out_d[r] = acc.astype(BF16)

    def merge(jobs, count):
        tiles = [[pad8(x[1][...]) for x in ins] for ins, _ in jobs]
        ready = [prepare(stats, count) for stats in tiles]
        for (ins, dst), (tile, cols) in zip(jobs, ready):
            apply(tile, cols, lambda k, r: ins[k][0][r], len(ins), count, *dst)

    per_row = 128 // d.rg

    class Part:
        def __init__(self, first, second, rows, recv, recv_s, mine, mine_s, send_sem, recv_sem):
            self.first, self.second = first, second
            self.start, self.count = rows
            self.recv, self.recv_s, self.mine, self.mine_s = recv, recv_s, mine, mine_s
            self.send_sem, self.recv_sem = send_sem, recv_sem
            self.n1, self.lanes = d.size[first], d.size[second]
            self.h1, self.h2 = d.hops[first], d.hops[second]
            self.phase2 = sum(self.h1) * self.lanes
            self.to = {
                (axis, way): neighbour(axis, 1 - 2 * way) for axis in (first, second) for way in (0, 1)
            }

        def id1(self, way, j, lane):
            return (way * self.h1[0] + j - 1) * self.lanes + lane

        def id2(self, way, j):
            return self.phase2 + way * self.h2[0] + j - 1

        def bufs(self, n):
            return self.recv.at[n], self.recv_s.at[n]

        def chip_sum(self, o1, lane):
            n = (o1 % self.n1) * self.lanes + lane
            return self.mine.at[n], self.mine_s.at[n]

        def copies(self, src, n, axis, way):
            return [
                remote(a, b, self.send_sem.at[k, n], self.recv_sem.at[k, n], self.to[axis, way])
                for k, (a, b) in enumerate(zip(src, self.bufs(n)))
            ]

        def send(self, src, n, axis, way):
            for cp in self.copies(src, n, axis, way):
                cp.start()

        def wait(self, n):
            for cp in self.copies(self.bufs(n), n, self.first, 0):
                cp.wait_recv()

        def wait_sent(self, n):
            for cp in self.copies(self.bufs(n), n, self.first, 0):
                cp.wait_send()

        def lane(self, k):
            return (self.h2[0] + ((k + 1) // 2) * (1 if k % 2 else -1)) % self.lanes

        def build(self, o1, k):
            lane = self.lane(k)
            oy, oz = (o1, lane) if self.first == "y" else (lane, o1)
            kv_to = kv_at(oy, oz)
            line, col = lax.div(kv_to, per_row), lax.rem(kv_to, per_row) * d.rg + self.start
            ids = [
                [meta[5 + side * chunks + line, col + r] for r in range(self.count)] for side in (0, 1)
            ]
            stats = [
                jnp.concatenate([t[side, pl.ds(i, 1), :] for i in ids[side]], axis=0) for side in (0, 1)
            ]
            dst, dst_s = self.chip_sum(o1, lane)
            dst_s[...] = jnp.where(
                lane8[: self.count] < 64, jnp.maximum(stats[0], stats[1]), stats[0] + stats[1]
            )
            for r in range(self.count):
                dst[r] = o[0, ids[0][r]] + o[1, ids[1][r]]

        def launch(self, way, k):
            o1 = (1 - 2 * way) * self.h1[way]
            self.build(o1, k)
            lane = self.lane(k)
            self.send(self.chip_sum(o1, lane), self.id1(way, 1, lane), self.first, way)

        def prebuild(self, way, j, k):
            self.build((1 - 2 * way) * (self.h1[way] - j), k)

        def relay(self, way, j, k):
            lane = self.lane(k)
            n = self.id1(way, j, lane)
            self.wait(n)
            left = (1 - 2 * way) * (self.h1[way] - j)
            src = self.bufs(n)
            merge([([src, self.chip_sum(left, lane)], src)], self.count)
            self.send(src, self.id1(way, j + 1, lane), self.first, way)

        def second_step(self, k, result):
            lane = self.lane(k)
            ids = [self.id1(way, self.h1[way], lane) for way in (0, 1) if self.h1[way]]
            last = k == self.lanes - 1
            if last:
                ids += [self.id2(way, self.h2[way]) for way in (0, 1) if self.h2[way]]
            elif k >= 2:
                ids.append(self.id2(k % 2, k // 2))
            for n in ids:
                self.wait(n)
            ins = [self.bufs(n) for n in ids] + [self.chip_sum(0, lane)]
            dst = result if last else ins[0]
            merge([(ins, dst)], self.count)
            if not last:
                self.send(dst, self.id2(k % 2, k // 2 + 1), self.second, k % 2)

        def drain(self):
            def body(n, c):
                self.wait_sent(n)
                return c

            lax.fori_loop(0, self.phase2 + sum(self.h2), body, 0)

    p0 = Part("y", "z", d.rows_of[0], r0, r0s, d0, d0s, s0_send, s0_recv)
    p1 = Part("z", "y", d.rows_of[1], r1, r1s, d1, d1s, s1_send, s1_recv)
    fin0 = (f.at[pl.ds(p0.start, p0.count)], fs.at[pl.ds(p0.start, p0.count)])
    fin1 = (f.at[pl.ds(p1.start, p1.count)], fs.at[pl.ds(p1.start, p1.count)])

    parts, fins = (p0, p1), (fin0, fin1)
    for what, n, *rest in plan_reduce:
        if what == "second":
            parts[n].second_step(*rest, fins[n])
        else:
            getattr(parts[n], what)(*rest)

    for n in range(d.ntp):
        for i in range(d.rd):
            rfs_row = fs[n * d.rd + i : n * d.rd + i + 1, :]
            b1s_tmp = rfs_row
            rfs.at[d.ntp + n][i : i + 1, :] = b1s_tmp

    def final(k, dst_t, src_t, dev_t):
        return [
            remote(f.at[pl.ds(src_t * d.rd, d.rd)], rf.at[dst_t], fin_send.at[0, k], fin_recv.at[0, k], (kv, dev_t)),
            remote(rfs.at[d.ntp + src_t], rfs.at[dst_t], fin_send.at[1, k], fin_recv.at[1, k], (kv, dev_t)),
        ]

    for k in range(1, d.ntp):
        other = lax.rem(tp + k, d.ntp)
        for cp in final(k - 1, tp, other, other):
            cp.start()
            waits.append(cp)
    rf[tp] = f[pl.ds(tp * d.rd, d.rd)]
    rfs[tp] = rfs[d.ntp + tp]

    p0.drain()
    p1.drain()
    for k in range(1, d.ntp):
        source = lax.rem(tp - k + d.ntp, d.ntp)
        for cp in final(k - 1, source, tp, source):
            cp.wait_recv()
    for h in range(d.ntp):
        cols = jnp.transpose(pad8(rfs[h]))
        for i in range(d.rd):
            top_n, total_n, out_n = fresh[h, i, 0], fresh[h, i, 1], stage[h, i]
            top_c, total_c = cols[: d.q, i : i + 1], cols[64 : 64 + d.q, i : i + 1]
            top = jnp.maximum(top_n, top_c)
            a, b = jnp.exp(top_n - top), jnp.exp(top_c - top)
            numer = out_n * a + rf[h, i].astype(F32) * b
            result = (numer / (total_n * a + total_c * b)).astype(BF16)
            for step in range(d.steps):
                out[step, i, pl.ds(h * heads, heads)] = result[step * heads : (step + 1) * heads]

    for cp in waits:
        cp.wait_send()


def make_shards(d):
    order = gather_order(d)
    plan_reduce = reduce_order(d)

    def shards(queries, new_keys, new_values, key_cache, value_cache, context_lengths, piece_slots):
        steps, rd, width = queries.shape
        chunks = d.rows // 128
        vmem = pl.BlockSpec(memory_space=pltpu.VMEM)
        hbm = pl.BlockSpec(memory_space=pl.ANY)
        c0, c1 = d.rows_of[0][1], d.rows_of[1][1]
        n0 = sum(d.hops["y"]) * d.nz + sum(d.hops["z"])
        n1 = sum(d.hops["z"]) * d.ny + sum(d.hops["y"])
        pad = d.slots + 8
        dma = pltpu.SemaphoreType.DMA
        sem = lambda *shape: dma(shape)
        nt = max(d.ntp - 1, 1)
        plan_rows = -(-(7 + 2 * chunks) // 8) * 8
        scratch = [
            pltpu.VMEM((d.ntp, rd, d.q, HD), F32),
            pltpu.VMEM((d.ntp, rd, 2, d.q, 128), F32),
            pltpu.VMEM((d.ntp, rd, d.q, HD), BF16),
            pltpu.VMEM((plan_rows, 128), jnp.int32),
            pltpu.SMEM((plan_rows, 128), jnp.int32),
            pltpu.VMEM((d.rows // 2, d.q, HD), BF16),
            pltpu.VMEM((d.slots, d.q, HD), BF16),
            pltpu.VMEM((d.slots, d.q, HD), BF16),
            pltpu.VMEM(key_cache.shape, BF16),
            pltpu.VMEM(value_cache.shape, BF16),
            pltpu.VMEM((2, pad, d.q, HD), BF16),
            pltpu.VMEM((2, pad, 128), F32),
            pltpu.VMEM((n0, c0, d.q, HD), BF16),
            pltpu.VMEM((n0, c0, 128), F32),
            pltpu.VMEM((n1, c1, d.q, HD), BF16),
            pltpu.VMEM((n1, c1, 128), F32),
            pltpu.VMEM((d.ny * d.nz, c0, d.q, HD), BF16),
            pltpu.VMEM((d.ny * d.nz, c0, 128), F32),
            pltpu.VMEM((d.ny * d.nz, c1, d.q, HD), BF16),
            pltpu.VMEM((d.ny * d.nz, c1, 128), F32),
            pltpu.VMEM((d.rg, d.q, HD), BF16),
            pltpu.VMEM((d.rg, 128), F32),
            pltpu.VMEM((d.ntp, rd, d.q, HD), BF16),
            pltpu.VMEM((2 * d.ntp, rd, 128), F32),
            sem(1), sem(2, 4), sem(nt), sem(nt), sem(len(order) // 2), sem(len(order) // 2), sem(d.slots // 8), sem(d.slots // 8),
            sem(d.slots // 8 + 1), sem(d.slots // 8 + 1), sem(2, n0), sem(2, n0), sem(2, n1), sem(2, n1), sem(2, nt), sem(2, nt),
        ]
        result = pl.pallas_call(
            functools.partial(main_kernel, d, order, plan_reduce),
            out_shape=jax.ShapeDtypeStruct((steps, rd, width // HD, HD), BF16),
            in_specs=[vmem, vmem, vmem, vmem, vmem, hbm, hbm],
            out_specs=vmem,
            scratch_shapes=scratch,
            compiler_params=pltpu.CompilerParams(
                collective_id=0, has_side_effects=True, vmem_limit_bytes=52 * 1024 * 1024
            ),
        )(piece_slots, context_lengths.reshape(chunks, 128), queries, new_keys, new_values, key_cache, value_cache)
        return result.reshape(steps, rd, width)

    return shards


def solution(mesh):
    d = Dims(4, 8, 4, 2, 40, 256, 3, 2, 8)
    return build(mesh, d)


def build(mesh, d):
    placed = (
        P(None, ("kv", "tp"), None),
        P(None, ("kv", "tp"), None),
        P(None, ("kv", "tp"), None),
        P("kv", None, "tp"),
        P("kv", None, "tp"),
        P(),
        P(),
    )
    return jax.shard_map(
        make_shards(d),
        mesh=mesh,
        in_specs=placed,
        out_specs=P(None, ("kv", "tp"), None),
        check_vma=False,
    )
```

```python
import functools
import math

import jax
import jax.numpy as jnp
from jax import lax
from jax.experimental import pallas as pl
from jax.experimental.pallas import tpu as pltpu
from jax.sharding import PartitionSpec as P

HD = 128
NEG = -1e30
MESH = pl.DeviceIdType.MESH
F32 = jnp.float32
BF16 = jnp.bfloat16


class Dims:
    def __init__(self, ny, nz, ntp, rows_dev, slots, slot_len, steps, kv_local, group):
        self.ny, self.nz, self.ntp, self.rd = ny, nz, ntp, rows_dev
        self.slots, self.slot_len = slots, slot_len
        self.steps, self.kvl, self.group = steps, kv_local, group
        self.rg = rows_dev * ntp
        self.kv = ny * nz * 2
        self.rows = self.kv * self.rg
        self.q = steps * kv_local * group
        self.split = (5 * self.rg) // 8
        self.size = {"y": ny, "z": nz}
        self.hops = {a: (n // 2, n - 1 - n // 2) for a, n in self.size.items()}
        self.rows_of = ((0, self.split), (self.split, self.rg - self.split))


def list_order(tasks, limit, latency, rate=95e3, tick=0.02):
    left = {t[0]: t for t in tasks}
    flying = {"y": [], "z": []}
    arrived, order = {}, []
    now, busy, running = 0.0, 0.0, None
    while left or running:
        if now >= busy - 1e-9:
            if running:
                for msg, axis, size in running[4]:
                    flying[axis].append([msg, size])
                running = None
            ready, urgent = [], set()
            for name, _, waits, before, _, paced, rank in left.values():
                if any(arrived.get(w, 1e9) > now for w in waits):
                    continue
                if any(x in left for x in before):
                    urgent.update(before)
                elif not paced or len(flying[paced]) < limit:
                    ready.append((rank, name))
            ready = [((0.5,) + r[1:] if n in urgent and r[0] > 0.5 else r, n) for r, n in ready]
            if ready:
                name = min(ready)[1]
                running = left.pop(name)
                order.append(name)
                busy = now + running[1]
        for axis, copies in flying.items():
            room = rate * tick
            for c in copies:
                part = min(room, c[1])
                c[1] -= part
                room -= part
                if c[1] <= 1e-9:
                    arrived[c[0]] = now + tick + latency
            flying[axis] = [c for c in copies if c[1] > 1e-9]
        now += tick
    return order


def gather_order(d, limit=2, latency=2.0):
    tasks, depth = [], {}

    def hops(msg):
        return max([1 + hops(c) for c in gather_children(d, msg)], default=0)

    def add(msg):
        for child in gather_children(d, msg):
            part, phase = child[0], child[1]
            axis = "zy"[part] if phase == 1 else "yz"[part]
            size = d.rows_of[part][1] * d.q * HD * 2
            before = [("wait", msg)] if msg else []
            rank = (0, -hops(child), len(tasks))
            tasks.append((("send", child), 0.06, [], before, [(child, axis, size)], axis, rank))
            tasks.append((("wait", child), 0.12, [child], [], [], None, (1, 0, len(tasks))))
            add(child)

    add(None)
    return list_order(tasks, limit, latency)


def gather_children(d, msg):
    out = []
    if msg is None:
        for phase in (1, 2):
            for part in (0, 1):
                axis = "zy"[part] if phase == 1 else "yz"[part]
                for way in (0, 1):
                    if d.hops[axis][way] >= 1:
                        out.append((part, phase, way, 1, 0))
        return out
    part, phase, way, j, oa = msg
    first, second = ("z", "y") if part == 0 else ("y", "z")
    axis = first if phase == 1 else second
    if j < d.hops[axis][way]:
        out.append((part, phase, way, j + 1, oa))
    if phase == 1:
        here = -j if way == 0 else j
        for w2 in (0, 1):
            if d.hops[second][w2] >= 1:
                out.append((part, 2, w2, 1, here))
    return out


def reduce_order(d, limit=2, latency=2.75):
    tasks = []

    def add(name, cost, waits, before, sends, paced, kind, ahead):
        tasks.append((name, cost, waits, before, sends, paced, (kind, -ahead, len(tasks))))

    for n, (first, second) in enumerate((("y", "z"), ("z", "y"))):
        h1, h2, lanes = d.hops[first], d.hops[second], d.size[second]
        size = d.rows_of[n][1] * (d.q * HD * 2 + 512)
        for k in range(lanes):
            last = k == lanes - 1
            tail = 0 if last else h2[k % 2] - k // 2
            for w in (0, 1):
                if not h1[w]:
                    continue
                go = [((n, 1, w, 1, k), first, size)]
                add(("launch", n, w, k), 0.08, [], [], go, first, 1, h1[w] + tail)
                for j in range(1, h1[w]):
                    ahead = h1[w] - j + tail
                    pre = ("prebuild", n, w, j, k)
                    add(pre, 0.06, [], [], [], None, 2, ahead)
                    go = [((n, 1, w, j + 1, k), first, size)]
                    add(("relay", n, w, j, k), 0.22, [(n, 1, w, j, k)], [pre], go, None, 0, ahead)
            waits = [(n, 1, w, h1[w], k) for w in (0, 1) if h1[w]]
            if last:
                waits += [(n, 2, w, h2[w]) for w in (0, 1) if h2[w]]
            elif k >= 2:
                waits.append((n, 2, k % 2, k // 2))
            pre = ("build", n, 0, k)
            add(pre, 0.06, [], [], [], None, 2, tail)
            go = [] if last else [((n, 2, k % 2, k // 2 + 1), second, size)]
            add(("second", n, k), 0.28, waits, [pre], go, None, 0, tail)
    return list_order(tasks, limit, latency)


def iota(shape, dim):
    return lax.broadcasted_iota(jnp.int32, shape, dim)


def slot_plan(d, kv, ps, ctx, out, pieces):
    partner = kv + 1 - 2 * lax.rem(kv, 2)
    core = lax.rem(kv, 2)
    chunks = d.rows // 128
    eye = iota((128, 128), 0) == iota((128, 128), 1)
    lane = iota((128, 128), 1)
    row_in = iota((128, 128), 0)

    def to_col(row):
        return jnp.sum(jnp.where(eye, jnp.broadcast_to(row, (128, 128)), 0), axis=1, keepdims=True)

    def to_row(col):
        return jnp.sum(jnp.where(eye, jnp.broadcast_to(col, (128, 128)), 0), axis=0, keepdims=True)

    zero = jnp.zeros((1, 128), jnp.int32)
    base = [jnp.zeros((1, 1), jnp.int32) for _ in (0, 1)]
    acc = [[zero, zero, zero] for _ in (0, 1)]
    held = {}

    def piece(side, c):
        if side == 0:
            for n, owner in enumerate((kv, partner)):
                local = ps[c * 128 : (c + 1) * 128, :] - owner * d.slots
                hit = (local >= 0) & (local < d.slots)
                many = jnp.sum(hit.astype(jnp.int32), axis=1, keepdims=True)
                before = jnp.sum(jnp.where(row_in < lane, many, 0), axis=0, keepdims=True)
                start = to_col(before + base[n])
                last = jnp.where(many > 0, jnp.clip(start + many - 1, 0, d.slots), d.slots)
                out[5 + n * chunks + c : 6 + n * chunks + c, :] = to_row(last)
                base[n] = base[n] + jnp.sum(many, axis=0, keepdims=True)
                held[n] = (local, hit, many, start, last)
        local, hit, many, start, _ = held[side]
        elsewhere = held[1 - side][4]
        if side == 0:
            length = to_col(ctx[c : c + 1, :])
            left = jnp.clip(length - lane * d.slot_len, 0, d.slot_len)
            far = 1 << 30
            code = jnp.where(hit, lane * 32768 + local * 512 + left, far)
        for k in range(3):
            at = (lane == start + k) & (many > k)
            acc[side][1] += jnp.sum(jnp.where(at, row_in + c * 128, 0), axis=0, keepdims=True)
            acc[side][2] += jnp.sum(jnp.where(at, elsewhere, 0), axis=0, keepdims=True)
            if side == 0:
                first = jnp.min(code, axis=1, keepdims=True)
                code = jnp.where(code == first, far, code)
                acc[side][0] += jnp.sum(jnp.where(at, lax.rem(first, 32768), 0), axis=0, keepdims=True)

    def finish():
        for side in (0, 1):
            acc_val, acc_row, other = acc[side]
            out[5 + 2 * chunks + side : 6 + 2 * chunks + side, :] = jnp.clip(other, 0, d.slots)
            mine = lax.rem(acc_row // d.rg, 2) == core
            place = (acc_row // (2 * d.rg)) * d.rg + lax.rem(acc_row, d.rg)
            place = jnp.clip(place, 0, d.rows // 2 - 1)
            if side == 0:
                same = (iota((1, 128), 1) > 0) & (pltpu.roll(acc_row, 1, 1) == acc_row)
                out[0:1, :] = jnp.where(mine, place, -1)
                out[1:2, :] = jnp.clip(acc_val // 512, 0, d.slots - 1)
                out[2:3, :] = lax.rem(acc_val, 512)
                out[3:4, :] = jnp.where(same, 1, 0)
            else:
                out[4:5, :] = jnp.where(mine, place, 0)

    for c in range(chunks):
        for side in (0, 1):
            pieces.append(functools.partial(piece, side, c))
    pieces.append(finish)


def main_kernel(
    d, order, plan_reduce, ps, ctx_in, q_in, nk_in, nv_in, kc, vc, out,
    ctx, q_raw, nk, nv, stage, fresh, qx, psv, planv, meta, g, qp, qs, kb, vb, o, t, r0, r0s, r1, r1s, d0, d0s, d1, d1s, f, fs, rf, rfs,
    io_sem, kv_sem, tp_send, tp_recv, ag_send, ag_recv, fw_send, fw_recv, ex_send, ex_recv,
    s0_send, s0_recv, s1_send, s1_recv, fin_send, fin_recv,
):
    kv = lax.axis_index("kv")
    tp = lax.axis_index("tp")
    core = lax.rem(kv, 2)
    sgn = 2 * core - 1
    chip = kv // 2
    pos = {"y": chip // d.nz, "z": lax.rem(chip, d.nz)}

    near = {}

    def coord(axis, k):
        n = d.size[axis]
        if (axis, k) not in near:
            near[axis, k] = lax.rem(pos[axis] + sgn * k + n, n)
        return near[axis, k]

    def chip_at(oy, oz):
        return coord("y", oy) * d.nz + coord("z", oz)

    def kv_at(oy, oz):
        return chip_at(oy, oz) * 2 + core

    def neighbour(axis, step):
        return (kv_at(step, 0) if axis == "y" else kv_at(0, step), tp)

    partner = (kv + 1 - 2 * core, tp)

    def remote(src, dst, ss, rs, dev):
        return pltpu.make_async_remote_copy(
            src_ref=src, dst_ref=dst, send_sem=ss, recv_sem=rs, device_id=dev, device_id_type=MESH
        )

    chunks = d.rows // 128

    q_copy = pltpu.make_async_copy(q_in, q_raw, io_sem.at[2])
    q_copy.start()
    new_copies = [
        pltpu.make_async_copy(src, dst, io_sem.at[n])
        for n, (src, dst) in enumerate(((nk_in, nk), (nv_in, nv), (ctx_in, ctx)), 3)
    ]
    for cp in new_copies:
        cp.start()
    ps_copy = pltpu.make_async_copy(ps, psv, io_sem.at[0])
    ps_copy.start()
    parts_kv = kv_sem.shape[1]
    per = d.slots // parts_kv
    kv_copies = []
    for n in range(parts_kv):
        for which, (src, dst) in enumerate(((kc, kb), (vc, vb))):
            cp = pltpu.make_async_copy(
                src.at[pl.ds(n * per, per)], dst.at[pl.ds(n * per, per)], kv_sem.at[which, n]
            )
            cp.start()
            kv_copies.append(cp)

    friends = [partner]
    for axis in ("y", "z"):
        for way in (0, 1):
            if d.hops[axis][way]:
                friends.append(neighbour(axis, 1 - 2 * way))
    for k in range(1, d.ntp):
        friends.append((kv, lax.rem(tp + k, d.ntp)))
    barrier = pltpu.get_barrier_semaphore()
    for dev in friends:
        pl.semaphore_signal(barrier, inc=1, device_id=dev, device_id_type=MESH)

    q_copy.wait()
    heads = d.kvl * d.group
    for step in range(d.steps):
        q_step = q_raw[step].astype(F32)
        for h in range(d.ntp):
            for i in range(d.rd):
                for j in range(heads):
                    at = (h * heads + j) * HD
                    stage[h, i, pl.ds(step * heads + j, 1), :] = q_step[i : i + 1, at : at + HD]
    qx[...] = stage[...].astype(BF16)
    pl.semaphore_wait(barrier, len(friends))

    waits = []

    own = chip * d.rg
    tp_copies = []
    for k in range(1, d.ntp):
        other = lax.rem(tp + k, d.ntp)
        cp = remote(
            qx.at[other], g.at[pl.ds(own + tp * d.rd, d.rd)], tp_send.at[k - 1], tp_recv.at[k - 1], (kv, other)
        )
        cp.start()
        waits.append(cp)
    g[pl.ds(own + tp * d.rd, d.rd)] = qx[tp]
    for k in range(1, d.ntp):
        source = lax.rem(tp - k + d.ntp, d.ntp)
        remote(
            qx.at[tp], g.at[pl.ds(own + source * d.rd, d.rd)], tp_send.at[k - 1], tp_recv.at[k - 1], (kv, source)
        ).wait_recv()

    number = {msg: n for n, msg in enumerate(msg for what, msg in order if what == "send")}

    def place(msg, back):
        part, phase, way, j, oa = msg
        turn = 1 if way == 0 else -1
        steps = j - 1 if back else j
        o1 = -turn * steps if phase == 1 else oa
        o2 = 0 if phase == 1 else -turn * steps
        oz, oy = (o1, o2) if part == 0 else (o2, o1)
        start, count = d.rows_of[part]
        return g.at[pl.ds(chip_at(oy, oz) * d.rg + start, count)]

    def ship(msg):
        part, phase, way, j, oa = msg
        axis = "zy"[part] if phase == 1 else "yz"[part]
        n = number[msg]
        src = place(msg, True)
        cp = remote(src, src, ag_send.at[n], ag_recv.at[n], neighbour(axis, 1 - 2 * way))
        cp.start()
        waits.append(cp)

    ps_copy.wait()
    new_copies.pop().wait()
    pieces = []
    slot_plan(d, kv, psv, ctx, planv, pieces)
    plan_copy = pltpu.make_async_copy(planv, meta, io_sem.at[1])
    for place_in, (what, msg) in enumerate(order):
        if what == "send":
            ship(msg)
            continue
        n = number[msg]
        landed = place(msg, False)
        remote(landed, landed, ag_send.at[n], ag_recv.at[n], partner).wait_recv()
        if place_in >= 16 and pieces:
            pieces.pop(0)()
            if not pieces:
                plan_copy.start()
    if pieces:
        while pieces:
            pieces.pop(0)()
        plan_copy.start()
    plan_copy.wait()

    unroll = 8

    def chunk(src, dst, send, recv, n):
        at = pl.ds(n * unroll, unroll)
        return remote(src.at[at], dst.at[at], send.at[n], recv.at[n], partner)

    def pick(n, c):
        for u in range(unroll):
            qs[n * unroll + u] = g[meta[4, n * unroll + u]]
        chunk(qs, qp, fw_send, fw_recv, n).start()
        return c

    chunks_of_slots = d.slots // unroll
    lax.fori_loop(0, chunks_of_slots, pick, 0)
    for copy in kv_copies + new_copies:
        copy.wait()
    for other in waits:
        other.wait_send()
    waits.clear()

    head = lax.rem(iota((d.q, 128), 0) // d.group, d.kvl)
    head_masks = [(head == k).astype(F32).astype(BF16) for k in range(d.kvl)]
    lane128 = iota((d.q, 128), 1)
    lane_slot = iota((d.q, d.slot_len), 1)
    scale = 1.0 / math.sqrt(HD)

    def attend_many(it, carry):
        chunk(qs, qp, fw_send, fw_recv, it).wait_recv()
        m_p, l_p, o_p, mc, lc = carry
        at = [it * unroll + u for u in range(unroll)]
        rows = [meta[0, i] for i in at]
        q1 = [jnp.where(row >= 0, g[jnp.maximum(row, 0)], qp[i]) for row, i in zip(rows, at)]
        q2 = [jnp.concatenate([q * mask for mask in head_masks], axis=1) for q in q1]
        slots = [meta[1, i] for i in at]
        score = [
            lax.dot_general(q, kb[slot], (((1,), (1,)), ((), ())), preferred_element_type=F32)
            for q, slot in zip(q2, slots)
        ]
        score = [jnp.where(lane_slot < meta[2, i], x * scale, NEG) for x, i in zip(score, at)]
        tops = [jnp.max(x, axis=1, keepdims=True) for x in score]
        ps = [jnp.exp(x - m) for x, m in zip(score, tops)]
        sums = [jnp.dot(p.astype(BF16), vb[slot], preferred_element_type=F32) for p, slot in zip(ps, slots)]
        totals = [jnp.sum(p, axis=1, keepdims=True) for p in ps]
        accs = []
        for u, i in enumerate(at):
            o_s = sums[u][:, :HD]
            for k in range(1, d.kvl):
                o_s = jnp.where(head == k, sums[u][:, k * HD : (k + 1) * HD], o_s)
            m_q = jnp.where(meta[3, i] > 0, m_p, NEG)
            m = jnp.maximum(m_q, tops[u])
            a, b = jnp.exp(m_q - m), jnp.exp(tops[u] - m)
            l_p = l_p * a + totals[u] * b
            o_p = o_p * a + o_s * b
            m_p = m
            accs.append(o_p.astype(BF16))
            mc = jnp.where(lane128 == i, m_p, mc)
            lc = jnp.where(lane128 == i, l_p, lc)
        for u, i in enumerate(at):
            o[0, i] = accs[u]
        chunk(o.at[0], o.at[1], ex_send, ex_recv, it).start()
        return m_p, l_p, o_p, mc, lc

    zero_col = jnp.zeros((d.q, 1), F32)
    zero = jnp.zeros((d.q, 128), F32)
    _, _, _, mc, lc = lax.fori_loop(
        0, d.slots // unroll, attend_many, (zero_col, zero_col, zero, jnp.full((d.q, 128), NEG, F32), zero)
    )
    pad = jnp.zeros((128 - d.q, 128), F32)
    mt = jnp.transpose(jnp.concatenate([mc, pad], axis=0))
    lt = jnp.transpose(jnp.concatenate([lc, pad], axis=0))
    table = jnp.where(iota((128, 128), 1) < 64, mt, pltpu.roll(lt, 64, 1))
    spare = t.shape[1] - d.slots
    t[0] = table[: t.shape[1]]
    nobody = jnp.where(iota((spare, 128), 1) < 64, NEG, 0.0)
    for side in (0, 1):
        t[side, pl.ds(d.slots, spare)] = nobody
        o[side, d.slots] = jnp.zeros((d.q, 128), BF16)

    table_copy = remote(
        t.at[0, pl.ds(0, d.slots)],
        t.at[1, pl.ds(0, d.slots)],
        ex_send.at[chunks_of_slots],
        ex_recv.at[chunks_of_slots],
        partner,
    )
    table_copy.start()

    nkf = [nk[u].astype(F32) for u in range(d.steps)]
    nvf = [nv[u].astype(F32) for u in range(d.steps)]
    for h in range(d.ntp):
        for i in range(d.rd):
            tops, totals, outs = [], [], []
            qf = qx[h, i].astype(F32)
            for step in range(d.steps):
                for k in range(d.kvl):
                    at = (step * d.kvl + k) * d.group
                    kk = h * d.kvl + k
                    q_k = qf[at : at + d.group]
                    scores = [
                        jnp.sum(q_k * nkf[u][i : i + 1, kk * HD : (kk + 1) * HD], axis=1, keepdims=True) * scale
                        for u in range(step + 1)
                    ]
                    top = functools.reduce(jnp.maximum, scores)
                    ws = [jnp.exp(x - top) for x in scores]
                    tops.append(top)
                    totals.append(sum(ws))
                    outs.append(sum(w * nvf[u][i : i + 1, kk * HD : (kk + 1) * HD] for u, w in enumerate(ws)))
            for n, x in enumerate((tops, totals)):
                fresh[h, i, n] = jnp.broadcast_to(jnp.concatenate(x, axis=0), (d.q, 128))
            stage[h, i] = jnp.concatenate(outs, axis=0)

    def exchanged(n, c):
        chunk(qs, qp, fw_send, fw_recv, n).wait_send()
        chunk(o.at[0], o.at[1], ex_send, ex_recv, n).wait()
        return c

    lax.fori_loop(0, chunks_of_slots, exchanged, 0)
    table_copy.wait()

    lane8 = iota((8, 128), 1)
    factors, tiles = [], {}
    for side in (0, 1):
        for at in range(0, d.slots, 8):
            ids = [meta[5 + 2 * chunks + side, at + u] for u in range(8)]
            theirs = jnp.concatenate([t[1 - side, pl.ds(i, 1), :] for i in ids], axis=0)
            mine = t[side, pl.ds(at, 8), :]
            top = jnp.maximum(mine, theirs)
            factor = jnp.exp(mine - top)
            factors.append(factor)
            tiles[side, at] = jnp.where(lane8 < 64, top, mine * pltpu.roll(factor, 64, 1))
    cols = jnp.transpose(jnp.concatenate(factors, axis=0))
    for (side, at), tile in tiles.items():
        t[side, pl.ds(at, 8), :] = tile
    for side in (0, 1):
        for i in range(d.slots):
            n = side * d.slots + i
            o[side, i] = (o[side, i].astype(F32) * cols[: d.q, n : n + 1]).astype(BF16)

    def pad8(x):
        if x.shape[0] == 8:
            return x
        return jnp.concatenate([x, jnp.zeros((8 - x.shape[0], 128), F32)], axis=0)

    def prepare(stats, count):
        top = functools.reduce(jnp.maximum, stats)
        es = [jnp.exp(st - top) for st in stats]
        total = sum(e * pltpu.roll(st, 64, 1) for e, st in zip(es, stats))
        tile = jnp.where(lane8 < 64, top, pltpu.roll(total, 64, 1))[:count]
        return tile, jnp.transpose(jnp.concatenate(es, axis=0))

    def apply(tile, cols, rows, many, count, out_d, out_s):
        out_s[...] = tile
        for r in range(count):
            acc = None
            for k in range(many):
                term = rows(k, r).astype(F32) * cols[: d.q, k * 8 + r : k * 8 + r + 1]
                acc = term if acc is None else acc + term
            out_d[r] = acc.astype(BF16)

    def merge(jobs, count):
        tiles = [[pad8(x[1][...]) for x in ins] for ins, _ in jobs]
        ready = [prepare(stats, count) for stats in tiles]
        for (ins, dst), (tile, cols) in zip(jobs, ready):
            apply(tile, cols, lambda k, r: ins[k][0][r], len(ins), count, *dst)

    per_row = 128 // d.rg

    class Part:
        def __init__(self, first, second, rows, recv, recv_s, mine, mine_s, send_sem, recv_sem):
            self.first, self.second = first, second
            self.start, self.count = rows
            self.recv, self.recv_s, self.mine, self.mine_s = recv, recv_s, mine, mine_s
            self.send_sem, self.recv_sem = send_sem, recv_sem
            self.n1, self.lanes = d.size[first], d.size[second]
            self.h1, self.h2 = d.hops[first], d.hops[second]
            self.phase2 = sum(self.h1) * self.lanes
            self.to = {
                (axis, way): neighbour(axis, 1 - 2 * way) for axis in (first, second) for way in (0, 1)
            }

        def id1(self, way, j, lane):
            return (way * self.h1[0] + j - 1) * self.lanes + lane

        def id2(self, way, j):
            return self.phase2 + way * self.h2[0] + j - 1

        def bufs(self, n):
            return self.recv.at[n], self.recv_s.at[n]

        def chip_sum(self, o1, lane):
            n = (o1 % self.n1) * self.lanes + lane
            return self.mine.at[n], self.mine_s.at[n]

        def copies(self, src, n, axis, way):
            return [
                remote(a, b, self.send_sem.at[k, n], self.recv_sem.at[k, n], self.to[axis, way])
                for k, (a, b) in enumerate(zip(src, self.bufs(n)))
            ]

        def send(self, src, n, axis, way):
            for cp in self.copies(src, n, axis, way):
                cp.start()

        def wait(self, n):
            for cp in self.copies(self.bufs(n), n, self.first, 0):
                cp.wait_recv()

        def wait_sent(self, n):
            for cp in self.copies(self.bufs(n), n, self.first, 0):
                cp.wait_send()

        def lane(self, k):
            return (self.h2[0] + ((k + 1) // 2) * (1 if k % 2 else -1)) % self.lanes

        def build(self, o1, k):
            lane = self.lane(k)
            oy, oz = (o1, lane) if self.first == "y" else (lane, o1)
            kv_to = kv_at(oy, oz)
            line, col = lax.div(kv_to, per_row), lax.rem(kv_to, per_row) * d.rg + self.start
            ids = [
                [meta[5 + side * chunks + line, col + r] for r in range(self.count)] for side in (0, 1)
            ]
            stats = [
                jnp.concatenate([t[side, pl.ds(i, 1), :] for i in ids[side]], axis=0) for side in (0, 1)
            ]
            dst, dst_s = self.chip_sum(o1, lane)
            dst_s[...] = jnp.where(
                lane8[: self.count] < 64, jnp.maximum(stats[0], stats[1]), stats[0] + stats[1]
            )
            for r in range(self.count):
                dst[r] = o[0, ids[0][r]] + o[1, ids[1][r]]

        def launch(self, way, k):
            o1 = (1 - 2 * way) * self.h1[way]
            self.build(o1, k)
            lane = self.lane(k)
            self.send(self.chip_sum(o1, lane), self.id1(way, 1, lane), self.first, way)

        def prebuild(self, way, j, k):
            self.build((1 - 2 * way) * (self.h1[way] - j), k)

        def relay(self, way, j, k):
            lane = self.lane(k)
            n = self.id1(way, j, lane)
            self.wait(n)
            left = (1 - 2 * way) * (self.h1[way] - j)
            src = self.bufs(n)
            merge([([src, self.chip_sum(left, lane)], src)], self.count)
            self.send(src, self.id1(way, j + 1, lane), self.first, way)

        def second_step(self, k, result):
            lane = self.lane(k)
            ids = [self.id1(way, self.h1[way], lane) for way in (0, 1) if self.h1[way]]
            last = k == self.lanes - 1
            if last:
                ids += [self.id2(way, self.h2[way]) for way in (0, 1) if self.h2[way]]
            elif k >= 2:
                ids.append(self.id2(k % 2, k // 2))
            for n in ids:
                self.wait(n)
            ins = [self.bufs(n) for n in ids] + [self.chip_sum(0, lane)]
            dst = result if last else ins[0]
            merge([(ins, dst)], self.count)
            if not last:
                self.send(dst, self.id2(k % 2, k // 2 + 1), self.second, k % 2)

        def drain(self):
            def body(n, c):
                self.wait_sent(n)
                return c

            lax.fori_loop(0, self.phase2 + sum(self.h2), body, 0)

    p0 = Part("y", "z", d.rows_of[0], r0, r0s, d0, d0s, s0_send, s0_recv)
    p1 = Part("z", "y", d.rows_of[1], r1, r1s, d1, d1s, s1_send, s1_recv)
    fin0 = (f.at[pl.ds(p0.start, p0.count)], fs.at[pl.ds(p0.start, p0.count)])
    fin1 = (f.at[pl.ds(p1.start, p1.count)], fs.at[pl.ds(p1.start, p1.count)])

    parts, fins = (p0, p1), (fin0, fin1)
    for what, n, *rest in plan_reduce:
        if what == "second":
            parts[n].second_step(*rest, fins[n])
        else:
            getattr(parts[n], what)(*rest)

    for n in range(d.ntp):
        for i in range(d.rd):
            rfs_row = fs[n * d.rd + i : n * d.rd + i + 1, :]
            b1s_tmp = rfs_row
            rfs.at[d.ntp + n][i : i + 1, :] = b1s_tmp

    def final(k, dst_t, src_t, dev_t):
        return [
            remote(f.at[pl.ds(src_t * d.rd, d.rd)], rf.at[dst_t], fin_send.at[0, k], fin_recv.at[0, k], (kv, dev_t)),
            remote(rfs.at[d.ntp + src_t], rfs.at[dst_t], fin_send.at[1, k], fin_recv.at[1, k], (kv, dev_t)),
        ]

    for k in range(1, d.ntp):
        other = lax.rem(tp + k, d.ntp)
        for cp in final(k - 1, tp, other, other):
            cp.start()
            waits.append(cp)
    rf[tp] = f[pl.ds(tp * d.rd, d.rd)]
    rfs[tp] = rfs[d.ntp + tp]

    p0.drain()
    p1.drain()
    for k in range(1, d.ntp):
        source = lax.rem(tp - k + d.ntp, d.ntp)
        for cp in final(k - 1, source, tp, source):
            cp.wait_recv()
    for h in range(d.ntp):
        cols = jnp.transpose(pad8(rfs[h]))
        for i in range(d.rd):
            top_n, total_n, out_n = fresh[h, i, 0], fresh[h, i, 1], stage[h, i]
            top_c, total_c = cols[: d.q, i : i + 1], cols[64 : 64 + d.q, i : i + 1]
            top = jnp.maximum(top_n, top_c)
            a, b = jnp.exp(top_n - top), jnp.exp(top_c - top)
            numer = out_n * a + rf[h, i].astype(F32) * b
            result = (numer / (total_n * a + total_c * b)).astype(BF16)
            for step in range(d.steps):
                out[step, i, pl.ds(h * heads, heads)] = result[step * heads : (step + 1) * heads]

    for cp in waits:
        cp.wait_send()


def make_shards(d):
    order = gather_order(d)
    plan_reduce = reduce_order(d)

    def shards(queries, new_keys, new_values, key_cache, value_cache, context_lengths, piece_slots):
        steps, rd, width = queries.shape
        chunks = d.rows // 128
        vmem = pl.BlockSpec(memory_space=pltpu.VMEM)
        hbm = pl.BlockSpec(memory_space=pl.ANY)
        c0, c1 = d.rows_of[0][1], d.rows_of[1][1]
        n0 = sum(d.hops["y"]) * d.nz + sum(d.hops["z"])
        n1 = sum(d.hops["z"]) * d.ny + sum(d.hops["y"])
        pad = d.slots + 8
        dma = pltpu.SemaphoreType.DMA
        sem = lambda *shape: dma(shape)
        nt = max(d.ntp - 1, 1)
        plan_rows = -(-(7 + 2 * chunks) // 8) * 8
        scratch = [
            pltpu.VMEM((chunks, 128), jnp.int32),
            pltpu.VMEM(queries.shape, BF16),
            pltpu.VMEM(new_keys.shape, BF16),
            pltpu.VMEM(new_values.shape, BF16),
            pltpu.VMEM((d.ntp, rd, d.q, HD), F32),
            pltpu.VMEM((d.ntp, rd, 2, d.q, 128), F32),
            pltpu.VMEM((d.ntp, rd, d.q, HD), BF16),
            pltpu.VMEM(piece_slots.shape, jnp.int32),
            pltpu.VMEM((plan_rows, 128), jnp.int32),
            pltpu.SMEM((plan_rows, 128), jnp.int32),
            pltpu.VMEM((d.rows // 2, d.q, HD), BF16),
            pltpu.VMEM((d.slots, d.q, HD), BF16),
            pltpu.VMEM((d.slots, d.q, HD), BF16),
            pltpu.VMEM(key_cache.shape, BF16),
            pltpu.VMEM(value_cache.shape, BF16),
            pltpu.VMEM((2, pad, d.q, HD), BF16),
            pltpu.VMEM((2, pad, 128), F32),
            pltpu.VMEM((n0, c0, d.q, HD), BF16),
            pltpu.VMEM((n0, c0, 128), F32),
            pltpu.VMEM((n1, c1, d.q, HD), BF16),
            pltpu.VMEM((n1, c1, 128), F32),
            pltpu.VMEM((d.ny * d.nz, c0, d.q, HD), BF16),
            pltpu.VMEM((d.ny * d.nz, c0, 128), F32),
            pltpu.VMEM((d.ny * d.nz, c1, d.q, HD), BF16),
            pltpu.VMEM((d.ny * d.nz, c1, 128), F32),
            pltpu.VMEM((d.rg, d.q, HD), BF16),
            pltpu.VMEM((d.rg, 128), F32),
            pltpu.VMEM((d.ntp, rd, d.q, HD), BF16),
            pltpu.VMEM((2 * d.ntp, rd, 128), F32),
            sem(6), sem(2, 4), sem(nt), sem(nt), sem(len(order) // 2), sem(len(order) // 2), sem(d.slots // 8), sem(d.slots // 8),
            sem(d.slots // 8 + 1), sem(d.slots // 8 + 1), sem(2, n0), sem(2, n0), sem(2, n1), sem(2, n1), sem(2, nt), sem(2, nt),
        ]
        result = pl.pallas_call(
            functools.partial(main_kernel, d, order, plan_reduce),
            out_shape=pltpu.VMEM((steps, rd, width // HD, HD), BF16),
            in_specs=[hbm] * 7,
            out_specs=vmem,
            scratch_shapes=scratch,
            compiler_params=pltpu.CompilerParams(
                collective_id=0, has_side_effects=True, vmem_limit_bytes=56 * 1024 * 1024
            ),
        )(piece_slots, context_lengths.reshape(chunks, 128), queries, new_keys, new_values, key_cache, value_cache)
        return result.reshape(steps, rd, width)

    return shards


def solution(mesh):
    d = Dims(4, 8, 4, 2, 40, 256, 3, 2, 8)
    return build(mesh, d)


def build(mesh, d):
    placed = (
        P(None, ("kv", "tp"), None),
        P(None, ("kv", "tp"), None),
        P(None, ("kv", "tp"), None),
        P("kv", None, "tp"),
        P("kv", None, "tp"),
        P(),
        P(),
    )
    return jax.shard_map(
        make_shards(d),
        mesh=mesh,
        in_specs=placed,
        out_specs=P(None, ("kv", "tp"), None),
        check_vma=False,
    )
```

```python
import functools
import math

import jax
import jax.numpy as jnp
from jax import lax
from jax.experimental import pallas as pl
from jax.experimental.pallas import tpu as pltpu
from jax.sharding import PartitionSpec as P

HD = 128
NEG = -1e30
MESH = pl.DeviceIdType.MESH
F32 = jnp.float32
BF16 = jnp.bfloat16


class Dims:
    def __init__(self, ny, nz, ntp, rows_dev, slots, slot_len, steps, kv_local, group):
        self.ny, self.nz, self.ntp, self.rd = ny, nz, ntp, rows_dev
        self.slots, self.slot_len = slots, slot_len
        self.steps, self.kvl, self.group = steps, kv_local, group
        self.rg = rows_dev * ntp
        self.kv = ny * nz * 2
        self.rows = self.kv * self.rg
        self.q = steps * kv_local * group
        self.split = (5 * self.rg) // 8
        self.size = {"y": ny, "z": nz}
        self.hops = {a: (n // 2, n - 1 - n // 2) for a, n in self.size.items()}
        self.rows_of = ((0, self.split), (self.split, self.rg - self.split))


def list_order(tasks, limit, latency, rate=95e3, tick=0.02):
    left = {t[0]: t for t in tasks}
    flying = {"y": [], "z": []}
    arrived, order = {}, []
    now, busy, running = 0.0, 0.0, None
    while left or running:
        if now >= busy - 1e-9:
            if running:
                for msg, axis, size in running[4]:
                    flying[axis].append([msg, size])
                running = None
            ready, urgent = [], set()
            for name, _, waits, before, _, paced, rank in left.values():
                if any(arrived.get(w, 1e9) > now for w in waits):
                    continue
                if any(x in left for x in before):
                    urgent.update(before)
                elif not paced or len(flying[paced]) < limit:
                    ready.append((rank, name))
            ready = [((0.5,) + r[1:] if n in urgent and r[0] > 0.5 else r, n) for r, n in ready]
            if ready:
                name = min(ready)[1]
                running = left.pop(name)
                order.append(name)
                busy = now + running[1]
        for axis, copies in flying.items():
            room = rate * tick
            for c in copies:
                part = min(room, c[1])
                c[1] -= part
                room -= part
                if c[1] <= 1e-9:
                    arrived[c[0]] = now + tick + latency
            flying[axis] = [c for c in copies if c[1] > 1e-9]
        now += tick
    return order


def gather_order(d, limit=2, latency=2.0):
    tasks, depth = [], {}

    def hops(msg):
        return max([1 + hops(c) for c in gather_children(d, msg)], default=0)

    def add(msg):
        for child in gather_children(d, msg):
            part, phase = child[0], child[1]
            axis = "zy"[part] if phase == 1 else "yz"[part]
            size = d.rows_of[part][1] * d.q * HD * 2
            before = [("wait", msg)] if msg else []
            rank = (0, -hops(child), len(tasks))
            tasks.append((("send", child), 0.06, [], before, [(child, axis, size)], axis, rank))
            tasks.append((("wait", child), 0.12, [child], [], [], None, (1, 0, len(tasks))))
            add(child)

    add(None)
    return list_order(tasks, limit, latency)


def gather_children(d, msg):
    out = []
    if msg is None:
        for phase in (1, 2):
            for part in (0, 1):
                axis = "zy"[part] if phase == 1 else "yz"[part]
                for way in (0, 1):
                    if d.hops[axis][way] >= 1:
                        out.append((part, phase, way, 1, 0))
        return out
    part, phase, way, j, oa = msg
    first, second = ("z", "y") if part == 0 else ("y", "z")
    axis = first if phase == 1 else second
    if j < d.hops[axis][way]:
        out.append((part, phase, way, j + 1, oa))
    if phase == 1:
        here = -j if way == 0 else j
        for w2 in (0, 1):
            if d.hops[second][w2] >= 1:
                out.append((part, 2, w2, 1, here))
    return out


def reduce_order(d, limit=2, latency=2.75):
    tasks = []

    def add(name, cost, waits, before, sends, paced, kind, ahead):
        tasks.append((name, cost, waits, before, sends, paced, (kind, -ahead, len(tasks))))

    for n, (first, second) in enumerate((("y", "z"), ("z", "y"))):
        h1, h2, lanes = d.hops[first], d.hops[second], d.size[second]
        size = d.rows_of[n][1] * (d.q * HD * 2 + 512)
        for k in range(lanes):
            last = k == lanes - 1
            tail = 0 if last else h2[k % 2] - k // 2
            for w in (0, 1):
                if not h1[w]:
                    continue
                go = [((n, 1, w, 1, k), first, size)]
                add(("launch", n, w, k), 0.08, [], [], go, first, 1, h1[w] + tail)
                for j in range(1, h1[w]):
                    ahead = h1[w] - j + tail
                    pre = ("prebuild", n, w, j, k)
                    add(pre, 0.06, [], [], [], None, 2, ahead)
                    go = [((n, 1, w, j + 1, k), first, size)]
                    add(("relay", n, w, j, k), 0.22, [(n, 1, w, j, k)], [pre], go, None, 0, ahead)
            waits = [(n, 1, w, h1[w], k) for w in (0, 1) if h1[w]]
            if last:
                waits += [(n, 2, w, h2[w]) for w in (0, 1) if h2[w]]
            elif k >= 2:
                waits.append((n, 2, k % 2, k // 2))
            pre = ("build", n, 0, k)
            add(pre, 0.06, [], [], [], None, 2, tail)
            go = [] if last else [((n, 2, k % 2, k // 2 + 1), second, size)]
            add(("second", n, k), 0.28, waits, [pre], go, None, 0, tail)
    return list_order(tasks, limit, latency)


def iota(shape, dim):
    return lax.broadcasted_iota(jnp.int32, shape, dim)


def slot_plan(d, kv, ps, ctx, out, pieces):
    partner = kv + 1 - 2 * lax.rem(kv, 2)
    core = lax.rem(kv, 2)
    chunks = d.rows // 128
    eye = iota((128, 128), 0) == iota((128, 128), 1)
    lane = iota((128, 128), 1)
    row_in = iota((128, 128), 0)

    def to_col(row):
        return jnp.sum(jnp.where(eye, jnp.broadcast_to(row, (128, 128)), 0), axis=1, keepdims=True)

    def to_row(col):
        return jnp.sum(jnp.where(eye, jnp.broadcast_to(col, (128, 128)), 0), axis=0, keepdims=True)

    zero = jnp.zeros((1, 128), jnp.int32)
    base = [jnp.zeros((1, 1), jnp.int32) for _ in (0, 1)]
    acc = [[zero, zero, zero] for _ in (0, 1)]
    held = {}

    def piece(side, c):
        if side == 0:
            for n, owner in enumerate((kv, partner)):
                local = ps[c * 128 : (c + 1) * 128, :] - owner * d.slots
                hit = (local >= 0) & (local < d.slots)
                many = jnp.sum(hit.astype(jnp.int32), axis=1, keepdims=True)
                before = jnp.sum(jnp.where(row_in < lane, many, 0), axis=0, keepdims=True)
                start = to_col(before + base[n])
                last = jnp.where(many > 0, jnp.clip(start + many - 1, 0, d.slots), d.slots)
                out[5 + n * chunks + c : 6 + n * chunks + c, :] = to_row(last)
                base[n] = base[n] + jnp.sum(many, axis=0, keepdims=True)
                held[n] = (local, hit, many, start, last)
        local, hit, many, start, _ = held[side]
        elsewhere = held[1 - side][4]
        if side == 0:
            length = to_col(ctx[c : c + 1, :])
            left = jnp.clip(length - lane * d.slot_len, 0, d.slot_len)
            far = 1 << 30
            code = jnp.where(hit, lane * 32768 + local * 512 + left, far)
        for k in range(3):
            at = (lane == start + k) & (many > k)
            acc[side][1] += jnp.sum(jnp.where(at, row_in + c * 128, 0), axis=0, keepdims=True)
            acc[side][2] += jnp.sum(jnp.where(at, elsewhere, 0), axis=0, keepdims=True)
            if side == 0:
                first = jnp.min(code, axis=1, keepdims=True)
                code = jnp.where(code == first, far, code)
                acc[side][0] += jnp.sum(jnp.where(at, lax.rem(first, 32768), 0), axis=0, keepdims=True)

    def finish():
        for side in (0, 1):
            acc_val, acc_row, other = acc[side]
            out[5 + 2 * chunks + side : 6 + 2 * chunks + side, :] = jnp.clip(other, 0, d.slots)
            mine = lax.rem(acc_row // d.rg, 2) == core
            place = (acc_row // (2 * d.rg)) * d.rg + lax.rem(acc_row, d.rg)
            place = jnp.clip(place, 0, d.rows // 2 - 1)
            if side == 0:
                same = (iota((1, 128), 1) > 0) & (pltpu.roll(acc_row, 1, 1) == acc_row)
                out[0:1, :] = jnp.where(mine, place, -1)
                out[1:2, :] = jnp.clip(acc_val // 512, 0, d.slots - 1)
                out[2:3, :] = lax.rem(acc_val, 512)
                out[3:4, :] = jnp.where(same, 1, 0)
            else:
                out[4:5, :] = jnp.where(mine, place, 0)

    for c in range(chunks):
        for side in (0, 1):
            pieces.append(functools.partial(piece, side, c))
    pieces.append(finish)


def main_kernel(
    d, order, plan_reduce, ps, ctx_in, q_in, nk_in, nv_in, kc, vc, out,
    ctx, q_raw, nk, nv, stage, fresh, qx, psv, planv, meta, g, qp, qs, kb, vb, o, t, r0, r0s, r1, r1s, d0, d0s, d1, d1s, f, fs, rf, rfs,
    io_sem, kv_sem, tp_send, tp_recv, ag_send, ag_recv, fw_send, fw_recv, ex_send, ex_recv,
    s0_send, s0_recv, s1_send, s1_recv, fin_send, fin_recv,
):
    kv = lax.axis_index("kv")
    tp = lax.axis_index("tp")
    core = lax.rem(kv, 2)
    sgn = 2 * core - 1
    chip = kv // 2
    pos = {"y": chip // d.nz, "z": lax.rem(chip, d.nz)}

    near = {}

    def coord(axis, k):
        n = d.size[axis]
        if (axis, k) not in near:
            near[axis, k] = lax.rem(pos[axis] + sgn * k + n, n)
        return near[axis, k]

    def chip_at(oy, oz):
        return coord("y", oy) * d.nz + coord("z", oz)

    def kv_at(oy, oz):
        return chip_at(oy, oz) * 2 + core

    def neighbour(axis, step):
        return (kv_at(step, 0) if axis == "y" else kv_at(0, step), tp)

    partner = (kv + 1 - 2 * core, tp)

    def remote(src, dst, ss, rs, dev):
        return pltpu.make_async_remote_copy(
            src_ref=src, dst_ref=dst, send_sem=ss, recv_sem=rs, device_id=dev, device_id_type=MESH
        )

    chunks = d.rows // 128

    q_copy = pltpu.make_async_copy(q_in, q_raw, io_sem.at[2])
    q_copy.start()
    friends = [partner]
    for axis in ("y", "z"):
        for way in (0, 1):
            if d.hops[axis][way]:
                friends.append(neighbour(axis, 1 - 2 * way))
    for k in range(1, d.ntp):
        friends.append((kv, lax.rem(tp + k, d.ntp)))
    barrier = pltpu.get_barrier_semaphore()
    for dev in friends:
        pl.semaphore_signal(barrier, inc=1, device_id=dev, device_id_type=MESH)

    new_copies = [
        pltpu.make_async_copy(src, dst, io_sem.at[n])
        for n, (src, dst) in enumerate(((nk_in, nk), (nv_in, nv), (ctx_in, ctx)), 3)
    ]
    for cp in new_copies:
        cp.start()
    ps_copy = pltpu.make_async_copy(ps, psv, io_sem.at[0])
    ps_copy.start()

    q_copy.wait()
    heads = d.kvl * d.group
    for step in range(d.steps):
        q_step = q_raw[step].astype(F32)
        for h in range(d.ntp):
            for i in range(d.rd):
                for j in range(heads):
                    at = (h * heads + j) * HD
                    stage[h, i, pl.ds(step * heads + j, 1), :] = q_step[i : i + 1, at : at + HD]
    qx[...] = stage[...].astype(BF16)
    pl.semaphore_wait(barrier, len(friends))

    waits = []

    own = chip * d.rg
    tp_copies = []
    for k in range(1, d.ntp):
        other = lax.rem(tp + k, d.ntp)
        cp = remote(
            qx.at[other], g.at[pl.ds(own + tp * d.rd, d.rd)], tp_send.at[k - 1], tp_recv.at[k - 1], (kv, other)
        )
        cp.start()
        waits.append(cp)

    parts_kv = kv_sem.shape[1]
    per = d.slots // parts_kv
    kv_copies = []
    for n in range(parts_kv):
        for which, (src, dst) in enumerate(((kc, kb), (vc, vb))):
            cp = pltpu.make_async_copy(
                src.at[pl.ds(n * per, per)], dst.at[pl.ds(n * per, per)], kv_sem.at[which, n]
            )
            cp.start()
            kv_copies.append(cp)

    g[pl.ds(own + tp * d.rd, d.rd)] = qx[tp]
    for k in range(1, d.ntp):
        source = lax.rem(tp - k + d.ntp, d.ntp)
        remote(
            qx.at[tp], g.at[pl.ds(own + source * d.rd, d.rd)], tp_send.at[k - 1], tp_recv.at[k - 1], (kv, source)
        ).wait_recv()

    number = {msg: n for n, msg in enumerate(msg for what, msg in order if what == "send")}

    def place(msg, back):
        part, phase, way, j, oa = msg
        turn = 1 if way == 0 else -1
        steps = j - 1 if back else j
        o1 = -turn * steps if phase == 1 else oa
        o2 = 0 if phase == 1 else -turn * steps
        oz, oy = (o1, o2) if part == 0 else (o2, o1)
        start, count = d.rows_of[part]
        return g.at[pl.ds(chip_at(oy, oz) * d.rg + start, count)]

    def ship(msg):
        part, phase, way, j, oa = msg
        axis = "zy"[part] if phase == 1 else "yz"[part]
        n = number[msg]
        src = place(msg, True)
        cp = remote(src, src, ag_send.at[n], ag_recv.at[n], neighbour(axis, 1 - 2 * way))
        cp.start()
        waits.append(cp)

    ps_copy.wait()
    new_copies.pop().wait()
    pieces = []
    slot_plan(d, kv, psv, ctx, planv, pieces)
    plan_copy = pltpu.make_async_copy(planv, meta, io_sem.at[1])
    for place_in, (what, msg) in enumerate(order):
        if what == "send":
            ship(msg)
            continue
        n = number[msg]
        landed = place(msg, False)
        remote(landed, landed, ag_send.at[n], ag_recv.at[n], partner).wait_recv()
        if place_in >= 16 and pieces:
            pieces.pop(0)()
            if not pieces:
                plan_copy.start()
    if pieces:
        while pieces:
            pieces.pop(0)()
        plan_copy.start()
    plan_copy.wait()

    unroll = 8

    def chunk(src, dst, send, recv, n):
        at = pl.ds(n * unroll, unroll)
        return remote(src.at[at], dst.at[at], send.at[n], recv.at[n], partner)

    def pick(n, c):
        for u in range(unroll):
            qs[n * unroll + u] = g[meta[4, n * unroll + u]]
        chunk(qs, qp, fw_send, fw_recv, n).start()
        return c

    chunks_of_slots = d.slots // unroll
    lax.fori_loop(0, chunks_of_slots, pick, 0)
    for copy in kv_copies + new_copies:
        copy.wait()
    for other in waits:
        other.wait_send()
    waits.clear()

    head = lax.rem(iota((d.q, 128), 0) // d.group, d.kvl)
    head_masks = [(head == k).astype(F32).astype(BF16) for k in range(d.kvl)]
    lane128 = iota((d.q, 128), 1)
    lane_slot = iota((d.q, d.slot_len), 1)
    scale = 1.0 / math.sqrt(HD)

    def attend_many(it, carry):
        chunk(qs, qp, fw_send, fw_recv, it).wait_recv()
        m_p, l_p, o_p, mc, lc = carry
        at = [it * unroll + u for u in range(unroll)]
        rows = [meta[0, i] for i in at]
        q1 = [jnp.where(row >= 0, g[jnp.maximum(row, 0)], qp[i]) for row, i in zip(rows, at)]
        q2 = [jnp.concatenate([q * mask for mask in head_masks], axis=1) for q in q1]
        slots = [meta[1, i] for i in at]
        score = [
            lax.dot_general(q, kb[slot], (((1,), (1,)), ((), ())), preferred_element_type=F32)
            for q, slot in zip(q2, slots)
        ]
        score = [jnp.where(lane_slot < meta[2, i], x * scale, NEG) for x, i in zip(score, at)]
        tops = [jnp.max(x, axis=1, keepdims=True) for x in score]
        ps = [jnp.exp(x - m) for x, m in zip(score, tops)]
        sums = [jnp.dot(p.astype(BF16), vb[slot], preferred_element_type=F32) for p, slot in zip(ps, slots)]
        totals = [jnp.sum(p, axis=1, keepdims=True) for p in ps]
        accs = []
        for u, i in enumerate(at):
            o_s = sums[u][:, :HD]
            for k in range(1, d.kvl):
                o_s = jnp.where(head == k, sums[u][:, k * HD : (k + 1) * HD], o_s)
            m_q = jnp.where(meta[3, i] > 0, m_p, NEG)
            m = jnp.maximum(m_q, tops[u])
            a, b = jnp.exp(m_q - m), jnp.exp(tops[u] - m)
            l_p = l_p * a + totals[u] * b
            o_p = o_p * a + o_s * b
            m_p = m
            accs.append(o_p.astype(BF16))
            mc = jnp.where(lane128 == i, m_p, mc)
            lc = jnp.where(lane128 == i, l_p, lc)
        for u, i in enumerate(at):
            o[0, i] = accs[u]
        chunk(o.at[0], o.at[1], ex_send, ex_recv, it).start()
        return m_p, l_p, o_p, mc, lc

    zero_col = jnp.zeros((d.q, 1), F32)
    zero = jnp.zeros((d.q, 128), F32)
    _, _, _, mc, lc = lax.fori_loop(
        0, d.slots // unroll, attend_many, (zero_col, zero_col, zero, jnp.full((d.q, 128), NEG, F32), zero)
    )
    pad = jnp.zeros((128 - d.q, 128), F32)
    mt = jnp.transpose(jnp.concatenate([mc, pad], axis=0))
    lt = jnp.transpose(jnp.concatenate([lc, pad], axis=0))
    table = jnp.where(iota((128, 128), 1) < 64, mt, pltpu.roll(lt, 64, 1))
    spare = t.shape[1] - d.slots
    t[0] = table[: t.shape[1]]
    nobody = jnp.where(iota((spare, 128), 1) < 64, NEG, 0.0)
    for side in (0, 1):
        t[side, pl.ds(d.slots, spare)] = nobody
        o[side, d.slots] = jnp.zeros((d.q, 128), BF16)

    table_copy = remote(
        t.at[0, pl.ds(0, d.slots)],
        t.at[1, pl.ds(0, d.slots)],
        ex_send.at[chunks_of_slots],
        ex_recv.at[chunks_of_slots],
        partner,
    )
    table_copy.start()

    nkf = [nk[u].astype(F32) for u in range(d.steps)]
    nvf = [nv[u].astype(F32) for u in range(d.steps)]
    for h in range(d.ntp):
        for i in range(d.rd):
            tops, totals, outs = [], [], []
            qf = qx[h, i].astype(F32)
            for step in range(d.steps):
                for k in range(d.kvl):
                    at = (step * d.kvl + k) * d.group
                    kk = h * d.kvl + k
                    q_k = qf[at : at + d.group]
                    scores = [
                        jnp.sum(q_k * nkf[u][i : i + 1, kk * HD : (kk + 1) * HD], axis=1, keepdims=True) * scale
                        for u in range(step + 1)
                    ]
                    top = functools.reduce(jnp.maximum, scores)
                    ws = [jnp.exp(x - top) for x in scores]
                    tops.append(top)
                    totals.append(sum(ws))
                    outs.append(sum(w * nvf[u][i : i + 1, kk * HD : (kk + 1) * HD] for u, w in enumerate(ws)))
            for n, x in enumerate((tops, totals)):
                fresh[h, i, n] = jnp.broadcast_to(jnp.concatenate(x, axis=0), (d.q, 128))
            stage[h, i] = jnp.concatenate(outs, axis=0)

    def exchanged(n, c):
        chunk(qs, qp, fw_send, fw_recv, n).wait_send()
        chunk(o.at[0], o.at[1], ex_send, ex_recv, n).wait()
        return c

    lax.fori_loop(0, chunks_of_slots, exchanged, 0)
    table_copy.wait()

    lane8 = iota((8, 128), 1)
    factors, tiles = [], {}
    for side in (0, 1):
        for at in range(0, d.slots, 8):
            ids = [meta[5 + 2 * chunks + side, at + u] for u in range(8)]
            theirs = jnp.concatenate([t[1 - side, pl.ds(i, 1), :] for i in ids], axis=0)
            mine = t[side, pl.ds(at, 8), :]
            top = jnp.maximum(mine, theirs)
            factor = jnp.exp(mine - top)
            factors.append(factor)
            tiles[side, at] = jnp.where(lane8 < 64, top, mine * pltpu.roll(factor, 64, 1))
    cols = jnp.transpose(jnp.concatenate(factors, axis=0))
    for (side, at), tile in tiles.items():
        t[side, pl.ds(at, 8), :] = tile
    for side in (0, 1):
        for i in range(d.slots):
            n = side * d.slots + i
            o[side, i] = (o[side, i].astype(F32) * cols[: d.q, n : n + 1]).astype(BF16)

    def pad8(x):
        if x.shape[0] == 8:
            return x
        return jnp.concatenate([x, jnp.zeros((8 - x.shape[0], 128), F32)], axis=0)

    def prepare(stats, count):
        top = functools.reduce(jnp.maximum, stats)
        es = [jnp.exp(st - top) for st in stats]
        total = sum(e * pltpu.roll(st, 64, 1) for e, st in zip(es, stats))
        tile = jnp.where(lane8 < 64, top, pltpu.roll(total, 64, 1))[:count]
        return tile, jnp.transpose(jnp.concatenate(es, axis=0))

    def apply(tile, cols, rows, many, count, out_d, out_s):
        out_s[...] = tile
        for r in range(count):
            acc = None
            for k in range(many):
                term = rows(k, r).astype(F32) * cols[: d.q, k * 8 + r : k * 8 + r + 1]
                acc = term if acc is None else acc + term
            out_d[r] = acc.astype(BF16)

    def merge(jobs, count):
        tiles = [[pad8(x[1][...]) for x in ins] for ins, _ in jobs]
        ready = [prepare(stats, count) for stats in tiles]
        for (ins, dst), (tile, cols) in zip(jobs, ready):
            apply(tile, cols, lambda k, r: ins[k][0][r], len(ins), count, *dst)

    per_row = 128 // d.rg

    class Part:
        def __init__(self, first, second, rows, recv, recv_s, mine, mine_s, send_sem, recv_sem):
            self.first, self.second = first, second
            self.start, self.count = rows
            self.recv, self.recv_s, self.mine, self.mine_s = recv, recv_s, mine, mine_s
            self.send_sem, self.recv_sem = send_sem, recv_sem
            self.n1, self.lanes = d.size[first], d.size[second]
            self.h1, self.h2 = d.hops[first], d.hops[second]
            self.phase2 = sum(self.h1) * self.lanes
            self.to = {
                (axis, way): neighbour(axis, 1 - 2 * way) for axis in (first, second) for way in (0, 1)
            }

        def id1(self, way, j, lane):
            return (way * self.h1[0] + j - 1) * self.lanes + lane

        def id2(self, way, j):
            return self.phase2 + way * self.h2[0] + j - 1

        def bufs(self, n):
            return self.recv.at[n], self.recv_s.at[n]

        def chip_sum(self, o1, lane):
            n = (o1 % self.n1) * self.lanes + lane
            return self.mine.at[n], self.mine_s.at[n]

        def copies(self, src, n, axis, way):
            return [
                remote(a, b, self.send_sem.at[k, n], self.recv_sem.at[k, n], self.to[axis, way])
                for k, (a, b) in enumerate(zip(src, self.bufs(n)))
            ]

        def send(self, src, n, axis, way):
            for cp in self.copies(src, n, axis, way):
                cp.start()

        def wait(self, n):
            for cp in self.copies(self.bufs(n), n, self.first, 0):
                cp.wait_recv()

        def wait_sent(self, n):
            for cp in self.copies(self.bufs(n), n, self.first, 0):
                cp.wait_send()

        def lane(self, k):
            return (self.h2[0] + ((k + 1) // 2) * (1 if k % 2 else -1)) % self.lanes

        def build(self, o1, k):
            lane = self.lane(k)
            oy, oz = (o1, lane) if self.first == "y" else (lane, o1)
            kv_to = kv_at(oy, oz)
            line, col = lax.div(kv_to, per_row), lax.rem(kv_to, per_row) * d.rg + self.start
            ids = [
                [meta[5 + side * chunks + line, col + r] for r in range(self.count)] for side in (0, 1)
            ]
            stats = [
                jnp.concatenate([t[side, pl.ds(i, 1), :] for i in ids[side]], axis=0) for side in (0, 1)
            ]
            dst, dst_s = self.chip_sum(o1, lane)
            dst_s[...] = jnp.where(
                lane8[: self.count] < 64, jnp.maximum(stats[0], stats[1]), stats[0] + stats[1]
            )
            for r in range(self.count):
                dst[r] = o[0, ids[0][r]] + o[1, ids[1][r]]

        def launch(self, way, k):
            o1 = (1 - 2 * way) * self.h1[way]
            self.build(o1, k)
            lane = self.lane(k)
            self.send(self.chip_sum(o1, lane), self.id1(way, 1, lane), self.first, way)

        def prebuild(self, way, j, k):
            self.build((1 - 2 * way) * (self.h1[way] - j), k)

        def relay(self, way, j, k):
            lane = self.lane(k)
            n = self.id1(way, j, lane)
            self.wait(n)
            left = (1 - 2 * way) * (self.h1[way] - j)
            src = self.bufs(n)
            merge([([src, self.chip_sum(left, lane)], src)], self.count)
            self.send(src, self.id1(way, j + 1, lane), self.first, way)

        def second_step(self, k, result):
            lane = self.lane(k)
            ids = [self.id1(way, self.h1[way], lane) for way in (0, 1) if self.h1[way]]
            last = k == self.lanes - 1
            if last:
                ids += [self.id2(way, self.h2[way]) for way in (0, 1) if self.h2[way]]
            elif k >= 2:
                ids.append(self.id2(k % 2, k // 2))
            for n in ids:
                self.wait(n)
            ins = [self.bufs(n) for n in ids] + [self.chip_sum(0, lane)]
            dst = result if last else ins[0]
            merge([(ins, dst)], self.count)
            if not last:
                self.send(dst, self.id2(k % 2, k // 2 + 1), self.second, k % 2)

        def drain(self):
            def body(n, c):
                self.wait_sent(n)
                return c

            lax.fori_loop(0, self.phase2 + sum(self.h2), body, 0)

    p0 = Part("y", "z", d.rows_of[0], r0, r0s, d0, d0s, s0_send, s0_recv)
    p1 = Part("z", "y", d.rows_of[1], r1, r1s, d1, d1s, s1_send, s1_recv)
    fin0 = (f.at[pl.ds(p0.start, p0.count)], fs.at[pl.ds(p0.start, p0.count)])
    fin1 = (f.at[pl.ds(p1.start, p1.count)], fs.at[pl.ds(p1.start, p1.count)])

    parts, fins = (p0, p1), (fin0, fin1)
    for what, n, *rest in plan_reduce:
        if what == "second":
            parts[n].second_step(*rest, fins[n])
        else:
            getattr(parts[n], what)(*rest)

    for n in range(d.ntp):
        for i in range(d.rd):
            rfs_row = fs[n * d.rd + i : n * d.rd + i + 1, :]
            b1s_tmp = rfs_row
            rfs.at[d.ntp + n][i : i + 1, :] = b1s_tmp

    def final(k, dst_t, src_t, dev_t):
        return [
            remote(f.at[pl.ds(src_t * d.rd, d.rd)], rf.at[dst_t], fin_send.at[0, k], fin_recv.at[0, k], (kv, dev_t)),
            remote(rfs.at[d.ntp + src_t], rfs.at[dst_t], fin_send.at[1, k], fin_recv.at[1, k], (kv, dev_t)),
        ]

    for k in range(1, d.ntp):
        other = lax.rem(tp + k, d.ntp)
        for cp in final(k - 1, tp, other, other):
            cp.start()
            waits.append(cp)
    rf[tp] = f[pl.ds(tp * d.rd, d.rd)]
    rfs[tp] = rfs[d.ntp + tp]

    p0.drain()
    p1.drain()
    for k in range(1, d.ntp):
        source = lax.rem(tp - k + d.ntp, d.ntp)
        for cp in final(k - 1, source, tp, source):
            cp.wait_recv()
    for h in range(d.ntp):
        cols = jnp.transpose(pad8(rfs[h]))
        for i in range(d.rd):
            top_n, total_n, out_n = fresh[h, i, 0], fresh[h, i, 1], stage[h, i]
            top_c, total_c = cols[: d.q, i : i + 1], cols[64 : 64 + d.q, i : i + 1]
            top = jnp.maximum(top_n, top_c)
            a, b = jnp.exp(top_n - top), jnp.exp(top_c - top)
            numer = out_n * a + rf[h, i].astype(F32) * b
            result = (numer / (total_n * a + total_c * b)).astype(BF16)
            for step in range(d.steps):
                out[step, i, pl.ds(h * heads, heads)] = result[step * heads : (step + 1) * heads]

    for cp in waits:
        cp.wait_send()


def make_shards(d):
    order = gather_order(d)
    plan_reduce = reduce_order(d)

    def shards(queries, new_keys, new_values, key_cache, value_cache, context_lengths, piece_slots):
        steps, rd, width = queries.shape
        chunks = d.rows // 128
        vmem = pl.BlockSpec(memory_space=pltpu.VMEM)
        hbm = pl.BlockSpec(memory_space=pl.ANY)
        c0, c1 = d.rows_of[0][1], d.rows_of[1][1]
        n0 = sum(d.hops["y"]) * d.nz + sum(d.hops["z"])
        n1 = sum(d.hops["z"]) * d.ny + sum(d.hops["y"])
        pad = d.slots + 8
        dma = pltpu.SemaphoreType.DMA
        sem = lambda *shape: dma(shape)
        nt = max(d.ntp - 1, 1)
        plan_rows = -(-(7 + 2 * chunks) // 8) * 8
        scratch = [
            pltpu.VMEM((chunks, 128), jnp.int32),
            pltpu.VMEM(queries.shape, BF16),
            pltpu.VMEM(new_keys.shape, BF16),
            pltpu.VMEM(new_values.shape, BF16),
            pltpu.VMEM((d.ntp, rd, d.q, HD), F32),
            pltpu.VMEM((d.ntp, rd, 2, d.q, 128), F32),
            pltpu.VMEM((d.ntp, rd, d.q, HD), BF16),
            pltpu.VMEM(piece_slots.shape, jnp.int32),
            pltpu.VMEM((plan_rows, 128), jnp.int32),
            pltpu.SMEM((plan_rows, 128), jnp.int32),
            pltpu.VMEM((d.rows // 2, d.q, HD), BF16),
            pltpu.VMEM((d.slots, d.q, HD), BF16),
            pltpu.VMEM((d.slots, d.q, HD), BF16),
            pltpu.VMEM(key_cache.shape, BF16),
            pltpu.VMEM(value_cache.shape, BF16),
            pltpu.VMEM((2, pad, d.q, HD), BF16),
            pltpu.VMEM((2, pad, 128), F32),
            pltpu.VMEM((n0, c0, d.q, HD), BF16),
            pltpu.VMEM((n0, c0, 128), F32),
            pltpu.VMEM((n1, c1, d.q, HD), BF16),
            pltpu.VMEM((n1, c1, 128), F32),
            pltpu.VMEM((d.ny * d.nz, c0, d.q, HD), BF16),
            pltpu.VMEM((d.ny * d.nz, c0, 128), F32),
            pltpu.VMEM((d.ny * d.nz, c1, d.q, HD), BF16),
            pltpu.VMEM((d.ny * d.nz, c1, 128), F32),
            pltpu.VMEM((d.rg, d.q, HD), BF16),
            pltpu.VMEM((d.rg, 128), F32),
            pltpu.VMEM((d.ntp, rd, d.q, HD), BF16),
            pltpu.VMEM((2 * d.ntp, rd, 128), F32),
            sem(6), sem(2, 4), sem(nt), sem(nt), sem(len(order) // 2), sem(len(order) // 2), sem(d.slots // 8), sem(d.slots // 8),
            sem(d.slots // 8 + 1), sem(d.slots // 8 + 1), sem(2, n0), sem(2, n0), sem(2, n1), sem(2, n1), sem(2, nt), sem(2, nt),
        ]
        result = pl.pallas_call(
            functools.partial(main_kernel, d, order, plan_reduce),
            out_shape=pltpu.VMEM((steps, rd, width // HD, HD), BF16),
            in_specs=[hbm] * 7,
            out_specs=vmem,
            scratch_shapes=scratch,
            compiler_params=pltpu.CompilerParams(
                collective_id=0, has_side_effects=True, vmem_limit_bytes=56 * 1024 * 1024
            ),
        )(piece_slots, context_lengths.reshape(chunks, 128), queries, new_keys, new_values, key_cache, value_cache)
        return result.reshape(steps, rd, width)

    return shards


def solution(mesh):
    d = Dims(4, 8, 4, 2, 40, 256, 3, 2, 8)
    return build(mesh, d)


def build(mesh, d):
    placed = (
        P(None, ("kv", "tp"), None),
        P(None, ("kv", "tp"), None),
        P(None, ("kv", "tp"), None),
        P("kv", None, "tp"),
        P("kv", None, "tp"),
        P(),
        P(),
    )
    return jax.shard_map(
        make_shards(d),
        mesh=mesh,
        in_specs=placed,
        out_specs=P(None, ("kv", "tp"), None),
        check_vma=False,
    )
```

```python
import functools
import math

import jax
import jax.numpy as jnp
from jax import lax
from jax.experimental import pallas as pl
from jax.experimental.pallas import tpu as pltpu
from jax.sharding import PartitionSpec as P

HD = 128
NEG = -1e30
MESH = pl.DeviceIdType.MESH
F32 = jnp.float32
BF16 = jnp.bfloat16


class Dims:
    def __init__(self, ny, nz, ntp, rows_dev, slots, slot_len, steps, kv_local, group):
        self.ny, self.nz, self.ntp, self.rd = ny, nz, ntp, rows_dev
        self.slots, self.slot_len = slots, slot_len
        self.steps, self.kvl, self.group = steps, kv_local, group
        self.rg = rows_dev * ntp
        self.kv = ny * nz * 2
        self.rows = self.kv * self.rg
        self.q = steps * kv_local * group
        self.split = (5 * self.rg) // 8
        self.size = {"y": ny, "z": nz}
        self.hops = {a: (n // 2, n - 1 - n // 2) for a, n in self.size.items()}
        self.rows_of = ((0, self.split), (self.split, self.rg - self.split))


def list_order(tasks, limit, latency, rate=95e3, tick=0.02):
    left = {t[0]: t for t in tasks}
    flying = {"y": [], "z": []}
    arrived, order = {}, []
    now, busy, running = 0.0, 0.0, None
    while left or running:
        if now >= busy - 1e-9:
            if running:
                for msg, axis, size in running[4]:
                    flying[axis].append([msg, size])
                running = None
            ready, urgent = [], set()
            for name, _, waits, before, _, paced, rank in left.values():
                if any(arrived.get(w, 1e9) > now for w in waits):
                    continue
                if any(x in left for x in before):
                    urgent.update(before)
                elif not paced or len(flying[paced]) < limit:
                    ready.append((rank, name))
            ready = [((0.5,) + r[1:] if n in urgent and r[0] > 0.5 else r, n) for r, n in ready]
            if ready:
                name = min(ready)[1]
                running = left.pop(name)
                order.append(name)
                busy = now + running[1]
        for axis, copies in flying.items():
            room = rate * tick
            for c in copies:
                part = min(room, c[1])
                c[1] -= part
                room -= part
                if c[1] <= 1e-9:
                    arrived[c[0]] = now + tick + latency
            flying[axis] = [c for c in copies if c[1] > 1e-9]
        now += tick
    return order


def gather_order(d, limit=2, latency=2.0):
    tasks, depth = [], {}

    def hops(msg):
        return max([1 + hops(c) for c in gather_children(d, msg)], default=0)

    def add(msg):
        for child in gather_children(d, msg):
            part, phase = child[0], child[1]
            axis = "zy"[part] if phase == 1 else "yz"[part]
            size = d.rows_of[part][1] * d.q * HD * 2
            before = [("wait", msg)] if msg else []
            rank = (0, -hops(child), len(tasks))
            tasks.append((("send", child), 0.06, [], before, [(child, axis, size)], axis, rank))
            tasks.append((("wait", child), 0.12, [child], [], [], None, (1, 0, len(tasks))))
            add(child)

    add(None)
    return list_order(tasks, limit, latency)


def gather_children(d, msg):
    out = []
    if msg is None:
        for phase in (1, 2):
            for part in (0, 1):
                axis = "zy"[part] if phase == 1 else "yz"[part]
                for way in (0, 1):
                    if d.hops[axis][way] >= 1:
                        out.append((part, phase, way, 1, 0))
        return out
    part, phase, way, j, oa = msg
    first, second = ("z", "y") if part == 0 else ("y", "z")
    axis = first if phase == 1 else second
    if j < d.hops[axis][way]:
        out.append((part, phase, way, j + 1, oa))
    if phase == 1:
        here = -j if way == 0 else j
        for w2 in (0, 1):
            if d.hops[second][w2] >= 1:
                out.append((part, 2, w2, 1, here))
    return out


def reduce_order(d, limit=2, latency=2.75):
    tasks = []

    def add(name, cost, waits, before, sends, paced, kind, ahead):
        tasks.append((name, cost, waits, before, sends, paced, (kind, -ahead, len(tasks))))

    for n, (first, second) in enumerate((("y", "z"), ("z", "y"))):
        h1, h2, lanes = d.hops[first], d.hops[second], d.size[second]
        size = d.rows_of[n][1] * (d.q * HD * 2 + 512)
        for k in range(lanes):
            last = k == lanes - 1
            tail = 0 if last else h2[k % 2] - k // 2
            for w in (0, 1):
                if not h1[w]:
                    continue
                go = [((n, 1, w, 1, k), first, size)]
                add(("launch", n, w, k), 0.08, [], [], go, first, 1, h1[w] + tail)
                for j in range(1, h1[w]):
                    ahead = h1[w] - j + tail
                    pre = ("prebuild", n, w, j, k)
                    add(pre, 0.06, [], [], [], None, 2, ahead)
                    go = [((n, 1, w, j + 1, k), first, size)]
                    add(("relay", n, w, j, k), 0.22, [(n, 1, w, j, k)], [pre], go, None, 0, ahead)
            waits = [(n, 1, w, h1[w], k) for w in (0, 1) if h1[w]]
            if last:
                waits += [(n, 2, w, h2[w]) for w in (0, 1) if h2[w]]
            elif k >= 2:
                waits.append((n, 2, k % 2, k // 2))
            pre = ("build", n, 0, k)
            add(pre, 0.06, [], [], [], None, 2, tail)
            go = [] if last else [((n, 2, k % 2, k // 2 + 1), second, size)]
            add(("second", n, k), 0.28, waits, [pre], go, None, 0, tail)
    return list_order(tasks, limit, latency)


def iota(shape, dim):
    return lax.broadcasted_iota(jnp.int32, shape, dim)


def slot_plan(d, kv, ps, ctx, out, pieces):
    partner = kv + 1 - 2 * lax.rem(kv, 2)
    core = lax.rem(kv, 2)
    chunks = d.rows // 128
    eye = iota((128, 128), 0) == iota((128, 128), 1)
    lane = iota((128, 128), 1)
    row_in = iota((128, 128), 0)

    def to_col(row):
        return jnp.sum(jnp.where(eye, jnp.broadcast_to(row, (128, 128)), 0), axis=1, keepdims=True)

    def to_row(col):
        return jnp.sum(jnp.where(eye, jnp.broadcast_to(col, (128, 128)), 0), axis=0, keepdims=True)

    zero = jnp.zeros((1, 128), jnp.int32)
    base = [jnp.zeros((1, 1), jnp.int32) for _ in (0, 1)]
    acc = [[zero, zero, zero] for _ in (0, 1)]
    held = {}

    def piece(side, c):
        if side == 0:
            for n, owner in enumerate((kv, partner)):
                local = ps[c * 128 : (c + 1) * 128, :] - owner * d.slots
                hit = (local >= 0) & (local < d.slots)
                many = jnp.sum(hit.astype(jnp.int32), axis=1, keepdims=True)
                before = jnp.sum(jnp.where(row_in < lane, many, 0), axis=0, keepdims=True)
                start = to_col(before + base[n])
                last = jnp.where(many > 0, jnp.clip(start + many - 1, 0, d.slots), d.slots)
                out[5 + n * chunks + c : 6 + n * chunks + c, :] = to_row(last)
                base[n] = base[n] + jnp.sum(many, axis=0, keepdims=True)
                held[n] = (local, hit, many, start, last)
        local, hit, many, start, _ = held[side]
        elsewhere = held[1 - side][4]
        if side == 0:
            length = to_col(ctx[c : c + 1, :])
            left = jnp.clip(length - lane * d.slot_len, 0, d.slot_len)
            far = 1 << 30
            code = jnp.where(hit, lane * 32768 + local * 512 + left, far)
        for k in range(3):
            at = (lane == start + k) & (many > k)
            acc[side][1] += jnp.sum(jnp.where(at, row_in + c * 128, 0), axis=0, keepdims=True)
            acc[side][2] += jnp.sum(jnp.where(at, elsewhere, 0), axis=0, keepdims=True)
            if side == 0:
                first = jnp.min(code, axis=1, keepdims=True)
                code = jnp.where(code == first, far, code)
                acc[side][0] += jnp.sum(jnp.where(at, lax.rem(first, 32768), 0), axis=0, keepdims=True)

    def finish():
        for side in (0, 1):
            acc_val, acc_row, other = acc[side]
            out[5 + 2 * chunks + side : 6 + 2 * chunks + side, :] = jnp.clip(other, 0, d.slots)
            mine = lax.rem(acc_row // d.rg, 2) == core
            place = (acc_row // (2 * d.rg)) * d.rg + lax.rem(acc_row, d.rg)
            place = jnp.clip(place, 0, d.rows // 2 - 1)
            if side == 0:
                same = (iota((1, 128), 1) > 0) & (pltpu.roll(acc_row, 1, 1) == acc_row)
                out[0:1, :] = jnp.where(mine, place, -1)
                out[1:2, :] = jnp.clip(acc_val // 512, 0, d.slots - 1)
                out[2:3, :] = lax.rem(acc_val, 512)
                out[3:4, :] = jnp.where(same, 1, 0)
            else:
                out[4:5, :] = jnp.where(mine, place, 0)

    for c in range(chunks):
        for side in (0, 1):
            pieces.append(functools.partial(piece, side, c))
    pieces.append(finish)


def main_kernel(
    d, order, plan_reduce, ps, ctx_in, q_in, nk_in, nv_in, kc, vc, out,
    ctx, q_raw, nk, nv, stage, fresh, qx, psv, planv, meta, g, qp, qs, kb, vb, o, t, r0, r0s, r1, r1s, d0, d0s, d1, d1s, f, fs, rf, rfs,
    io_sem, kv_sem, tp_send, tp_recv, ag_send, ag_recv, fw_send, fw_recv, ex_send, ex_recv,
    s0_send, s0_recv, s1_send, s1_recv, fin_send, fin_recv,
):
    kv = lax.axis_index("kv")
    tp = lax.axis_index("tp")
    core = lax.rem(kv, 2)
    sgn = 2 * core - 1
    chip = kv // 2
    pos = {"y": chip // d.nz, "z": lax.rem(chip, d.nz)}

    near = {}

    def coord(axis, k):
        n = d.size[axis]
        if (axis, k) not in near:
            near[axis, k] = lax.rem(pos[axis] + sgn * k + n, n)
        return near[axis, k]

    def chip_at(oy, oz):
        return coord("y", oy) * d.nz + coord("z", oz)

    def kv_at(oy, oz):
        return chip_at(oy, oz) * 2 + core

    def neighbour(axis, step):
        return (kv_at(step, 0) if axis == "y" else kv_at(0, step), tp)

    partner = (kv + 1 - 2 * core, tp)

    def remote(src, dst, ss, rs, dev):
        return pltpu.make_async_remote_copy(
            src_ref=src, dst_ref=dst, send_sem=ss, recv_sem=rs, device_id=dev, device_id_type=MESH
        )

    chunks = d.rows // 128

    q_copy = pltpu.make_async_copy(q_in, q_raw, io_sem.at[2])
    q_copy.start()
    friends = [partner]
    for axis in ("y", "z"):
        for way in (0, 1):
            if d.hops[axis][way]:
                friends.append(neighbour(axis, 1 - 2 * way))
    for k in range(1, d.ntp):
        friends.append((kv, lax.rem(tp + k, d.ntp)))
    barrier = pltpu.get_barrier_semaphore()
    for dev in friends:
        pl.semaphore_signal(barrier, inc=1, device_id=dev, device_id_type=MESH)

    new_copies = [
        pltpu.make_async_copy(src, dst, io_sem.at[n])
        for n, (src, dst) in enumerate(((nk_in, nk), (nv_in, nv), (ctx_in, ctx)), 3)
    ]
    for cp in new_copies:
        cp.start()
    ps_copy = pltpu.make_async_copy(ps, psv, io_sem.at[0])
    ps_copy.start()

    q_copy.wait()
    heads = d.kvl * d.group
    for step in range(d.steps):
        q_step = q_raw[step].astype(F32)
        for h in range(d.ntp):
            for i in range(d.rd):
                for j in range(heads):
                    at = (h * heads + j) * HD
                    stage[h, i, pl.ds(step * heads + j, 1), :] = q_step[i : i + 1, at : at + HD]
    qx[...] = stage[...].astype(BF16)
    pl.semaphore_wait(barrier, len(friends))

    waits = []

    own = chip * d.rg
    tp_copies = []
    for k in range(1, d.ntp):
        other = lax.rem(tp + k, d.ntp)
        cp = remote(
            qx.at[other], g.at[pl.ds(own + tp * d.rd, d.rd)], tp_send.at[k - 1], tp_recv.at[k - 1], (kv, other)
        )
        cp.start()
        waits.append(cp)

    parts_kv = kv_sem.shape[1]
    per = d.slots // parts_kv
    kv_copies = []
    for n in range(parts_kv):
        for which, (src, dst) in enumerate(((kc, kb), (vc, vb))):
            cp = pltpu.make_async_copy(
                src.at[pl.ds(n * per, per)], dst.at[pl.ds(n * per, per)], kv_sem.at[which, n]
            )
            cp.start()
            kv_copies.append(cp)

    g[pl.ds(own + tp * d.rd, d.rd)] = qx[tp]
    for k in range(1, d.ntp):
        source = lax.rem(tp - k + d.ntp, d.ntp)
        remote(
            qx.at[tp], g.at[pl.ds(own + source * d.rd, d.rd)], tp_send.at[k - 1], tp_recv.at[k - 1], (kv, source)
        ).wait_recv()

    number = {msg: n for n, msg in enumerate(msg for what, msg in order if what == "send")}

    def place(msg, back):
        part, phase, way, j, oa = msg
        turn = 1 if way == 0 else -1
        steps = j - 1 if back else j
        o1 = -turn * steps if phase == 1 else oa
        o2 = 0 if phase == 1 else -turn * steps
        oz, oy = (o1, o2) if part == 0 else (o2, o1)
        start, count = d.rows_of[part]
        return g.at[pl.ds(chip_at(oy, oz) * d.rg + start, count)]

    def ship(msg):
        part, phase, way, j, oa = msg
        axis = "zy"[part] if phase == 1 else "yz"[part]
        n = number[msg]
        src = place(msg, True)
        cp = remote(src, src, ag_send.at[n], ag_recv.at[n], neighbour(axis, 1 - 2 * way))
        cp.start()
        waits.append(cp)

    ps_copy.wait()
    new_copies.pop().wait()
    pieces = []
    slot_plan(d, kv, psv, ctx, planv, pieces)
    plan_copy = pltpu.make_async_copy(planv, meta, io_sem.at[1])
    for place_in, (what, msg) in enumerate(order):
        if what == "send":
            ship(msg)
            continue
        n = number[msg]
        landed = place(msg, False)
        remote(landed, landed, ag_send.at[n], ag_recv.at[n], partner).wait_recv()
        if place_in >= 16 and pieces:
            pieces.pop(0)()
            if not pieces:
                plan_copy.start()
    if pieces:
        while pieces:
            pieces.pop(0)()
        plan_copy.start()
    plan_copy.wait()

    unroll = 8

    def chunk(src, dst, send, recv, n):
        at = pl.ds(n * unroll, unroll)
        return remote(src.at[at], dst.at[at], send.at[n], recv.at[n], partner)

    def pick(n, c):
        for u in range(unroll):
            qs[n * unroll + u] = g[meta[4, n * unroll + u]]
        chunk(qs, qp, fw_send, fw_recv, n).start()
        return c

    chunks_of_slots = d.slots // unroll
    lax.fori_loop(0, chunks_of_slots, pick, 0)
    for copy in kv_copies + new_copies:
        copy.wait()
    for other in waits:
        other.wait_send()
    waits.clear()

    head = lax.rem(iota((d.q, 128), 0) // d.group, d.kvl)
    head_masks = [(head == k).astype(F32).astype(BF16) for k in range(d.kvl)]
    lane128 = iota((d.q, 128), 1)
    lane_slot = iota((d.q, d.slot_len), 1)
    scale = 1.0 / math.sqrt(HD)

    batch = 4

    def attend_batch(first, carry):
        m_p, l_p, o_p, mc, lc = carry
        at = [first + u for u in range(batch)]
        rows = [meta[0, i] for i in at]
        q1 = [jnp.where(row >= 0, g[jnp.maximum(row, 0)], qp[i]) for row, i in zip(rows, at)]
        q2 = [jnp.concatenate([q * mask for mask in head_masks], axis=1) for q in q1]
        slots = [meta[1, i] for i in at]
        score = [
            lax.dot_general(q, kb[slot], (((1,), (1,)), ((), ())), preferred_element_type=F32)
            for q, slot in zip(q2, slots)
        ]
        score = [jnp.where(lane_slot < meta[2, i], x * scale, NEG) for x, i in zip(score, at)]
        tops = [jnp.max(x, axis=1, keepdims=True) for x in score]
        ps = [jnp.exp(x - m) for x, m in zip(score, tops)]
        sums = [jnp.dot(p.astype(BF16), vb[slot], preferred_element_type=F32) for p, slot in zip(ps, slots)]
        totals = [jnp.sum(p, axis=1, keepdims=True) for p in ps]
        accs = []
        for u, i in enumerate(at):
            o_s = sums[u][:, :HD]
            for k in range(1, d.kvl):
                o_s = jnp.where(head == k, sums[u][:, k * HD : (k + 1) * HD], o_s)
            m_q = jnp.where(meta[3, i] > 0, m_p, NEG)
            m = jnp.maximum(m_q, tops[u])
            a, b = jnp.exp(m_q - m), jnp.exp(tops[u] - m)
            l_p = l_p * a + totals[u] * b
            o_p = o_p * a + o_s * b
            m_p = m
            accs.append(o_p.astype(BF16))
            mc = jnp.where(lane128 == i, m_p, mc)
            lc = jnp.where(lane128 == i, l_p, lc)
        for u, i in enumerate(at):
            o[0, i] = accs[u]
        return m_p, l_p, o_p, mc, lc

    def attend_many(it, carry):
        chunk(qs, qp, fw_send, fw_recv, it).wait_recv()
        for n in range(unroll // batch):
            carry = attend_batch(it * unroll + n * batch, carry)
        chunk(o.at[0], o.at[1], ex_send, ex_recv, it).start()
        return carry

    zero_col = jnp.zeros((d.q, 1), F32)
    zero = jnp.zeros((d.q, 128), F32)
    _, _, _, mc, lc = lax.fori_loop(
        0, d.slots // unroll, attend_many, (zero_col, zero_col, zero, jnp.full((d.q, 128), NEG, F32), zero)
    )
    pad = jnp.zeros((128 - d.q, 128), F32)
    mt = jnp.transpose(jnp.concatenate([mc, pad], axis=0))
    lt = jnp.transpose(jnp.concatenate([lc, pad], axis=0))
    table = jnp.where(iota((128, 128), 1) < 64, mt, pltpu.roll(lt, 64, 1))
    spare = t.shape[1] - d.slots
    t[0] = table[: t.shape[1]]
    nobody = jnp.where(iota((spare, 128), 1) < 64, NEG, 0.0)
    for side in (0, 1):
        t[side, pl.ds(d.slots, spare)] = nobody
        o[side, d.slots] = jnp.zeros((d.q, 128), BF16)

    table_copy = remote(
        t.at[0, pl.ds(0, d.slots)],
        t.at[1, pl.ds(0, d.slots)],
        ex_send.at[chunks_of_slots],
        ex_recv.at[chunks_of_slots],
        partner,
    )
    table_copy.start()

    nkf = [nk[u].astype(F32) for u in range(d.steps)]
    nvf = [nv[u].astype(F32) for u in range(d.steps)]
    for h in range(d.ntp):
        for i in range(d.rd):
            tops, totals, outs = [], [], []
            qf = qx[h, i].astype(F32)
            for step in range(d.steps):
                for k in range(d.kvl):
                    at = (step * d.kvl + k) * d.group
                    kk = h * d.kvl + k
                    q_k = qf[at : at + d.group]
                    scores = [
                        jnp.sum(q_k * nkf[u][i : i + 1, kk * HD : (kk + 1) * HD], axis=1, keepdims=True) * scale
                        for u in range(step + 1)
                    ]
                    top = functools.reduce(jnp.maximum, scores)
                    ws = [jnp.exp(x - top) for x in scores]
                    tops.append(top)
                    totals.append(sum(ws))
                    outs.append(sum(w * nvf[u][i : i + 1, kk * HD : (kk + 1) * HD] for u, w in enumerate(ws)))
            for n, x in enumerate((tops, totals)):
                fresh[h, i, n] = jnp.broadcast_to(jnp.concatenate(x, axis=0), (d.q, 128))
            stage[h, i] = jnp.concatenate(outs, axis=0)

    def exchanged(n, c):
        chunk(qs, qp, fw_send, fw_recv, n).wait_send()
        chunk(o.at[0], o.at[1], ex_send, ex_recv, n).wait()
        return c

    lax.fori_loop(0, chunks_of_slots, exchanged, 0)
    table_copy.wait()

    lane8 = iota((8, 128), 1)
    factors, tiles = [], {}
    for side in (0, 1):
        for at in range(0, d.slots, 8):
            ids = [meta[5 + 2 * chunks + side, at + u] for u in range(8)]
            theirs = jnp.concatenate([t[1 - side, pl.ds(i, 1), :] for i in ids], axis=0)
            mine = t[side, pl.ds(at, 8), :]
            top = jnp.maximum(mine, theirs)
            factor = jnp.exp(mine - top)
            factors.append(factor)
            tiles[side, at] = jnp.where(lane8 < 64, top, mine * pltpu.roll(factor, 64, 1))
    cols = jnp.transpose(jnp.concatenate(factors, axis=0))
    for (side, at), tile in tiles.items():
        t[side, pl.ds(at, 8), :] = tile
    for side in (0, 1):
        for i in range(d.slots):
            n = side * d.slots + i
            o[side, i] = (o[side, i].astype(F32) * cols[: d.q, n : n + 1]).astype(BF16)

    def pad8(x):
        if x.shape[0] == 8:
            return x
        return jnp.concatenate([x, jnp.zeros((8 - x.shape[0], 128), F32)], axis=0)

    def prepare(stats, count):
        top = functools.reduce(jnp.maximum, stats)
        es = [jnp.exp(st - top) for st in stats]
        total = sum(e * pltpu.roll(st, 64, 1) for e, st in zip(es, stats))
        tile = jnp.where(lane8 < 64, top, pltpu.roll(total, 64, 1))[:count]
        return tile, jnp.transpose(jnp.concatenate(es, axis=0))

    def apply(tile, cols, rows, many, count, out_d, out_s):
        out_s[...] = tile
        for r in range(count):
            acc = None
            for k in range(many):
                term = rows(k, r).astype(F32) * cols[: d.q, k * 8 + r : k * 8 + r + 1]
                acc = term if acc is None else acc + term
            out_d[r] = acc.astype(BF16)

    def merge(jobs, count):
        tiles = [[pad8(x[1][...]) for x in ins] for ins, _ in jobs]
        ready = [prepare(stats, count) for stats in tiles]
        for (ins, dst), (tile, cols) in zip(jobs, ready):
            apply(tile, cols, lambda k, r: ins[k][0][r], len(ins), count, *dst)

    per_row = 128 // d.rg

    class Part:
        def __init__(self, first, second, rows, recv, recv_s, mine, mine_s, send_sem, recv_sem):
            self.first, self.second = first, second
            self.start, self.count = rows
            self.recv, self.recv_s, self.mine, self.mine_s = recv, recv_s, mine, mine_s
            self.send_sem, self.recv_sem = send_sem, recv_sem
            self.n1, self.lanes = d.size[first], d.size[second]
            self.h1, self.h2 = d.hops[first], d.hops[second]
            self.phase2 = sum(self.h1) * self.lanes
            self.to = {
                (axis, way): neighbour(axis, 1 - 2 * way) for axis in (first, second) for way in (0, 1)
            }

        def id1(self, way, j, lane):
            return (way * self.h1[0] + j - 1) * self.lanes + lane

        def id2(self, way, j):
            return self.phase2 + way * self.h2[0] + j - 1

        def bufs(self, n):
            return self.recv.at[n], self.recv_s.at[n]

        def chip_sum(self, o1, lane):
            n = (o1 % self.n1) * self.lanes + lane
            return self.mine.at[n], self.mine_s.at[n]

        def copies(self, src, n, axis, way):
            return [
                remote(a, b, self.send_sem.at[k, n], self.recv_sem.at[k, n], self.to[axis, way])
                for k, (a, b) in enumerate(zip(src, self.bufs(n)))
            ]

        def send(self, src, n, axis, way):
            for cp in self.copies(src, n, axis, way):
                cp.start()

        def wait(self, n):
            for cp in self.copies(self.bufs(n), n, self.first, 0):
                cp.wait_recv()

        def wait_sent(self, n):
            for cp in self.copies(self.bufs(n), n, self.first, 0):
                cp.wait_send()

        def lane(self, k):
            return (self.h2[0] + ((k + 1) // 2) * (1 if k % 2 else -1)) % self.lanes

        def build(self, o1, k):
            lane = self.lane(k)
            oy, oz = (o1, lane) if self.first == "y" else (lane, o1)
            kv_to = kv_at(oy, oz)
            line, col = lax.div(kv_to, per_row), lax.rem(kv_to, per_row) * d.rg + self.start
            ids = [
                [meta[5 + side * chunks + line, col + r] for r in range(self.count)] for side in (0, 1)
            ]
            stats = [
                jnp.concatenate([t[side, pl.ds(i, 1), :] for i in ids[side]], axis=0) for side in (0, 1)
            ]
            dst, dst_s = self.chip_sum(o1, lane)
            dst_s[...] = jnp.where(
                lane8[: self.count] < 64, jnp.maximum(stats[0], stats[1]), stats[0] + stats[1]
            )
            for r in range(self.count):
                dst[r] = o[0, ids[0][r]] + o[1, ids[1][r]]

        def launch(self, way, k):
            o1 = (1 - 2 * way) * self.h1[way]
            self.build(o1, k)
            lane = self.lane(k)
            self.send(self.chip_sum(o1, lane), self.id1(way, 1, lane), self.first, way)

        def prebuild(self, way, j, k):
            self.build((1 - 2 * way) * (self.h1[way] - j), k)

        def relay(self, way, j, k):
            lane = self.lane(k)
            n = self.id1(way, j, lane)
            self.wait(n)
            left = (1 - 2 * way) * (self.h1[way] - j)
            src = self.bufs(n)
            merge([([src, self.chip_sum(left, lane)], src)], self.count)
            self.send(src, self.id1(way, j + 1, lane), self.first, way)

        def second_step(self, k, result):
            lane = self.lane(k)
            ids = [self.id1(way, self.h1[way], lane) for way in (0, 1) if self.h1[way]]
            last = k == self.lanes - 1
            if last:
                ids += [self.id2(way, self.h2[way]) for way in (0, 1) if self.h2[way]]
            elif k >= 2:
                ids.append(self.id2(k % 2, k // 2))
            for n in ids:
                self.wait(n)
            ins = [self.bufs(n) for n in ids] + [self.chip_sum(0, lane)]
            dst = result if last else ins[0]
            merge([(ins, dst)], self.count)
            if not last:
                self.send(dst, self.id2(k % 2, k // 2 + 1), self.second, k % 2)

        def drain(self):
            def body(n, c):
                self.wait_sent(n)
                return c

            lax.fori_loop(0, self.phase2 + sum(self.h2), body, 0)

    p0 = Part("y", "z", d.rows_of[0], r0, r0s, d0, d0s, s0_send, s0_recv)
    p1 = Part("z", "y", d.rows_of[1], r1, r1s, d1, d1s, s1_send, s1_recv)
    fin0 = (f.at[pl.ds(p0.start, p0.count)], fs.at[pl.ds(p0.start, p0.count)])
    fin1 = (f.at[pl.ds(p1.start, p1.count)], fs.at[pl.ds(p1.start, p1.count)])

    parts, fins = (p0, p1), (fin0, fin1)
    for what, n, *rest in plan_reduce:
        if what == "second":
            parts[n].second_step(*rest, fins[n])
        else:
            getattr(parts[n], what)(*rest)

    for n in range(d.ntp):
        for i in range(d.rd):
            rfs_row = fs[n * d.rd + i : n * d.rd + i + 1, :]
            b1s_tmp = rfs_row
            rfs.at[d.ntp + n][i : i + 1, :] = b1s_tmp

    def final(k, dst_t, src_t, dev_t):
        return [
            remote(f.at[pl.ds(src_t * d.rd, d.rd)], rf.at[dst_t], fin_send.at[0, k], fin_recv.at[0, k], (kv, dev_t)),
            remote(rfs.at[d.ntp + src_t], rfs.at[dst_t], fin_send.at[1, k], fin_recv.at[1, k], (kv, dev_t)),
        ]

    for k in range(1, d.ntp):
        other = lax.rem(tp + k, d.ntp)
        for cp in final(k - 1, tp, other, other):
            cp.start()
            waits.append(cp)
    rf[tp] = f[pl.ds(tp * d.rd, d.rd)]
    rfs[tp] = rfs[d.ntp + tp]

    p0.drain()
    p1.drain()
    for k in range(1, d.ntp):
        source = lax.rem(tp - k + d.ntp, d.ntp)
        for cp in final(k - 1, source, tp, source):
            cp.wait_recv()
    for h in range(d.ntp):
        cols = jnp.transpose(pad8(rfs[h]))
        for i in range(d.rd):
            top_n, total_n, out_n = fresh[h, i, 0], fresh[h, i, 1], stage[h, i]
            top_c, total_c = cols[: d.q, i : i + 1], cols[64 : 64 + d.q, i : i + 1]
            top = jnp.maximum(top_n, top_c)
            a, b = jnp.exp(top_n - top), jnp.exp(top_c - top)
            numer = out_n * a + rf[h, i].astype(F32) * b
            result = (numer / (total_n * a + total_c * b)).astype(BF16)
            for step in range(d.steps):
                out[step, i, pl.ds(h * heads, heads)] = result[step * heads : (step + 1) * heads]

    for cp in waits:
        cp.wait_send()


def make_shards(d):
    order = gather_order(d)
    plan_reduce = reduce_order(d)

    def shards(queries, new_keys, new_values, key_cache, value_cache, context_lengths, piece_slots):
        steps, rd, width = queries.shape
        chunks = d.rows // 128
        vmem = pl.BlockSpec(memory_space=pltpu.VMEM)
        hbm = pl.BlockSpec(memory_space=pl.ANY)
        c0, c1 = d.rows_of[0][1], d.rows_of[1][1]
        n0 = sum(d.hops["y"]) * d.nz + sum(d.hops["z"])
        n1 = sum(d.hops["z"]) * d.ny + sum(d.hops["y"])
        pad = d.slots + 8
        dma = pltpu.SemaphoreType.DMA
        sem = lambda *shape: dma(shape)
        nt = max(d.ntp - 1, 1)
        plan_rows = -(-(7 + 2 * chunks) // 8) * 8
        scratch = [
            pltpu.VMEM((chunks, 128), jnp.int32),
            pltpu.VMEM(queries.shape, BF16),
            pltpu.VMEM(new_keys.shape, BF16),
            pltpu.VMEM(new_values.shape, BF16),
            pltpu.VMEM((d.ntp, rd, d.q, HD), F32),
            pltpu.VMEM((d.ntp, rd, 2, d.q, 128), F32),
            pltpu.VMEM((d.ntp, rd, d.q, HD), BF16),
            pltpu.VMEM(piece_slots.shape, jnp.int32),
            pltpu.VMEM((plan_rows, 128), jnp.int32),
            pltpu.SMEM((plan_rows, 128), jnp.int32),
            pltpu.VMEM((d.rows // 2, d.q, HD), BF16),
            pltpu.VMEM((d.slots, d.q, HD), BF16),
            pltpu.VMEM((d.slots, d.q, HD), BF16),
            pltpu.VMEM(key_cache.shape, BF16),
            pltpu.VMEM(value_cache.shape, BF16),
            pltpu.VMEM((2, pad, d.q, HD), BF16),
            pltpu.VMEM((2, pad, 128), F32),
            pltpu.VMEM((n0, c0, d.q, HD), BF16),
            pltpu.VMEM((n0, c0, 128), F32),
            pltpu.VMEM((n1, c1, d.q, HD), BF16),
            pltpu.VMEM((n1, c1, 128), F32),
            pltpu.VMEM((d.ny * d.nz, c0, d.q, HD), BF16),
            pltpu.VMEM((d.ny * d.nz, c0, 128), F32),
            pltpu.VMEM((d.ny * d.nz, c1, d.q, HD), BF16),
            pltpu.VMEM((d.ny * d.nz, c1, 128), F32),
            pltpu.VMEM((d.rg, d.q, HD), BF16),
            pltpu.VMEM((d.rg, 128), F32),
            pltpu.VMEM((d.ntp, rd, d.q, HD), BF16),
            pltpu.VMEM((2 * d.ntp, rd, 128), F32),
            sem(6), sem(2, 4), sem(nt), sem(nt), sem(len(order) // 2), sem(len(order) // 2), sem(d.slots // 8), sem(d.slots // 8),
            sem(d.slots // 8 + 1), sem(d.slots // 8 + 1), sem(2, n0), sem(2, n0), sem(2, n1), sem(2, n1), sem(2, nt), sem(2, nt),
        ]
        result = pl.pallas_call(
            functools.partial(main_kernel, d, order, plan_reduce),
            out_shape=pltpu.VMEM((steps, rd, width // HD, HD), BF16),
            in_specs=[hbm] * 7,
            out_specs=vmem,
            scratch_shapes=scratch,
            compiler_params=pltpu.CompilerParams(
                collective_id=0, has_side_effects=True, vmem_limit_bytes=56 * 1024 * 1024
            ),
        )(piece_slots, context_lengths.reshape(chunks, 128), queries, new_keys, new_values, key_cache, value_cache)
        return result.reshape(steps, rd, width)

    return shards


def solution(mesh):
    d = Dims(4, 8, 4, 2, 40, 256, 3, 2, 8)
    return build(mesh, d)


def build(mesh, d):
    placed = (
        P(None, ("kv", "tp"), None),
        P(None, ("kv", "tp"), None),
        P(None, ("kv", "tp"), None),
        P("kv", None, "tp"),
        P("kv", None, "tp"),
        P(),
        P(),
    )
    return jax.shard_map(
        make_shards(d),
        mesh=mesh,
        in_specs=placed,
        out_specs=P(None, ("kv", "tp"), None),
        check_vma=False,
    )
```
